128 devices in a mesh: row: 32 (over z, y, x_lo), col: 4 (over x_hi, core).
Axes of the slice: x: 4 (x_hi: 2, x_lo: 2; x = x_hi * 2 + x_lo), y: 4, z: 4, core: 2. Of those that a mesh axis runs over, the one named last changes fastest.
Arguments:
- tokens: bfloat16 [32768, 1024], P('row', 'col'), may hold values from -6 to 6
- seg_ids: int32 [64, 512], P('row'), may hold values from 0 to 5, never falling along the last dimension, each value on 1 to 256 neighbouring positions
- qkv_weight: float32 [1024, 3, 1024], P('row', None, 'col'), may hold values from -0.1875 to 0.1875
- q_bias: float32 [1024], P('col'), may hold values from -3 to 3
- v_bias: float32 [1024], P('col'), may hold values from -3 to 3
- out_weight: float32 [1024, 1024], P('row', 'col'), may hold values from -0.5 to 0.5
- out_bias: float32 [1024], P('col'), may hold values from -3 to 3
- gain_attn: float32 [1024], P('col'), may hold values from 0.5 to 1.5
- shift_attn: float32 [1024], P('col'), may hold values from -3 to 3
- up_weight: float32 [1024, 4096], P('row', 'col'), may hold values from -0.1875 to 0.1875
- up_bias: float32 [4096], P('col'), may hold values from -3 to 3
- down_weight: float32 [1024, 4096], P('row', 'col'), may hold values from -0.09375 to 0.09375
- down_bias: float32 [1024], P('col'), may hold values from -3 to 3
- gain_ffn: float32 [1024], P('col'), may hold values from 0.5 to 1.5
- shift_ffn: float32 [1024], P('col'), may hold values from -3 to 3
- out_grad: float32 [32768, 1024], P('row', 'col'), may hold values from -6 to 6
Outputs:
- layer_out: float32 [32768, 1024], P('row', 'col')
- input_grad: float32 [32768, 1024], P('row', 'col')
- qkv_weight_grad: float32 [1024, 3, 1024], P('row', None, 'col')
- q_bias_grad: float32 [1024], P('col')
- v_bias_grad: float32 [1024], P('col')
- out_weight_grad: float32 [1024, 1024], P('row', 'col')
- out_bias_grad: float32 [1024], P('col')
- gain_attn_grad: float32 [1024], P('col')
- shift_attn_grad: float32 [1024], P('col')
- up_weight_grad: float32 [1024, 4096], P('row', 'col')
- up_bias_grad: float32 [4096], P('col')
- down_weight_grad: float32 [1024, 4096], P('row', 'col')
- down_bias_grad: float32 [1024], P('col')
- gain_ffn_grad: float32 [1024], P('col')
- shift_ffn_grad: float32 [1024], P('col')
The draws below stay inside these ranges and needn't reach their ends.
Inputs may be any that keep to these rules, and one draw needn't show every extreme that they name: `seg_ids`: along each sequence the ids never fall, so each id marks one document of consecutive tokens; no document holds more than 256 tokens.
All inputs are finite; a program needn't handle non-finite values.
Results may differ from the reference program's by a relative error of at most 0.028.
Values may be sent and summed in bfloat16 or wider, within the bound.
No kernel may reach another device: no remote copies, remote signals or barrier semaphores. Data moves between devices by JAX's collectives and lax.ppermute only.
A program may use at most 128 MiB of HBM per device.

```python
import math
import jax
import jax.numpy as jnp
import numpy as np
from jax import lax

D = 1024
H = 16
HD = 64
FF = 4096
LEN = 512
SEQS = 64
TOKENS = 32768


def steps_of(stream_key, dims, cuts, least, largest):
    level, own = 1.0, jax.random.fold_in(stream_key, 6)
    for position, shards_of in cuts:
        draws = jnp.exp(jax.random.uniform(jax.random.fold_in(own, position), (shards_of,), jnp.float32, least / len(cuts), largest / len(cuts)))
        level = level * jnp.repeat(draws, dims[position] // shards_of).reshape([-1 if axis == position else 1 for axis in range(len(dims))])
    return level


def length_profile(number_of, total, bound, lean):
    portions = [(1 << 20) // math.isqrt(grade ** lean) + 1 for grade in range(2, number_of + 1)]
    spare, given = total - bound - (number_of - 1), [1] * (number_of - 1)
    while spare > 0:
        free = [i for i in range(number_of - 1) if given[i] < bound]
        whole, remaining = sum([portions[i] for i in free]), spare
        for i in free:
            extra = min(bound - given[i], max(1, remaining * portions[i] // whole), spare)
            given[i] = given[i] + extra
            spare = spare - extra
    return np.array([bound] + given)


def uneven(rng, count, total, limit, slope):
    if count == 2:
        one = jax.random.randint(rng, (), max(1, total - limit), min(limit, total - 1) + 1)
        return jnp.stack([one, total - one])
    lengths = jnp.asarray(length_profile(count, total, limit, slope), jnp.int32)
    twos = (count - 1) // 2
    giver, taker = lengths[1:1 + 2 * twos:2], lengths[2:2 + 2 * twos:2]
    slack = jnp.minimum(giver - 1, limit - taker)
    passed = jax.random.randint(jax.random.fold_in(rng, 1), (twos,), 0, 1 << 20) % (slack + 1)
    lengths = lengths.at[1:1 + 2 * twos:2].set(giver - passed).at[2:2 + 2 * twos:2].set(taker + passed)
    return lengths[jax.random.permutation(jax.random.fold_in(rng, 2), count)]


def normal_values(stream_key, shape, width, reach, cuts=(), held_as=jnp.bfloat16):
    entries = jax.random.normal(stream_key, shape, jnp.float32) * width
    if len(cuts) > 0:
        entries = steps_of(stream_key, shape, cuts, -0.22, 0.18) * entries
    return jnp.clip(entries, min=-reach, max=reach).astype(held_as)


def setup_inputs(seed: int = 0) -> dict:
    key_of = jax.random.split(jax.random.key(seed), 17)
    return {
        "tokens": normal_values(key_of[0], (TOKENS, D), 1.0, 6.0, ((0, 32), (1, 4))),
        "seg_ids": jax.vmap(lambda own: jnp.searchsorted(jnp.cumsum(uneven(own, 6, LEN, LEN // 2, 2)), jnp.arange(LEN), side="right"))(jax.random.split(key_of[1], SEQS)).reshape((SEQS, LEN)).astype(jnp.int32),
        "qkv_weight": normal_values(key_of[2], (D, 3, D), D ** -0.5, 0.1875, ((0, 32), (2, 4)), jnp.float32),
        "q_bias": normal_values(key_of[3], (D,), 0.5, 3.0, ((0, 4),), jnp.float32),
        "v_bias": normal_values(key_of[4], (D,), 0.5, 3.0, ((0, 4),), jnp.float32),
        "out_weight": normal_values(key_of[5], (D, D), (D // 8) ** -0.5, 0.5, ((0, 32), (1, 4)), jnp.float32),
        "out_bias": normal_values(key_of[6], (D,), 0.5, 3.0, ((0, 4),), jnp.float32),
        "gain_attn": jnp.clip(1.0 + 0.1 * jax.random.normal(key_of[7], (D,), jnp.float32), 0.5, 1.5),
        "shift_attn": normal_values(key_of[8], (D,), 0.5, 3.0, ((0, 4),), jnp.float32),
        "up_weight": normal_values(key_of[9], (D, FF), D ** -0.5, 0.1875, ((0, 32), (1, 4)), jnp.float32),
        "up_bias": normal_values(key_of[10], (FF,), 0.5, 3.0, ((0, 4),), jnp.float32),
        "down_weight": normal_values(key_of[11], (D, FF), FF ** -0.5, 0.09375, ((0, 32), (1, 4)), jnp.float32),
        "down_bias": normal_values(key_of[12], (D,), 0.5, 3.0, ((0, 4),), jnp.float32),
        "gain_ffn": jnp.clip(1.0 + 0.1 * jax.random.normal(key_of[13], (D,), jnp.float32), 0.5, 1.5),
        "shift_ffn": normal_values(key_of[14], (D,), 0.5, 3.0, ((0, 4),), jnp.float32),
        "out_grad": normal_values(key_of[15], (TOKENS, D), 1.0, 6.0, ((0, 32), (1, 4)), jnp.float32),
    }


@jax.custom_vjp
def low(v):
    return lax.optimization_barrier(v.astype(jnp.bfloat16)).astype(jnp.float32)

@jax.custom_vjp
def low_back(v):
    return v

def low_keep(v):
    return (low(v), None)

def low_pass(kept, grad):
    return (grad,)

def back_keep(v):
    return (v, None)

def back_low(kept, grad):
    return (low(grad),)
low.defvjp(low_keep, low_pass)
low_back.defvjp(back_keep, back_low)
highest = lax.Precision.HIGHEST
lowest = -1e+30
epsilon = 1e-06

def layer_norm(residual, gain_vec, shift_vec):
    center = residual - lax.optimization_barrier(jnp.mean(residual, axis=-1, keepdims=True))
    spread = lax.optimization_barrier(jnp.mean(center * center, axis=-1, keepdims=True))
    return center * lax.rsqrt(spread + epsilon) * gain_vec + shift_vec

def attend(pieces):
    query_rows, key_rows, value_rows, segment = pieces
    raw_scores = jnp.einsum('qhd,khd->hqk', query_rows, key_rows, precision=highest)
    scores = low_back(raw_scores) * HD ** (-0.5)
    allowed = segment[:, None] == segment[None, :]
    scores = jnp.where(allowed[None], scores, lowest)
    attn_probs = jax.nn.softmax(scores, axis=-1)
    return jnp.einsum('hqk,khd->qhd', low(attn_probs), value_rows, precision=highest)

def forward_layer(token_rows, segments, params):
    qkv_weight, q_bias, v_bias, out_weight, out_bias, gain_attn, shift_attn, up_weight, up_bias, down_weight, down_bias, gain_ffn, shift_ffn = params
    seq_count = segments.shape[0]
    projected = low_back(jnp.einsum('td,dkc->tkc', token_rows, low(qkv_weight), precision=highest))
    queries_low = low(projected[:, 0] + q_bias)
    keys_low = low(projected[:, 1])
    values_low = low(projected[:, 2] + v_bias)

    def to_heads(matrix):
        return matrix.reshape(seq_count, LEN, H, HD)
    context = lax.map(jax.checkpoint(attend), (to_heads(queries_low), to_heads(keys_low), to_heads(values_low), segments))
    context = low_back(low(context.reshape(seq_count * LEN, D)))
    attn_out = low_back(jnp.dot(context, low(out_weight).T, precision=highest, preferred_element_type=jnp.float32))
    resid_attn = token_rows + attn_out + out_bias
    hidden_in = layer_norm(resid_attn, gain_attn, shift_attn)
    up_matrix = low_back(jnp.dot(low(hidden_in), low(up_weight), precision=highest, preferred_element_type=jnp.float32))
    pre_act = up_matrix + up_bias
    activated = low_back(low(jax.nn.gelu(pre_act, approximate=False)))
    ffn_out = low_back(jnp.dot(activated, low(down_weight).T, precision=highest, preferred_element_type=jnp.float32))
    resid_ffn = hidden_in + ffn_out + down_bias
    return layer_norm(resid_ffn, gain_ffn, shift_ffn)

def reference(tokens, seg_ids, qkv_weight, q_bias, v_bias, out_weight, out_bias, gain_attn, shift_attn, up_weight, up_bias, down_weight, down_bias, gain_ffn, shift_ffn, out_grad):
    params = (qkv_weight, q_bias, v_bias, out_weight, out_bias, gain_attn, shift_attn, up_weight, up_bias, down_weight, down_bias, gain_ffn, shift_ffn)
    group_size = max([candidate for candidate in (8, 4, 2, 1) if SEQS % candidate == 0])
    blocks = SEQS // group_size
    token_groups = tokens.astype(jnp.float32).reshape(blocks, group_size * LEN, D)
    seg_groups = seg_ids.reshape(blocks, group_size, LEN)
    cot_groups = out_grad.reshape(blocks, group_size * LEN, D)

    def one_group(totals, group_items):
        token_block, seg_block, cot_block = group_items

        def run_layer(token_arg, param_arg):
            return forward_layer(token_arg, seg_block, param_arg)
        layer_block, pullback = jax.vjp(run_layer, token_block, params)
        token_grad, param_grads = pullback(cot_block)
        return (jax.tree.map(jnp.add, totals, param_grads), (layer_block, token_grad))
    initial = jax.tree.map(jnp.zeros_like, params)
    totals, (layer_out, input_grad) = lax.scan(one_group, initial, (token_groups, seg_groups, cot_groups))
    qkv_weight_grad, q_bias_grad, v_bias_grad, out_weight_grad, out_bias_grad, gain_attn_grad, shift_attn_grad, up_weight_grad, up_bias_grad, down_weight_grad, down_bias_grad, gain_ffn_grad, shift_ffn_grad = totals
    return (layer_out.reshape(TOKENS, D), input_grad.reshape(TOKENS, D), qkv_weight_grad, q_bias_grad, v_bias_grad, out_weight_grad, out_bias_grad, gain_attn_grad, shift_attn_grad, up_weight_grad, up_bias_grad, down_weight_grad, down_bias_grad, gain_ffn_grad, shift_ffn_grad)
```

```python
import itertools

import jax
import jax.numpy as jnp
from jax import lax
from jax.experimental import pallas as pl
from jax.experimental.pallas import tpu as pltpu
from jax.sharding import Mesh, PartitionSpec as P

HD = 64
AXES = ("z", "y", "xl", "xh", "core")
ROW = ("z", "y", "xl")
COL = ("xh", "core")
lowest = -1e30
epsilon = 1e-06
bf16 = jnp.bfloat16
f32 = jnp.float32

ORDER = {
    "attn": ("xyz", "zxy"),
    "up": ("yzx", "xyz"),
    "down": ("zxy", "yzx"),
}


def device_at(x, y, z, core):
    return ((z * 4 + y) * 2 + x % 2) * 4 + (x // 2) * 2 + core


def shifts(axes, step):
    pairs = []
    for x, y, z, core in itertools.product(range(4), range(4), range(4), range(2)):
        to = {"x": x, "y": y, "z": z}
        axis = axes[core]
        to[axis] = (to[axis] + (step if core == 0 else -step)) % 4
        pairs.append((device_at(x, y, z, core), device_at(to["x"], to["y"], to["z"], core)))
    return pairs


def send(value, axes, step):
    return lax.ppermute(value, AXES, shifts(axes, step))


def swap_core(value):
    return lax.ppermute(value, "core", [(0, 1), (1, 0)])


def swap_xh(value):
    return lax.ppermute(value, "xh", [(0, 1), (1, 0)])


def stage_axes(group, stage):
    return (ORDER[group][0][stage], ORDER[group][1][stage])


def gather_direct(value, axes):
    return jnp.concatenate(
        [value, send(value, axes, -1), send(value, axes, 2), send(value, axes, 1)], 0
    )


def gather_ring(value, axes):
    half = value.shape[0] // 2
    first = send(value, axes, 1)
    second = send(value, axes, -1)
    far_first = send(first[:half], axes, 1)
    far_second = send(second[half:], axes, -1)
    return jnp.concatenate([value, second, far_first, far_second, first], 0)


def gather_group(shard, group):
    value = gather_direct(shard, stage_axes(group, 0))
    value = gather_direct(value, stage_axes(group, 1))
    return gather_ring(value, stage_axes(group, 2))


def add_low(*terms):
    total = terms[0].astype(f32)
    for term in terms[1:]:
        total = total + term.astype(f32)
    return total.astype(bf16)


def scatter_ring(value, axes):
    quarter = value.shape[0] // 4
    half = quarter // 2
    own, near, far, back = (value[i * quarter : (i + 1) * quarter] for i in range(4))
    far_first = send(far[:half], axes, 1)
    far_second = send(far[half:], axes, -1)
    near = jnp.concatenate([add_low(near[:half], far_first), near[half:]], 0)
    back = jnp.concatenate([back[:half], add_low(back[half:], far_second)], 0)
    return add_low(own, send(near, axes, 1), send(back, axes, -1))


def scatter_direct(value, axes):
    quarter = value.shape[0] // 4
    own, near, far, back = (value[i * quarter : (i + 1) * quarter] for i in range(4))
    return (own, send(near, axes, 1), send(far, axes, 2), send(back, axes, -1))


def scatter_group(value, group):
    value = scatter_ring(value, stage_axes(group, 2))
    value = add_low(*scatter_direct(value, stage_axes(group, 1)))
    parts = scatter_direct(value, stage_axes(group, 0))
    return sum(part.astype(f32) for part in parts)


def block_table(group, place):
    index = jnp.arange(64, dtype=jnp.int32)
    offset = {0: index % 4, 1: (index // 4) % 4, 2: index // 16}
    tables = []
    for core in range(2):
        sign = 1 - 2 * core
        at = {}
        for stage in range(3):
            axis = ORDER[group][core][stage]
            at[axis] = (place[axis] + sign * offset[stage] + 4) % 4
        tables.append(
            (((at["x"] // 2) * 4 + at["z"]) * 4 + at["y"]) * 2 + at["x"] % 2
        )
    return jnp.where(place["core"] == 0, tables[0], tables[1])


def move_blocks(value, table, spread):
    def kernel(table_ref, value_ref, out_ref, sem):
        for i in range(64):
            there = pl.ds(pl.multiple_of(table_ref[i] * 32, 32), 32)
            here = pl.ds(i * 32, 32)
            if spread:
                pltpu.make_async_copy(value_ref.at[here], out_ref.at[there], sem).start()
            else:
                pltpu.make_async_copy(value_ref.at[there], out_ref.at[here], sem).start()
        pltpu.make_async_copy(value_ref, out_ref, sem).wait()

    whole = pl.BlockSpec(memory_space=pltpu.VMEM)
    apart = pl.BlockSpec(memory_space=pl.ANY)
    return pl.pallas_call(
        kernel,
        out_shape=jax.ShapeDtypeStruct(value.shape, value.dtype),
        in_specs=[pl.BlockSpec(memory_space=pltpu.SMEM), apart if spread else whole],
        out_specs=whole if spread else apart,
        scratch_shapes=[pltpu.SemaphoreType.DMA],
        compiler_params=pltpu.CompilerParams(vmem_limit_bytes=16 * 1024 * 1024),
    )(table, value)


def norm_stats(residual):
    center = residual - jnp.mean(residual, axis=-1, keepdims=True)
    spread = jnp.mean(center * center, axis=-1, keepdims=True)
    inverse = lax.rsqrt(spread + epsilon)
    return center * inverse, inverse


def norm_back(grad, normed, inverse, gain):
    scaled = grad * gain
    return inverse * (
        scaled
        - jnp.mean(scaled, axis=-1, keepdims=True)
        - normed * jnp.mean(scaled * normed, axis=-1, keepdims=True)
    )


def einsum(spec, left, right):
    return jnp.einsum(spec, left, right, preferred_element_type=f32)


def body(
    tokens,
    seg_ids,
    qkv_weight,
    q_bias,
    v_bias,
    out_weight,
    out_bias,
    gain_attn,
    shift_attn,
    up_weight,
    up_bias,
    down_weight,
    down_bias,
    gain_ffn,
    shift_ffn,
    out_grad,
):
    length = seg_ids.shape[1]
    cols = tokens.shape[1]
    rows = qkv_weight.shape[0]
    xh = lax.axis_index("xh")
    core = lax.axis_index("core")
    place = {
        "x": xh * 2 + lax.axis_index("xl"),
        "y": lax.axis_index("y"),
        "z": lax.axis_index("z"),
        "core": core,
    }

    def pick(pair, index):
        return lax.dynamic_index_in_dim(pair, index, 0, keepdims=False)

    def ordered(own, other, index, axis):
        return jnp.where(
            index == 0, jnp.stack([own, other], axis), jnp.stack([other, own], axis)
        )

    def to_sequence(local):
        pair = local.reshape(2, length, cols)
        own, other = pick(pair, xh), swap_xh(pick(pair, 1 - xh))
        half = ordered(own, other, xh, 1)
        return ordered(half, swap_core(half), core, 2).reshape(length, 4 * cols)

    def own_blocks(full):
        return lax.dynamic_index_in_dim(
            full.reshape(*full.shape[:-1], 2, 2, cols), core, full.ndim, keepdims=False
        )

    def from_sequence(blocks, low):
        own = lax.dynamic_index_in_dim(blocks, xh, 1, keepdims=False)
        other = lax.dynamic_index_in_dim(blocks, 1 - xh, 1, keepdims=False)
        other = swap_xh(other.astype(low)).astype(f32)
        return ordered(own, other, xh, 0).reshape(2 * length, cols)

    attn_shard = jnp.concatenate(
        [qkv_weight.reshape(rows, 3 * cols), out_weight], 1
    ).astype(bf16)
    shards = {"attn": attn_shard, "up": up_weight.astype(bf16), "down": down_weight.astype(bf16)}
    tables = {group: block_table(group, place) for group in ORDER}

    def gathered(group):
        flat = move_blocks(gather_group(shards[group], group), tables[group], True)
        return flat.reshape(2, 32 * rows, flat.shape[-1])

    def scattered(grad, group):
        flat = grad.astype(bf16).reshape(64 * rows, grad.shape[-1])
        return scatter_group(move_blocks(flat, tables[group], False), group)

    token_rows = to_sequence(tokens)
    vectors = jnp.concatenate(
        [q_bias, v_bias, out_bias, gain_attn, shift_attn, down_bias, gain_ffn, shift_ffn, up_bias]
    )
    vectors = ordered(vectors, swap_xh(vectors), xh, 0)
    both = ordered(vectors, swap_core(vectors), core, 1)
    q_bias_own, v_bias_own = vectors[:, :cols], vectors[:, cols : 2 * cols]
    up_bias_own = vectors[:, 8 * cols :]
    out_bias_all, gain_attn_all, shift_attn_all, down_bias_all, gain_ffn_all, shift_ffn_all = (
        both[:, :, i * cols : (i + 1) * cols].reshape(4 * cols) for i in range(2, 8)
    )
    segment = pick(seg_ids, xh)

    attn_full = gathered("attn").reshape(2, 32 * rows, 4, cols)
    up_full = gathered("up")
    down_full = gathered("down")
    cot_rows = to_sequence(out_grad.astype(bf16)).astype(f32)

    def to_heads(matrix):
        return matrix.reshape(length, -1, HD)

    def both_cores(part):
        return part + swap_core(part.astype(bf16)).astype(f32)

    projected = einsum("td,xdjc->jtxc", token_rows, attn_full[:, :, :3])
    queries = to_heads((projected[0] + q_bias_own).astype(bf16))
    keys = to_heads(projected[1].astype(bf16))
    values = to_heads((projected[2] + v_bias_own).astype(bf16))
    allowed = segment[:, None] == segment[None, :]
    scores = einsum("qhd,khd->hqk", queries, keys) * HD**-0.5
    scores = jnp.where(allowed[None], scores, lowest)
    shifted = jnp.exp(scores - jnp.max(scores, axis=-1, keepdims=True))
    attn_probs = shifted / jnp.sum(shifted, axis=-1, keepdims=True)
    probs_low = attn_probs.astype(bf16)
    context = einsum("hqk,khd->qhd", probs_low, values).astype(bf16)
    context = context.reshape(length, 2, cols)
    attn_part = einsum("txc,xdc->td", context, attn_full[:, :, 3])
    resid_attn = token_rows.astype(f32) + both_cores(attn_part) + out_bias_all
    normed_attn, inverse_attn = norm_stats(resid_attn)
    hidden_in = normed_attn * gain_attn_all + shift_attn_all
    hidden_low = hidden_in.astype(bf16)
    pre_act = einsum("td,xdf->txf", hidden_low, up_full) + up_bias_own
    cumulative = 0.5 * (1.0 + lax.erf(pre_act * 0.7071067811865476))
    activated = (pre_act * cumulative).astype(bf16)
    ffn_part = einsum("txf,xdf->td", activated, down_full)
    resid_ffn = hidden_in + both_cores(ffn_part) + down_bias_all
    normed_ffn, inverse_ffn = norm_stats(resid_ffn)
    layer_full = normed_ffn * gain_ffn_all + shift_ffn_all
    layer_out = from_sequence(own_blocks(layer_full), bf16)

    gain_ffn_grad = jnp.sum(cot_rows * normed_ffn, axis=0)
    shift_ffn_grad = jnp.sum(cot_rows, axis=0)
    grad_resid_ffn = norm_back(cot_rows, normed_ffn, inverse_ffn, gain_ffn_all)
    down_bias_grad = jnp.sum(grad_resid_ffn, axis=0)
    ffn_grad_low = grad_resid_ffn.astype(bf16)
    down_weight_grad = scattered(einsum("td,txf->xdf", ffn_grad_low, activated), "down")
    act_grad = einsum("td,xdf->txf", ffn_grad_low, down_full).astype(bf16)
    density = jnp.exp(-0.5 * pre_act * pre_act) * 0.3989422804014327
    pre_grad = act_grad.astype(f32) * (cumulative + pre_act * density)
    up_bias_grad = jnp.sum(pre_grad, axis=0)
    pre_grad_low = pre_grad.astype(bf16)
    up_weight_grad = scattered(einsum("td,txf->xdf", hidden_low, pre_grad_low), "up")
    hidden_part = einsum("txf,xdf->td", pre_grad_low, up_full)
    hidden_grad = grad_resid_ffn + both_cores(hidden_part)
    gain_attn_grad = jnp.sum(hidden_grad * normed_attn, axis=0)
    shift_attn_grad = jnp.sum(hidden_grad, axis=0)
    grad_resid_attn = norm_back(hidden_grad, normed_attn, inverse_attn, gain_attn_all)
    out_bias_grad = jnp.sum(grad_resid_attn, axis=0)
    attn_grad_low = grad_resid_attn.astype(bf16)
    out_weight_grad = einsum("td,txc->xdc", attn_grad_low, context)
    context_grad = to_heads(
        einsum("td,xdc->txc", attn_grad_low, attn_full[:, :, 3]).astype(bf16)
    )
    prob_grad = einsum("qhd,khd->hqk", context_grad, values)
    row_dot = jnp.sum(attn_probs * prob_grad, axis=-1, keepdims=True)
    score_low = (attn_probs * (prob_grad - row_dot) * HD**-0.5).astype(bf16)
    query_grad = einsum("hqk,khd->qhd", score_low, keys).reshape(length, 2, cols)
    key_grad = einsum("hqk,qhd->khd", score_low, queries).reshape(length, 2, cols)
    value_grad = einsum("hqk,qhd->khd", probs_low, context_grad).reshape(length, 2, cols)
    q_bias_grad = jnp.sum(query_grad, axis=0)
    v_bias_grad = jnp.sum(value_grad, axis=0)
    qkv_grad_low = jnp.stack([query_grad, key_grad, value_grad], 2).astype(bf16)
    qkv_weight_grad = einsum("td,txjc->xdjc", token_rows, qkv_grad_low)
    attn_weight_grad = jnp.concatenate(
        [qkv_weight_grad.reshape(2, 32 * rows, 3 * cols), out_weight_grad], 2
    )
    attn_weight_grad = scattered(attn_weight_grad, "attn")
    input_part = einsum("txjc,xdjc->td", qkv_grad_low, attn_full[:, :, :3])
    input_pair = input_part.reshape(length, 2, 2, cols)
    input_own = lax.dynamic_index_in_dim(input_pair, core, 2, keepdims=False)
    input_away = lax.dynamic_index_in_dim(input_pair, 1 - core, 2, keepdims=False)
    input_own = input_own + swap_core(input_away.astype(bf16)).astype(f32)
    input_grad = from_sequence(input_own + own_blocks(grad_resid_attn), bf16)

    vector_grads = jnp.concatenate(
        [
            q_bias_grad,
            v_bias_grad,
            *(
                own_blocks(vector)
                for vector in (
                    out_bias_grad,
                    gain_attn_grad,
                    shift_attn_grad,
                    down_bias_grad,
                    gain_ffn_grad,
                    shift_ffn_grad,
                )
            ),
            up_bias_grad,
        ],
        1,
    )
    total = pick(vector_grads, xh) + swap_xh(pick(vector_grads, 1 - xh))
    total = total + lax.ppermute(total, "xl", [(0, 1), (1, 0)])
    for axis in ("y", "z"):
        for bit in (1, 2):
            total = total + lax.ppermute(total, axis, [(i, i ^ bit) for i in range(4)])
    (
        q_bias_grad,
        v_bias_grad,
        out_bias_grad,
        gain_attn_grad,
        shift_attn_grad,
        down_bias_grad,
        gain_ffn_grad,
        shift_ffn_grad,
    ) = (total[i * cols : (i + 1) * cols] for i in range(8))
    up_bias_grad = total[8 * cols :]
    return (
        layer_out,
        input_grad,
        attn_weight_grad[:, : 3 * cols].reshape(rows, 3, cols),
        q_bias_grad,
        v_bias_grad,
        attn_weight_grad[:, 3 * cols :],
        out_bias_grad,
        gain_attn_grad,
        shift_attn_grad,
        up_weight_grad,
        up_bias_grad,
        down_weight_grad,
        down_bias_grad,
        gain_ffn_grad,
        shift_ffn_grad,
    )


def solution(mesh):
    placed_mesh = Mesh(mesh.devices.reshape(4, 4, 2, 2, 2), AXES)
    placed = (
        P(ROW, COL),
        P(ROW, None),
        P(ROW, None, COL),
        P(COL),
        P(COL),
        P(ROW, COL),
        P(COL),
        P(COL),
        P(COL),
        P(ROW, COL),
        P(COL),
        P(ROW, COL),
        P(COL),
        P(COL),
        P(COL),
        P(ROW, COL),
    )
    return jax.shard_map(
        body,
        mesh=placed_mesh,
        in_specs=placed,
        out_specs=(
            P(ROW, COL),
            P(ROW, COL),
            P(ROW, None, COL),
            P(COL),
            P(COL),
            P(ROW, COL),
            P(COL),
            P(COL),
            P(COL),
            P(ROW, COL),
            P(COL),
            P(ROW, COL),
            P(COL),
            P(COL),
            P(COL),
        ),
        check_vma=False,
    )
```

```python
import itertools

import jax
import jax.numpy as jnp
from jax import lax
from jax.experimental import pallas as pl
from jax.experimental.pallas import tpu as pltpu
from jax.sharding import Mesh, PartitionSpec as P

HD = 64
AXES = ("z", "y", "xl", "xh", "core")
ROW = ("z", "y", "xl")
COL = ("xh", "core")
lowest = -1e30
epsilon = 1e-06
bf16 = jnp.bfloat16
f32 = jnp.float32

ORDER = {
    "attn": ("xyz", "zxy"),
    "up": ("yzx", "xyz"),
    "down": ("zxy", "yzx"),
}


def device_at(x, y, z, core):
    return ((z * 4 + y) * 2 + x % 2) * 4 + (x // 2) * 2 + core


def shifts(axes, step):
    pairs = []
    for x, y, z, core in itertools.product(range(4), range(4), range(4), range(2)):
        to = {"x": x, "y": y, "z": z}
        axis = axes[core]
        to[axis] = (to[axis] + (step if core == 0 else -step)) % 4
        pairs.append((device_at(x, y, z, core), device_at(to["x"], to["y"], to["z"], core)))
    return pairs


def send(value, axes, step):
    return lax.ppermute(value, AXES, shifts(axes, step))


def swap_core(value):
    return lax.ppermute(value, "core", [(0, 1), (1, 0)])


def swap_xh(value):
    return lax.ppermute(value, "xh", [(0, 1), (1, 0)])


def stage_axes(group, stage):
    return (ORDER[group][0][stage], ORDER[group][1][stage])


def gather_direct(value, axes):
    return jnp.concatenate(
        [value, send(value, axes, -1), send(value, axes, 2), send(value, axes, 1)], 0
    )


def gather_ring(value, axes):
    half = value.shape[0] // 2
    first = send(value, axes, 1)
    second = send(value, axes, -1)
    far_first = send(first[:half], axes, 1)
    far_second = send(second[half:], axes, -1)
    return value, second, far_first, far_second, first


def gather_group(shard, group):
    value = gather_direct(shard, stage_axes(group, 0))
    value = gather_direct(value, stage_axes(group, 1))
    return gather_ring(value, stage_axes(group, 2))


def add_low(*terms):
    total = terms[0].astype(f32)
    for term in terms[1:]:
        total = total + term.astype(f32)
    return total.astype(bf16)


def scatter_ring(pieces, axes):
    own, plus, minus, near, back = pieces
    half = near.shape[0]
    plus = send(plus, axes, 1)
    minus = send(minus, axes, -1)
    near = send(add_low(near, plus[:half]), axes, 1)
    back = send(add_low(back, minus[:half]), axes, -1)
    return jnp.concatenate(
        [add_low(own[:half], near, minus[half:]), add_low(own[half:], plus[half:], back)], 0
    )


def scatter_direct(value, axes):
    quarter = value.shape[0] // 4
    own, near, far, back = (value[i * quarter : (i + 1) * quarter] for i in range(4))
    return (own, send(near, axes, 1), send(far, axes, 2), send(back, axes, -1))


def scatter_group(pieces, group):
    value = scatter_ring(pieces, stage_axes(group, 2))
    value = add_low(*scatter_direct(value, stage_axes(group, 1)))
    parts = scatter_direct(value, stage_axes(group, 0))
    return sum(part.astype(f32) for part in parts)


def block_table(group, place):
    index = jnp.arange(64, dtype=jnp.int32)
    offset = {0: index % 4, 1: (index // 4) % 4, 2: index // 16}
    tables = []
    for core in range(2):
        sign = 1 - 2 * core
        at = {}
        for stage in range(3):
            axis = ORDER[group][core][stage]
            at[axis] = (place[axis] + sign * offset[stage] + 4) % 4
        tables.append(
            (((at["x"] // 2) * 4 + at["z"]) * 4 + at["y"]) * 2 + at["x"] % 2
        )
    return jnp.where(place["core"] == 0, tables[0], tables[1])


SMEM = pl.BlockSpec(memory_space=pltpu.SMEM)
VMEM = pl.BlockSpec(memory_space=pltpu.VMEM)
BLOCK = 32
LANES = 128
PIECE_OF = ((0, 0), (0, 256), (3, 0), (1, 256), (1, 0), (2, 0), (2, 256), (4, 0))
PIECE_ROWS = (512, 512, 512, 256, 256)


def call(kernel, outs, args, scratch=(), scalars=0, flops=0):
    return pl.pallas_call(
        kernel,
        out_shape=[jax.ShapeDtypeStruct(shape, dtype) for shape, dtype in outs],
        in_specs=[SMEM] * scalars + [VMEM] * (len(args) - scalars),
        out_specs=[VMEM] * len(outs),
        scratch_shapes=[pltpu.VMEM(shape, dtype) for shape, dtype in scratch],
        compiler_params=pltpu.CompilerParams(vmem_limit_bytes=46 * 1024 * 1024),
        cost_estimate=pl.CostEstimate(flops=flops, bytes_accessed=1 << 22, transcendentals=0),
    )(*args)


def nn(left, right):
    return lax.dot_general(left, right, (((1,), (0,)), ((), ())), preferred_element_type=f32)


def nt(left, right):
    return lax.dot_general(left, right, (((1,), (1,)), ((), ())), preferred_element_type=f32)


def assemble(table, pieces):
    def kernel(table_ref, *refs):
        out_ref = refs[-1]
        block = 0
        for piece in refs[:-1]:
            for row in range(0, piece.shape[0], BLOCK):
                there = pl.multiple_of(table_ref[block] * BLOCK, BLOCK)
                out_ref[pl.ds(there, BLOCK), :] = piece[row : row + BLOCK, :]
                block += 1

    return call(kernel, [((2048, 1024), bf16)], (table, *pieces), scalars=1)[0]


def split_blocks(table_ref, grad_ref, piece_refs):
    for block in range(64):
        piece, first = PIECE_OF[block // 8]
        row = first + (block % 8) * BLOCK
        there = pl.multiple_of(table_ref[block] * BLOCK, BLOCK)
        piece_refs[piece][row : row + BLOCK, :] = grad_ref[pl.ds(there, BLOCK), :]


PIECES = [((rows, 1024), bf16) for rows in PIECE_ROWS]


def row_mean(value):
    return jnp.mean(value, axis=-1, keepdims=True)


def norm_stats(residual):
    center = residual - row_mean(residual)
    inverse = lax.rsqrt(row_mean(center * center) + epsilon)
    return center * inverse, inverse


def norm_back(grad, normed, inverse, gain):
    scaled = grad * gain
    return inverse * (scaled - row_mean(scaled) - normed * row_mean(scaled * normed))


def chunks(count, size, step):
    def run(i, carry):
        step(pl.ds(pl.multiple_of(i * size, size), size))
        return carry

    lax.fori_loop(0, count, run, 0)


def attention_forward(tokens, weights, q_bias, v_bias, seg_col, seg_row):
    def kernel(x_ref, w_ref, qb_ref, vb_ref, sc_ref, sr_ref, q_ref, k_ref, v_ref, ctx_ref, p_ref, part_ref, mask_ref):
        mask_ref[...] = jnp.where(sc_ref[...] == sr_ref[...], 0.0, lowest)
        for xh in range(2):
            cols = slice(xh * 256, xh * 256 + 256)
            w = w_ref.at[xh * 1024 : xh * 1024 + 1024]
            q_ref[:, cols] = (nn(x_ref[...], w[:, :256]) + qb_ref[xh : xh + 1, :]).astype(bf16)
            k_ref[:, cols] = nn(x_ref[...], w[:, 256:512]).astype(bf16)
            v_ref[:, cols] = (nn(x_ref[...], w[:, 512:768]) + vb_ref[xh : xh + 1, :]).astype(bf16)
        for pair in range(4):
            lanes = slice(pair * LANES, pair * LANES + LANES)

            def attend(rows, pair=pair, lanes=lanes):
                query = q_ref[rows, lanes]
                low_half = lax.broadcasted_iota(jnp.int32, query.shape, 1) < HD
                parts = []
                for h in range(2):
                    one = jnp.where(low_half == (h == 0), query, jnp.zeros_like(query))
                    scores = nt(one, k_ref[:, lanes]) * HD**-0.5 + mask_ref[rows, :]
                    shifted = jnp.exp(scores - jnp.max(scores, axis=-1, keepdims=True))
                    probs = shifted / jnp.sum(shifted, axis=-1, keepdims=True)
                    probs_low = probs.astype(bf16)
                    p_ref[2 * pair + h, rows, :] = probs_low
                    parts.append(nn(probs_low, v_ref[:, lanes]))
                ctx_ref[rows, lanes] = jnp.where(low_half, parts[0], parts[1]).astype(bf16)

            chunks(4, 128, attend)

        def project(rows):
            part_ref[rows, :] = (
                nt(ctx_ref[rows, :256], w_ref[:1024, 768:]) + nt(ctx_ref[rows, 256:], w_ref[1024:, 768:])
            ).astype(bf16)

        chunks(2, 256, project)

    half = ((512, 512), bf16)
    return call(
        kernel,
        [half, half, half, half, ((8, 512, 512), bf16), ((512, 1024), bf16)],
        (tokens, weights, q_bias, v_bias, seg_col, seg_row),
        scratch=[((512, 512), f32)],
        flops=3 << 30,
    )


def ffn_forward(tokens, own, other, out_bias, gain, shift, up, up_bias, down):
    def kernel(x_ref, own_ref, other_ref, ob_ref, g_ref, s_ref, up_ref, ub_ref, down_ref, normed_ref, inv_ref, hid_ref, act_ref, slope_ref, part_ref):
        def norm(rows):
            residual = x_ref[rows, :].astype(f32) + (own_ref[rows, :].astype(f32) + other_ref[rows, :].astype(f32)) + ob_ref[...]
            normed, inverse = norm_stats(residual)
            normed_ref[rows, :] = normed
            inv_ref[rows, :] = jnp.broadcast_to(inverse, (inverse.shape[0], LANES))
            hid_ref[rows, :] = (normed * g_ref[...] + s_ref[...]).astype(bf16)

        chunks(4, 128, norm)
        for xh in range(2):
            cols = slice(xh * 1024, xh * 1024 + 1024)

            def activate(rows, xh=xh, cols=cols):
                pre_act = nn(hid_ref[rows, :], up_ref[cols, :]) + ub_ref[xh : xh + 1, :]
                cumulative = 0.5 * (1.0 + lax.erf(pre_act * 0.7071067811865476))
                density = jnp.exp(-0.5 * pre_act * pre_act) * 0.3989422804014327
                act_ref[rows, cols] = (pre_act * cumulative).astype(bf16)
                slope_ref[rows, cols] = (cumulative + pre_act * density).astype(bf16)

            chunks(4, 128, activate)

        def project(rows):
            part_ref[rows, :] = (
                nt(act_ref[rows, :1024], down_ref[:1024, :]) + nt(act_ref[rows, 1024:], down_ref[1024:, :])
            ).astype(bf16)

        chunks(2, 256, project)

    return call(
        kernel,
        [((512, 1024), f32), ((512, LANES), f32), ((512, 1024), bf16), ((512, 2048), bf16), ((512, 2048), bf16), ((512, 1024), bf16)],
        (tokens, own, other, out_bias, gain, shift, up, up_bias, down),
        flops=5 << 30,
    )


def weight_grad(table_ref, left_ref, right_ref, grad_ref, pieces):
    for xh in range(2):

        def product(rows, xh=xh):
            there = pl.ds(pl.multiple_of(rows.start + xh * 1024, 256), 256)
            grad_ref[there, :] = nn(left_ref[rows, :], right_ref[:, xh * 1024 : xh * 1024 + 1024]).astype(bf16)

        chunks(4, 256, product)
    split_blocks(table_ref, grad_ref, pieces)


def down_backward(table, normed_in, gain_in, shift_in, own, other, down_bias, gain, shift, cot, act):
    def kernel(table_ref, ni_ref, gi_ref, si_ref, own_ref, other_ref, db_ref, g_ref, s_ref, cot_ref, act_ref, layer_ref, grad_ref, low_ref, sums_ref, *rest):
        pieces, (flip_ref, full_ref) = rest[:5], rest[5:]
        sums_ref[...] = jnp.zeros_like(sums_ref)

        def norm(rows):
            hidden = ni_ref[rows, :] * gi_ref[...] + si_ref[...]
            residual = hidden + (own_ref[rows, :].astype(f32) + other_ref[rows, :].astype(f32)) + db_ref[...]
            normed, inverse = norm_stats(residual)
            layer_ref[rows, :] = normed * g_ref[...] + s_ref[...]
            cot_rows = cot_ref[rows, :].astype(f32)
            grad = norm_back(cot_rows, normed, inverse, g_ref[...])
            grad_ref[rows, :] = grad
            low_ref[rows, :] = grad.astype(bf16)
            sums_ref[0:1, :] += jnp.sum(grad, axis=0, keepdims=True)
            sums_ref[1:2, :] += jnp.sum(cot_rows * normed, axis=0, keepdims=True)
            sums_ref[2:3, :] += jnp.sum(cot_rows, axis=0, keepdims=True)

        chunks(4, 128, norm)
        flip_ref[...] = low_ref[...].T
        weight_grad(table_ref, flip_ref, act_ref, full_ref, pieces)

    return call(
        kernel,
        [((512, 1024), f32), ((512, 1024), f32), ((512, 1024), bf16), ((8, 1024), f32), *PIECES],
        (table, normed_in, gain_in, shift_in, own, other, down_bias, gain, shift, cot, act),
        scratch=[((1024, 512), bf16), ((2048, 1024), bf16)],
        scalars=1,
        flops=2 << 30,
    )


def hidden_backward(low, slope, down, up):
    def kernel(low_ref, slope_ref, down_ref, up_ref, pre_ref, sums_ref, part_ref):
        sums_ref[...] = jnp.zeros_like(sums_ref)
        for xh in range(2):
            cols = slice(xh * 1024, xh * 1024 + 1024)

            def activate(rows, xh=xh, cols=cols):
                act_grad = nn(low_ref[rows, :], down_ref[cols, :]).astype(bf16)
                pre_grad = act_grad.astype(f32) * slope_ref[rows, cols].astype(f32)
                sums_ref[xh : xh + 1, :] += jnp.sum(pre_grad, axis=0, keepdims=True)
                pre_ref[rows, cols] = pre_grad.astype(bf16)

            chunks(4, 128, activate)

        def project(rows):
            part_ref[rows, :] = (
                nt(pre_ref[rows, :1024], up_ref[:1024, :]) + nt(pre_ref[rows, 1024:], up_ref[1024:, :])
            ).astype(bf16)

        chunks(2, 256, project)

    return call(
        kernel,
        [((512, 2048), bf16), ((8, 1024), f32), ((512, 1024), bf16)],
        (low, slope, down, up),
        flops=4 << 30,
    )


def up_backward(table, hidden_low, pre_low):
    def kernel(table_ref, hid_ref, pre_ref, *rest):
        pieces, (flip_ref, full_ref) = rest[:5], rest[5:]
        flip_ref[...] = hid_ref[...].T
        weight_grad(table_ref, flip_ref, pre_ref, full_ref, pieces)

    return call(
        kernel,
        PIECES,
        (table, hidden_low, pre_low),
        scratch=[((1024, 512), bf16), ((2048, 1024), bf16)],
        scalars=1,
        flops=2 << 30,
    )


def attention_backward(table, grad_ffn, own, other, normed, inverse, gain, weights, tokens, queries, keys, values, context, probs):
    def kernel(table_ref, gf_ref, own_ref, other_ref, n_ref, inv_ref, g_ref, w_ref, x_ref, q_ref, k_ref, v_ref, ctx_ref, p_ref, ga_ref, d_ref, sums_ref, bias_ref, *rest):
        pieces, (low_ref, flip_ref, cg_ref, acc_ref, full_ref) = rest[:5], rest[5:]
        sums_ref[...] = jnp.zeros_like(sums_ref)
        bias_ref[...] = jnp.zeros_like(bias_ref)

        def norm(rows):
            hidden_grad = gf_ref[rows, :] + (own_ref[rows, :].astype(f32) + other_ref[rows, :].astype(f32))
            normed = n_ref[rows, :]
            grad = norm_back(hidden_grad, normed, inv_ref[rows, :1], g_ref[...])
            ga_ref[rows, :] = grad
            low_ref[rows, :] = grad.astype(bf16)
            sums_ref[0:1, :] += jnp.sum(grad, axis=0, keepdims=True)
            sums_ref[1:2, :] += jnp.sum(hidden_grad * normed, axis=0, keepdims=True)
            sums_ref[2:3, :] += jnp.sum(hidden_grad, axis=0, keepdims=True)

        chunks(4, 128, norm)
        for xh in range(2):
            cg_ref[:, xh * 256 : xh * 256 + 256] = nn(low_ref[...], w_ref[xh * 1024 : xh * 1024 + 1024, 768:]).astype(bf16)
        for pair in range(4):
            lanes = slice(pair * LANES, pair * LANES + LANES)
            acc_ref[...] = jnp.zeros_like(acc_ref)
            base = (pair // 2) * 768 + (pair % 2) * LANES

            def attend(rows, pair=pair, lanes=lanes, base=base):
                grad = cg_ref[rows, lanes]
                query = q_ref[rows, lanes]
                low_half = lax.broadcasted_iota(jnp.int32, grad.shape, 1) < HD
                query_grads = []
                for h in range(2):
                    keep = low_half == (h == 0)
                    grad_one = jnp.where(keep, grad, jnp.zeros_like(grad))
                    query_one = jnp.where(keep, query, jnp.zeros_like(query))
                    probs_low = p_ref[2 * pair + h, rows, :]
                    attn = probs_low.astype(f32)
                    prob_grad = nt(grad_one, v_ref[:, lanes])
                    row_dot = jnp.sum(attn * prob_grad, axis=-1, keepdims=True)
                    score_low = (attn * (prob_grad - row_dot) * HD**-0.5).astype(bf16)
                    query_grads.append(nn(score_low, k_ref[:, lanes]))
                    acc_ref[0] += nn(score_low.T, query_one)
                    acc_ref[1] += nn(probs_low.T, grad_one)
                query_grad = jnp.where(low_half, query_grads[0], query_grads[1])
                bias_ref[0:1, lanes] += jnp.sum(query_grad, axis=0, keepdims=True)
                d_ref[rows, base : base + LANES] = query_grad.astype(bf16)

            chunks(4, 128, attend)
            bias_ref[1:2, lanes] = jnp.sum(acc_ref[1], axis=0, keepdims=True)
            d_ref[:, base + 256 : base + 256 + LANES] = acc_ref[0].astype(bf16)
            d_ref[:, base + 512 : base + 512 + LANES] = acc_ref[1].astype(bf16)
        flip_ref[...] = low_ref[...].T
        for xh in range(2):

            def out_grad(rows, xh=xh):
                there = pl.ds(pl.multiple_of(rows.start + xh * 1024, 256), 256)
                full_ref[there, 768:] = nn(flip_ref[rows, :], ctx_ref[:, xh * 256 : xh * 256 + 256]).astype(bf16)

            chunks(4, 256, out_grad)
        flip_ref[...] = x_ref[...].T
        for xh in range(2):

            def qkv_grad(rows, xh=xh):
                there = pl.ds(pl.multiple_of(rows.start + xh * 1024, 256), 256)
                full_ref[there, :768] = nn(flip_ref[rows, :], d_ref[:, xh * 768 : xh * 768 + 768]).astype(bf16)

            chunks(4, 256, qkv_grad)
        split_blocks(table_ref, full_ref, pieces)

    return call(
        kernel,
        [((512, 1024), f32), ((512, 1536), bf16), ((8, 1024), f32), ((8, 512), f32), *PIECES],
        (table, grad_ffn, own, other, normed, inverse, gain, weights, tokens, queries, keys, values, context, probs),
        scratch=[((512, 1024), bf16), ((1024, 512), bf16), ((512, 512), bf16), ((2, 512, LANES), f32), ((2048, 1024), bf16)],
        scalars=1,
        flops=5 << 30,
    )


def input_backward(qkv_grad, weights):
    def kernel(d_ref, w_ref, part_ref):
        def project(rows):
            part_ref[rows, :] = nt(d_ref[rows, :768], w_ref[:1024, :768]) + nt(d_ref[rows, 768:], w_ref[1024:, :768])

        chunks(2, 256, project)

    return call(kernel, [((512, 1024), f32)], (qkv_grad, weights), flops=2 << 30)[0]


def body(
    tokens,
    seg_ids,
    qkv_weight,
    q_bias,
    v_bias,
    out_weight,
    out_bias,
    gain_attn,
    shift_attn,
    up_weight,
    up_bias,
    down_weight,
    down_bias,
    gain_ffn,
    shift_ffn,
    out_grad,
):
    length = seg_ids.shape[1]
    cols = tokens.shape[1]
    rows = qkv_weight.shape[0]
    xh = lax.axis_index("xh")
    core = lax.axis_index("core")
    place = {
        "x": xh * 2 + lax.axis_index("xl"),
        "y": lax.axis_index("y"),
        "z": lax.axis_index("z"),
        "core": core,
    }

    def pick(pair, index):
        return lax.dynamic_index_in_dim(pair, index, 0, keepdims=False)

    def ordered(own, other, index, axis):
        return jnp.where(
            index == 0, jnp.stack([own, other], axis), jnp.stack([other, own], axis)
        )

    def to_sequence(local):
        pair = local.reshape(2, length, cols)
        own, other = pick(pair, xh), swap_xh(pick(pair, 1 - xh))
        half = ordered(own, other, xh, 1)
        return ordered(half, swap_core(half), core, 2).reshape(length, 4 * cols)

    def own_blocks(full):
        return lax.dynamic_index_in_dim(
            full.reshape(*full.shape[:-1], 2, 2, cols), core, full.ndim, keepdims=False
        )

    def from_sequence(blocks, low):
        own = lax.dynamic_index_in_dim(blocks, xh, 1, keepdims=False)
        other = lax.dynamic_index_in_dim(blocks, 1 - xh, 1, keepdims=False)
        other = swap_xh(other.astype(low)).astype(f32)
        return ordered(own, other, xh, 0).reshape(2 * length, cols)

    attn_shard = jnp.concatenate(
        [qkv_weight.reshape(rows, 3 * cols), out_weight], 1
    ).astype(bf16)
    shards = {"attn": attn_shard, "up": up_weight.astype(bf16), "down": down_weight.astype(bf16)}
    tables = {group: block_table(group, place) for group in ORDER}

    def gathered(group):
        return assemble(tables[group], gather_group(shards[group], group))

    token_rows = to_sequence(tokens)
    vectors = jnp.concatenate(
        [q_bias, v_bias, out_bias, gain_attn, shift_attn, down_bias, gain_ffn, shift_ffn, up_bias]
    )
    vectors = ordered(vectors, swap_xh(vectors), xh, 0)
    both = ordered(vectors, swap_core(vectors), core, 1)
    q_bias_own, v_bias_own = vectors[:, :cols], vectors[:, cols : 2 * cols]
    up_bias_own = vectors[:, 8 * cols :]
    out_bias_all, gain_attn_all, shift_attn_all, down_bias_all, gain_ffn_all, shift_ffn_all = (
        both[:, :, i * cols : (i + 1) * cols].reshape(1, 4 * cols) for i in range(2, 8)
    )
    segment = pick(seg_ids, xh)

    attn_full = gathered("attn")
    up_full = gathered("up")
    down_full = gathered("down")
    cot_rows = to_sequence(out_grad.astype(bf16))

    queries, keys, values, context, probs, attn_part = attention_forward(
        token_rows, attn_full, q_bias_own, v_bias_own, segment[:, None], segment[None, :]
    )
    normed_attn, inverse_attn, hidden_low, activated, slope, ffn_part = ffn_forward(
        token_rows, attn_part, swap_core(attn_part), out_bias_all, gain_attn_all, shift_attn_all,
        up_full, up_bias_own, down_full,
    )
    layer_full, grad_resid_ffn, ffn_grad_low, ffn_sums, *down_pieces = down_backward(
        tables["down"], normed_attn, gain_attn_all, shift_attn_all, ffn_part, swap_core(ffn_part),
        down_bias_all, gain_ffn_all, shift_ffn_all, cot_rows, activated,
    )
    layer_out = from_sequence(own_blocks(layer_full), bf16)
    down_weight_grad = scatter_group(down_pieces, "down")
    pre_grad_low, up_sums, hidden_part = hidden_backward(ffn_grad_low, slope, down_full, up_full)
    up_pieces = up_backward(tables["up"], hidden_low, pre_grad_low)
    up_weight_grad = scatter_group(up_pieces, "up")
    grad_resid_attn, qkv_grad_low, attn_sums, head_sums, *attn_pieces = attention_backward(
        tables["attn"], grad_resid_ffn, hidden_part, swap_core(hidden_part), normed_attn, inverse_attn,
        gain_attn_all, attn_full, token_rows, queries, keys, values, context, probs,
    )
    attn_weight_grad = scatter_group(attn_pieces, "attn")
    input_part = input_backward(qkv_grad_low, attn_full)
    input_pair = input_part.reshape(length, 2, 2, cols)
    input_own = lax.dynamic_index_in_dim(input_pair, core, 2, keepdims=False)
    input_away = lax.dynamic_index_in_dim(input_pair, 1 - core, 2, keepdims=False)
    input_own = input_own + swap_core(input_away.astype(bf16)).astype(f32)
    input_grad = from_sequence(input_own + own_blocks(grad_resid_attn), bf16)

    head_sums = head_sums[:2].reshape(2, 2, cols)
    rows_of = (attn_sums[0], attn_sums[1], attn_sums[2], ffn_sums[0], ffn_sums[1], ffn_sums[2])
    vector_grads = jnp.concatenate(
        [head_sums[0], head_sums[1], *(own_blocks(row) for row in rows_of), up_sums[:2]], 1
    )
    total = pick(vector_grads, xh) + swap_xh(pick(vector_grads, 1 - xh))
    total = total + lax.ppermute(total, "xl", [(0, 1), (1, 0)])
    for axis in ("y", "z"):
        for bit in (1, 2):
            total = total + lax.ppermute(total, axis, [(i, i ^ bit) for i in range(4)])
    (
        q_bias_grad,
        v_bias_grad,
        out_bias_grad,
        gain_attn_grad,
        shift_attn_grad,
        down_bias_grad,
        gain_ffn_grad,
        shift_ffn_grad,
    ) = (total[i * cols : (i + 1) * cols] for i in range(8))
    up_bias_grad = total[8 * cols :]
    return (
        layer_out,
        input_grad,
        attn_weight_grad[:, : 3 * cols].reshape(rows, 3, cols),
        q_bias_grad,
        v_bias_grad,
        attn_weight_grad[:, 3 * cols :],
        out_bias_grad,
        gain_attn_grad,
        shift_attn_grad,
        up_weight_grad,
        up_bias_grad,
        down_weight_grad,
        down_bias_grad,
        gain_ffn_grad,
        shift_ffn_grad,
    )


def solution(mesh):
    placed_mesh = Mesh(mesh.devices.reshape(4, 4, 2, 2, 2), AXES)
    placed = (
        P(ROW, COL),
        P(ROW, None),
        P(ROW, None, COL),
        P(COL),
        P(COL),
        P(ROW, COL),
        P(COL),
        P(COL),
        P(COL),
        P(ROW, COL),
        P(COL),
        P(ROW, COL),
        P(COL),
        P(COL),
        P(COL),
        P(ROW, COL),
    )
    return jax.shard_map(
        body,
        mesh=placed_mesh,
        in_specs=placed,
        out_specs=(
            P(ROW, COL),
            P(ROW, COL),
            P(ROW, None, COL),
            P(COL),
            P(COL),
            P(ROW, COL),
            P(COL),
            P(COL),
            P(COL),
            P(ROW, COL),
            P(COL),
            P(ROW, COL),
            P(COL),
            P(COL),
            P(COL),
        ),
        check_vma=False,
    )
```

```python
import itertools

import jax
import jax.numpy as jnp
from jax import lax
from jax.experimental import pallas as pl
from jax.experimental.pallas import tpu as pltpu
from jax.sharding import Mesh, PartitionSpec as P

HD = 64
AXES = ("z", "y", "xl", "xh", "core")
ROW = ("z", "y", "xl")
COL = ("xh", "core")
CHIPS = ("z", "y", "xl", "xh")
lowest = -1e30
epsilon = 1e-06
bf16 = jnp.bfloat16
f32 = jnp.float32

GATHER = {"attn": ("xyz", "zyx"), "up": ("xyz", "zyx"), "down": ("xzy", "zxy")}
SCATTER = {"attn": ("xyz", "zyx"), "up": ("xyz", "zyx"), "down": ("xzy", "zxy")}
SHARED = ("x", "z")


def device_at(x, y, z, core):
    return ((z * 4 + y) * 2 + x % 2) * 4 + (x // 2) * 2 + core


def shifts(axes, step):
    pairs = []
    for x, y, z, core in itertools.product(range(4), range(4), range(4), range(2)):
        to = {"x": x, "y": y, "z": z}
        axis = axes[core]
        to[axis] = (to[axis] + (step if core == 0 else -step)) % 4
        pairs.append((device_at(x, y, z, core), device_at(to["x"], to["y"], to["z"], core)))
    return pairs


def send(value, axes, step):
    return lax.ppermute(value, AXES, shifts(axes, step))


def swap_core(value):
    return lax.ppermute(value, "core", [(0, 1), (1, 0)])


def swap_xh(value):
    return lax.ppermute(value, "xh", [(0, 1), (1, 0)])


def stage_axes(orders, group, stage):
    return (orders[group][0][stage], orders[group][1][stage])


def gather_direct(value, axes):
    return value, send(value, axes, -1), send(value, axes, 2), send(value, axes, 1)


def scatter_direct(pieces, axes):
    own, near, far, back = pieces
    return own, send(near, axes, 1), send(far, axes, 2), send(back, axes, -1)


def after(value, *others):
    return lax.optimization_barrier((value, *others))[0]


def quarters(value):
    quarter = value.shape[0] // 4
    return [value[i * quarter : (i + 1) * quarter] for i in range(4)]


def block_table(orders, group, place):
    index = jnp.arange(64, dtype=jnp.int32)
    offset = {0: index % 4, 1: (index // 4) % 4, 2: index // 16}
    tables = []
    for core in range(2):
        sign = 1 - 2 * core
        at = {}
        for stage in range(3):
            axis = orders[group][core][stage]
            at[axis] = (place[axis] + sign * offset[stage] + 4) % 4
        if group == "down":
            at["y"] = offset[2]
        tables.append(
            (((at["x"] // 2) * 4 + at["z"]) * 4 + at["y"]) * 2 + at["x"] % 2
        )
    return jnp.where(place["core"] == 0, tables[0], tables[1])


VMEM_LIMIT = 44 * 1024 * 1024
BLOCK = 32
VECTOR_ROWS = 16
LANES = 128


class Late:
    def __init__(self, source, target, sems, count, cols):
        rows = target.shape[0] // count
        if cols is not None:
            source = source.at[:, cols]
        self.target, self.copies = target, []
        for i in range(count):
            part = pl.ds(i * rows, rows)
            self.copies.append(pltpu.make_async_copy(source.at[part], target.at[part], sems.at[i]))
        for copy in self.copies:
            copy.start()

    def part(self, upto):
        while len(self.copies) and upto >= 0:
            self.copies.pop(0).wait()
            upto -= 1
        return self.target

    @property
    def ref(self):
        return self.part(len(self.copies))


class Far:
    def __init__(self, target, source, sems, count):
        rows = source.shape[0] // count
        self.ref, self.target, self.started, self.waiting = source, target, [], []
        for i in range(count):
            part = pl.ds(i * rows, rows)
            self.waiting.append(pltpu.make_async_copy(source.at[part], target.at[part], sems.at[i]))

    def push(self, count=None):
        for _ in range(len(self.waiting) if count is None else count):
            copy = self.waiting.pop(0)
            copy.start()
            self.started.append(copy)

    def finish(self):
        self.push()
        for copy in self.started:
            copy.wait()


def late(value, count=1, cols=None):
    return ("late", value, count, cols)


def far(shape, dtype, count=1):
    return ("far", shape, dtype, count)


def call(body, outs, args, scratch=()):
    in_specs, values, extra, lates = [], [], [], {}
    for i, arg in enumerate(args):
        if not isinstance(arg, tuple):
            scalar = arg.ndim == 1 and arg.dtype == jnp.int32
            in_specs.append(pl.BlockSpec(memory_space=pltpu.SMEM if scalar else pltpu.VMEM))
            values.append(arg)
            continue
        in_specs.append(pl.BlockSpec(memory_space=pl.ANY))
        values.append(arg[1])
        if arg[0] == "late":
            _, value, count, cols = arg
            shape = value.shape if cols is None else (value.shape[0], cols.stop - cols.start)
            lates[i] = (len(extra), count, cols)
            extra += [pltpu.VMEM(shape, value.dtype), pltpu.SemaphoreType.DMA((count,))]
    out_specs, shapes, fars = [], [], {}
    for i, out in enumerate(outs):
        if out[0] == "far":
            fars[i] = (len(extra), out[3])
            extra += [pltpu.VMEM(out[1], out[2]), pltpu.SemaphoreType.DMA((out[3],))]
        plain = out[0] not in ("far", "any")
        out_specs.append(pl.BlockSpec(memory_space=pltpu.VMEM if plain else pl.ANY))
        shapes.append(jax.ShapeDtypeStruct(*(out if plain else out[1:3])))

    def kernel(*refs):
        ins, rest = list(refs[: len(args)]), refs[len(args) :]
        results, rest = list(rest[: len(outs)]), rest[len(outs) :]
        own, rest = rest[: len(extra)], rest[len(extra) :]
        for i, (at, count, cols) in lates.items():
            ins[i] = Late(ins[i], own[at], own[at + 1], count, cols)
        for i, (at, count) in fars.items():
            results[i] = Far(results[i], own[at], own[at + 1], count)
        body(*ins, *results, *rest)
        for i in lates:
            ins[i].ref
        for i in fars:
            results[i].finish()

    return pl.pallas_call(
        kernel,
        out_shape=shapes,
        in_specs=in_specs,
        out_specs=out_specs,
        scratch_shapes=[*extra, *(s if not isinstance(s, tuple) else pltpu.VMEM(*s) for s in scratch)],
        compiler_params=pltpu.CompilerParams(vmem_limit_bytes=VMEM_LIMIT),
        cost_estimate=pl.CostEstimate(flops=4 << 30, bytes_accessed=1 << 22, transcendentals=0),
    )(*values)


def nn(left, right):
    return lax.dot_general(left, right, (((1,), (0,)), ((), ())), preferred_element_type=f32)


def nt(left, right):
    return lax.dot_general(left, right, (((1,), (1,)), ((), ())), preferred_element_type=f32)


def chunks(count, size, step):
    for i in range(count):
        step(slice(i * size, i * size + size))


def narrow(total):
    return [slice(start, start + 256) for start in range(0, total, 256)]


def place_blocks(table_ref, pieces, full_ref, sem):
    block = 0
    for piece in pieces:
        for row in range(0, piece.shape[0], BLOCK):
            there = pl.ds(pl.multiple_of(table_ref[block] * BLOCK, BLOCK), BLOCK)
            pltpu.make_async_copy(piece.at[pl.ds(row, BLOCK)], full_ref.at[there], sem).start()
            block += 1


def split_blocks(table_ref, grad_ref, pieces, cols):
    for block in range(64):
        row = (block % 16) * BLOCK
        there = pl.multiple_of(table_ref[block] * BLOCK, BLOCK)
        pieces[block // 16].ref[row : row + BLOCK, cols] = grad_ref[pl.ds(there, BLOCK), :]


def weight_grad(left_ref, right_ref, grad_ref):
    half = right_ref.shape[1] // 2
    for xh in range(2):
        for cols in narrow(half):
            from_cols = slice(xh * half + cols.start, xh * half + cols.stop)
            grad_ref[xh * 1024 : xh * 1024 + 1024, cols] = nn(left_ref[...], right_ref[:, from_cols]).astype(bf16)


def row_mean(value):
    return jnp.mean(value, axis=-1, keepdims=True)


def norm_stats(residual):
    center = residual - row_mean(residual)
    inverse = lax.rsqrt(row_mean(center * center) + epsilon)
    return center * inverse, inverse


def norm_back(grad, normed, inverse, gain):
    scaled = grad * gain
    return inverse * (scaled - row_mean(scaled) - normed * row_mean(scaled * normed))


def both(own_ref, other_ref, rows):
    return own_ref[rows, :].astype(f32) + other_ref[rows, :].astype(f32)


def round_weights(qkv_weight, out_weight, up_weight, down_weight):
    def kernel(qkv_ref, out_ref, up_ref, down_ref, low_ref):
        for j in range(3):
            low_ref[0:32, j * 256 : j * 256 + 256] = qkv_ref[:, j, :].astype(bf16)
        low_ref[0:32, 768:] = out_ref[...].astype(bf16)
        low_ref[32:64, :] = up_ref[...].astype(bf16)
        low_ref[64:96, :] = down_ref[...].astype(bf16)

    return call(kernel, [((96, 1024), bf16)], (qkv_weight, out_weight, up_weight, down_weight))[0]


def part_groups(pieces):
    def kernel(*refs):
        for group in range(3):
            for i in range(4):
                refs[4 + group][i * BLOCK : i * BLOCK + BLOCK, :] = refs[i][group * BLOCK : group * BLOCK + BLOCK, :]

    return call(kernel, [((128, 1024), bf16)] * 3, pieces)


def stack_four(pieces):
    def kernel(*refs):
        for i in range(4):
            refs[4][i * 128 : i * 128 + 128, :] = refs[i][...]

    return call(kernel, [((512, 1024), bf16)], pieces)[0]


def collect_tokens(blocks, own, partner, across, flip):
    def kernel(blocks_ref, own_ref, partner_ref, across_ref, out, *flipped):
        parts = (own_ref[...], partner_ref[...], across_ref[0], across_ref[1])
        for i in range(4):
            out.ref[:, pl.ds(pl.multiple_of(blocks_ref[i] * 256, 256), 256)] = parts[i]
        out.push()
        if flip:
            flipped[0].ref[...] = out.ref[...].T

    outs = [far((512, 1024), bf16)] + ([far((1024, 512), bf16)] if flip else [])
    return call(kernel, outs, (blocks, own, partner, across))


def stack_vectors(vectors, up_bias):
    def kernel(*refs):
        for i in range(8):
            refs[9][i : i + 1, :] = refs[i][...]
        for i in range(4):
            refs[9][8 + i : 9 + i, :] = refs[8][:, i * 256 : i * 256 + 256]
        refs[9][12:16, :] = jnp.zeros((4, 256), f32)

    args = [vector.reshape(1, -1) for vector in (*vectors, up_bias)]
    return call(kernel, [((16, 256), f32)], args)[0]


def collect_vectors(blocks, own, partner, across):
    def kernel(blocks_ref, own_ref, partner_ref, across_ref, rows_ref, mine_ref):
        parts = (own_ref[...], partner_ref[...], across_ref[0], across_ref[1])
        for i in range(4):
            rows_ref[:, pl.ds(pl.multiple_of(blocks_ref[i] * 256, 256), 256)] = parts[i][0:8, :]
        mine_ref[blocks_ref[6]] = parts[0]
        mine_ref[1 - blocks_ref[6]] = parts[1]

    return call(kernel, [((8, 1024), f32), ((2, 16, 256), f32)], (blocks, own, partner, across))


def attention_forward(table, tokens, pieces, mine, seg_col, seg_row):
    def kernel(table_ref, x, p0, p1, p2, p3, mine_ref, sc_ref, sr_ref, weights, q, k, v, ctx, probs, part_ref, mask_ref, sem):
        place_blocks(table_ref, (p0, p1, p2, p3), weights.ref, sem)
        mask_ref[...] = jnp.where(sc_ref[...] == sr_ref[...], 0.0, lowest)
        x_ref = x.ref
        pltpu.make_async_copy(weights.target, weights.ref, sem).wait()
        weights.push()
        for xh in range(2):
            cols = slice(xh * 256, xh * 256 + 256)
            w = weights.ref.at[xh * 1024 : xh * 1024 + 1024]
            q.ref[:, cols] = (nn(x_ref[...], w[:, :256]) + mine_ref[xh, 0:1, :]).astype(bf16)
            k.ref[:, cols] = nn(x_ref[...], w[:, 256:512]).astype(bf16)
            v.ref[:, cols] = (nn(x_ref[...], w[:, 512:768]) + mine_ref[xh, 1:2, :]).astype(bf16)
        for result in (q, k, v):
            result.push()
        for pair in range(4):
            lanes = slice(pair * LANES, pair * LANES + LANES)
            for start in range(0, 512, 256):
                rows = slice(start, start + 256)
                query = q.ref[rows, lanes]
                low_half = lax.broadcasted_iota(jnp.int32, query.shape, 1) < HD
                parts = []
                for h in range(2):
                    one = jnp.where(low_half == (h == 0), query, jnp.zeros_like(query)) * HD**-0.5
                    scores = nt(one.astype(bf16), k.ref[:, lanes]) + mask_ref[rows, :]
                    shifted = jnp.exp(scores - jnp.max(scores, axis=-1, keepdims=True))
                    inverse = 1.0 / jnp.sum(shifted, axis=-1, keepdims=True)
                    probs_low = (shifted * inverse).astype(bf16)
                    probs.ref[2 * pair + h, rows, :] = probs_low
                    parts.append(nn(probs_low, v.ref[:, lanes]))
                ctx.ref[rows, lanes] = jnp.where(low_half, parts[0], parts[1]).astype(bf16)
            probs.push(1)
        ctx.push()
        for out in narrow(1024):
            low = slice(out.start + 1024, out.stop + 1024)
            part_ref[:, out] = (
                nt(ctx.ref[:, :256], weights.ref[out, 768:]) + nt(ctx.ref[:, 256:], weights.ref[low, 768:])
            ).astype(bf16)

    return call(
        kernel,
        [far((2048, 1024), bf16), *[far((512, 512), bf16)] * 4, far((8, 512, 512), bf16, 4), ((512, 1024), bf16)],
        (table, late(tokens), *(("any", piece) for piece in pieces), mine, seg_col, seg_row),
        scratch=[((512, 512), f32), pltpu.SemaphoreType.DMA],
    )


def ffn_forward(up_table, down_table, tokens, own, other, vectors, mine, up_pieces, down_piece):
    def kernel(ut_ref, dt_ref, x, own_ref, other_ref, vec_ref, mine_ref, u0, u1, u2, u3, d0, up, down, normed, inv_ref, hidden, act, slope, part_ref, up_sem, down_sem):
        place_blocks(ut_ref, (u0, u1, u2, u3), up.ref, up_sem)
        place_blocks(dt_ref, (d0,), down.ref, down_sem)
        x_ref = x.ref

        def norm(rows):
            residual = x_ref[rows, :].astype(f32) + both(own_ref, other_ref, rows) + vec_ref[2:3, :]
            centered, inverse = norm_stats(residual)
            normed.ref[rows, :] = centered
            inv_ref[rows, :] = jnp.broadcast_to(inverse, (inverse.shape[0], LANES))
            hidden.ref[rows, :] = (centered * vec_ref[3:4, :] + vec_ref[4:5, :]).astype(bf16)

        chunks(4, 128, norm)
        normed.push()
        hidden.push()
        pltpu.make_async_copy(up.target, up.ref, up_sem).wait()
        up.push()
        for xh in range(2):
            for i, out in enumerate(narrow(1024)):
                cols = slice(xh * 1024 + out.start, xh * 1024 + out.stop)
                pre_act = nn(hidden.ref[...], up.ref[xh * 1024 : xh * 1024 + 1024, out]) + mine_ref[xh, 8 + i : 9 + i, :]
                cumulative = 0.5 * (1.0 + lax.erf(pre_act * 0.7071067811865476))
                density = jnp.exp(-0.5 * pre_act * pre_act) * 0.3989422804014327
                act.ref[:, cols] = (pre_act * cumulative).astype(bf16)
                slope.ref[:, cols] = (cumulative + pre_act * density).astype(bf16)
        act.push()
        slope.push()
        pltpu.make_async_copy(down.target, down.ref, down_sem).wait()
        down.push()
        for out in narrow(1024):
            low = slice(out.start + 1024, out.stop + 1024)
            part_ref[:, out] = (
                nt(act.ref[:, :1024], down.ref[out, :]) + nt(act.ref[:, 1024:], down.ref[low, :])
            ).astype(bf16)

    return call(
        kernel,
        [
            far((2048, 1024), bf16),
            far((2048, 1024), bf16),
            far((512, 1024), f32),
            ((512, LANES), f32),
            far((512, 1024), bf16),
            far((512, 2048), bf16),
            far((512, 2048), bf16),
            ((512, 1024), bf16),
        ],
        (up_table, down_table, late(tokens), own, other, vectors, mine, *(("any", piece) for piece in up_pieces), ("any", down_piece)),
        scratch=[pltpu.SemaphoreType.DMA, pltpu.SemaphoreType.DMA],
    )


def ffn_backward(table, blocks, normed_in, own, other, vectors, cot, act, down, slope, up):
    def kernel(table_ref, blocks_ref, ni, own_ref, other_ref, vec_ref, cot_late, act_late, down_late, slope_late, up_late, keep_ref, away_ref, grad, low_ref, sums_ref, hidden_sums_ref, pre, part_ref, piece_ref, flip_ref, full_ref, layer_ref, sem):
        sums_ref[...] = jnp.zeros_like(sums_ref)
        hidden_sums_ref[...] = jnp.zeros_like(hidden_sums_ref)
        ni_ref, cot_ref = ni.ref, cot_late.ref

        def norm(rows):
            hidden = ni_ref[rows, :] * vec_ref[3:4, :] + vec_ref[4:5, :]
            residual = hidden + both(own_ref, other_ref, rows) + vec_ref[5:6, :]
            normed, inverse = norm_stats(residual)
            layer_ref[rows, :] = normed * vec_ref[6:7, :] + vec_ref[7:8, :]
            cot_rows = cot_ref[rows, :].astype(f32)
            grad_rows = norm_back(cot_rows, normed, inverse, vec_ref[6:7, :])
            grad.ref[rows, :] = grad_rows
            low_ref[rows, :] = grad_rows.astype(bf16)
            sums_ref[0:1, :] += jnp.sum(grad_rows, axis=0, keepdims=True)
            sums_ref[1:2, :] += jnp.sum(cot_rows * normed, axis=0, keepdims=True)
            sums_ref[2:3, :] += jnp.sum(cot_rows, axis=0, keepdims=True)

        chunks(4, 128, norm)
        grad.push()
        flip_ref[...] = low_ref[...].T
        weight_grad(flip_ref, act_late.ref, full_ref)
        for block in range(64):
            there = pl.ds(pl.multiple_of(table_ref[block] * BLOCK, BLOCK), BLOCK)
            pltpu.make_async_copy(full_ref.at[there], piece_ref.at[pl.ds(block * BLOCK, BLOCK)], sem).start()
        keep_ref[...] = layer_ref[:, pl.ds(pl.multiple_of(blocks_ref[0] * 256, 256), 256)]
        away_ref[...] = layer_ref[:, pl.ds(pl.multiple_of(blocks_ref[1] * 256, 256), 256)].astype(bf16)
        down_ref, slope_ref = down_late.ref, slope_late.ref
        for xh in range(2):
            for out in narrow(1024):
                cols = slice(xh * 1024 + out.start, xh * 1024 + out.stop)
                act_grad = nn(low_ref[...], down_ref[xh * 1024 : xh * 1024 + 1024, out]).astype(bf16)
                pre_grad = act_grad.astype(f32) * slope_ref[:, cols].astype(f32)
                hidden_sums_ref[xh : xh + 1, out] = jnp.sum(pre_grad, axis=0, keepdims=True)
                pre.ref[:, cols] = pre_grad.astype(bf16)
        pre.push()
        up_ref = up_late.ref
        for out in narrow(1024):
            low = slice(out.start + 1024, out.stop + 1024)
            part_ref[:, out] = (
                nt(pre.ref[:, :1024], up_ref[out, :]) + nt(pre.ref[:, 1024:], up_ref[low, :])
            ).astype(bf16)
        pltpu.make_async_copy(full_ref, piece_ref, sem).wait()

    return call(
        kernel,
        [
            ((512, 256), f32),
            ((512, 256), bf16),
            far((512, 1024), f32),
            ((512, 1024), bf16),
            ((8, 1024), f32),
            ((8, 1024), f32),
            far((512, 2048), bf16),
            ((512, 1024), bf16),
            ("any", (2048, 1024), bf16),
        ],
        (table, blocks, late(normed_in), own, other, vectors, late(cot), late(act), late(down), late(slope), late(up)),
        scratch=[((1024, 512), bf16), ((2048, 1024), bf16), ((512, 1024), f32), pltpu.SemaphoreType.DMA],
    )


def up_backward(hidden_low, pre_low):
    def kernel(hidden, pre, full_ref, flip_ref):
        flip_ref[...] = hidden.ref[...].T
        weight_grad(flip_ref, pre.ref, full_ref)

    return call(
        kernel, [((2048, 1024), bf16)], (late(hidden_low), late(pre_low)), scratch=[((1024, 512), bf16)]
    )[0]


def out_backward(table, grad_ffn, own, other, normed_in, inverse, vectors, weights, context, up_grad):
    def kernel(table_ref, gf, own_ref, other_ref, ni, inv_ref, vec_ref, w, ctx, up_ref, ga, cg_ref, sums_ref, o0, o1, o2, o3, low_ref, flip_ref, full_ref):
        pieces = (o0, o1, o2, o3)
        sums_ref[...] = jnp.zeros_like(sums_ref)
        gf_ref, n_ref = gf.ref, ni.ref

        def norm(rows):
            hidden_grad = gf_ref[rows, :] + both(own_ref, other_ref, rows)
            normed = n_ref[rows, :]
            grad = norm_back(hidden_grad, normed, inv_ref[rows, :1], vec_ref[3:4, :])
            ga.ref[rows, :] = grad
            low_ref[rows, :] = grad.astype(bf16)
            sums_ref[0:1, :] += jnp.sum(grad, axis=0, keepdims=True)
            sums_ref[1:2, :] += jnp.sum(hidden_grad * normed, axis=0, keepdims=True)
            sums_ref[2:3, :] += jnp.sum(hidden_grad, axis=0, keepdims=True)

        chunks(4, 128, norm)
        ga.push()
        flip_ref[...] = low_ref[...].T
        weight_grad(flip_ref, ctx.ref, full_ref)
        split_blocks(table_ref, up_ref, pieces, slice(0, 1024))
        split_blocks(table_ref, full_ref, pieces, slice(1024, 1280))
        for piece in pieces:
            piece.push()
        w_ref = w.ref
        for xh in range(2):
            cg_ref[:, xh * 256 : xh * 256 + 256] = nn(low_ref[...], w_ref[xh * 1024 : xh * 1024 + 1024, :]).astype(bf16)

    return call(
        kernel,
        [far((512, 1024), f32), ((512, 512), bf16), ((8, 1024), f32), *[far((512, 1280), bf16)] * 4],
        (table, late(grad_ffn), own, other, late(normed_in), inverse, vectors, late(weights, 1, slice(768, 1024)), late(context), up_grad),
        scratch=[((512, 1024), bf16), ((1024, 512), bf16), ((2048, 256), bf16)],
    )


def attention_backward(table, blocks, queries, keys, values, context_grad, probs, flip, weights, grad_attn, attn_sums, ffn_sums, hidden_sums):
    def kernel(table_ref, blocks_ref, q, k, v, cg_ref, probs, flip, w, ga, as_ref, fs_ref, hs_ref, keep_ref, away_ref, o0, o1, o2, o3, full_ref, d_ref, part_ref, bias_ref, vec_ref):
        pieces = (o0, o1, o2, o3)
        bias_ref[...] = jnp.zeros_like(bias_ref)
        q_ref, k_ref, v_ref = q.ref, k.ref, v.ref
        for pair in range(4):
            lanes = slice(pair * LANES, pair * LANES + LANES)
            base = (pair // 2) * 768 + (pair % 2) * LANES
            p_ref = probs.part(0)
            key_flips, value_flips = [0.0, 0.0], [0.0, 0.0]
            for start in range(0, 512, 256):
                rows = slice(start, start + 256)
                grad = cg_ref[rows, lanes]
                grad_flip = grad.T
                query_flip = q_ref[rows, lanes].T
                low_half = lax.broadcasted_iota(jnp.int32, grad.shape, 1) < HD
                query_grads = []
                for h in range(2):
                    one = slice(h * HD, h * HD + HD)
                    grad_one = jnp.where(low_half == (h == 0), grad, jnp.zeros_like(grad))
                    probs_low = p_ref[2 * pair + h, rows, :]
                    attn = probs_low.astype(f32)
                    prob_grad = nt(grad_one, v_ref[:, lanes])
                    row_dot = jnp.sum(attn * prob_grad, axis=-1, keepdims=True)
                    score_low = (attn * (prob_grad - row_dot) * HD**-0.5).astype(bf16)
                    query_grads.append(nn(score_low, k_ref[:, lanes]))
                    key_flips[h] = key_flips[h] + nn(query_flip[one], score_low)
                    value_flips[h] = value_flips[h] + nn(grad_flip[one], probs_low)
                query_grad = jnp.where(low_half, query_grads[0], query_grads[1])
                bias_ref[0:1, lanes] += jnp.sum(query_grad, axis=0, keepdims=True)
                d_ref[rows, base : base + LANES] = query_grad.astype(bf16)
            key_grad = jnp.concatenate(key_flips, 0).T
            value_grad = jnp.concatenate(value_flips, 0).T
            bias_ref[1:2, lanes] = jnp.sum(value_grad, axis=0, keepdims=True)
            d_ref[:, base + 256 : base + 256 + LANES] = key_grad.astype(bf16)
            d_ref[:, base + 512 : base + 512 + LANES] = value_grad.astype(bf16)
        for xh in range(2):
            own = pl.ds(pl.multiple_of(blocks_ref[4 + xh] * 256, 256), 256)
            here = slice(xh * 256, xh * 256 + 256)
            parts = [bias_ref[0:1, here], bias_ref[1:2, here]]
            parts += [ref[i : i + 1, own] for ref in (as_ref, fs_ref) for i in range(3)]
            parts += [hs_ref[xh : xh + 1, out] for out in narrow(1024)]
            for i, part in enumerate(parts):
                vec_ref[xh * 4 + i // 3 : xh * 4 + i // 3 + 1, (i % 3) * 256 : (i % 3) * 256 + 256] = part
        vec_ref[8:16, :] = jnp.zeros((8, 768), f32)
        for piece in pieces:
            piece.ref[512:528, :] = vec_ref[...].astype(bf16)
        weight_grad(flip.ref, d_ref, full_ref)
        split_blocks(table_ref, full_ref, pieces, slice(None))
        for piece in pieces:
            piece.push()
        w_ref, ga_ref = w.ref, ga.ref
        for out in narrow(1024):
            low = slice(out.start + 1024, out.stop + 1024)
            part_ref[:, out] = nt(d_ref[:, :768], w_ref[out, :]) + nt(d_ref[:, 768:], w_ref[low, :])
        for i in range(2):
            own = pl.ds(pl.multiple_of(blocks_ref[i] * 256, 256), 256)
            across = pl.ds(pl.multiple_of(blocks_ref[2 + i] * 256, 256), 256)
            keep_ref[i, :, :] = part_ref[:, own] + ga_ref[:, own]
            away_ref[i, :, :] = part_ref[:, across].astype(bf16)

    return call(
        kernel,
        [((2, 512, 256), f32), ((2, 512, 256), bf16), *[far((528, 768), bf16)] * 4],
        (table, blocks, late(queries), late(keys), late(values), context_grad, late(probs, 4), late(flip), late(weights, 1, slice(0, 768)), late(grad_attn), attn_sums, ffn_sums, hidden_sums),
        scratch=[((2048, 768), bf16), ((512, 1536), bf16), ((512, 1024), f32), ((8, 512), f32), ((16, 768), f32)],
    )


def add_refs(refs, rows, cols=slice(None)):
    total = refs[0][rows, cols].astype(f32)
    for ref in refs[1:]:
        total = total + ref[rows, cols].astype(f32)
    return total


def add_split(parts, tail):
    rows, width = parts[0].shape
    quarter = (rows - tail) // 4

    def kernel(*refs):
        ins, outs = refs[:4], refs[4:]
        for i in range(4):
            outs[i][0:quarter, :] = add_refs(ins, slice(i * quarter, i * quarter + quarter)).astype(bf16)
        if tail:
            vectors = add_refs(ins, slice(4 * quarter, rows)).astype(bf16)
            for i in range(4):
                outs[i][quarter : quarter + tail, :] = vectors

    return call(kernel, [((quarter + tail, width), bf16)] * 4, parts)


def merge_groups(attn, up, down):
    def kernel(*refs):
        ins, outs = (refs[0:4], refs[4:8], refs[8:12]), refs[12:]
        vectors = add_refs(ins[0], slice(128, 128 + VECTOR_ROWS)).astype(bf16)
        for i in range(4):
            rows = slice(i * BLOCK, i * BLOCK + BLOCK)
            outs[i][0:BLOCK, 0:768] = add_refs(ins[0], rows).astype(bf16)
            outs[i][0:BLOCK, 768:2048] = add_refs(ins[1], rows).astype(bf16)
            outs[i][0:BLOCK, 2048:3072] = add_refs(ins[2], rows).astype(bf16)
            outs[i][BLOCK : BLOCK + VECTOR_ROWS, 0:768] = vectors
            outs[i][BLOCK : BLOCK + VECTOR_ROWS, 768:] = jnp.zeros((VECTOR_ROWS, 2304), bf16)

    return call(kernel, [((BLOCK + VECTOR_ROWS, 3072), bf16)] * 4, (*attn, *up, *down))


def final_sums(blocks, parts):
    def kernel(blocks_ref, *refs):
        ins, (qkv_ref, out_ref, up_ref, down_ref, *vectors) = refs[:4], refs[4:]
        rows = slice(0, BLOCK)
        for j in range(3):
            qkv_ref[:, j, :] = add_refs(ins, rows, slice(j * 256, j * 256 + 256))
        up_ref[...] = add_refs(ins, rows, slice(768, 1792))
        out_ref[...] = add_refs(ins, rows, slice(1792, 2048))
        down_ref[...] = add_refs(ins, rows, slice(2048, 3072))
        sums = add_refs(ins, slice(BLOCK, BLOCK + VECTOR_ROWS), slice(0, 768))
        sums = jnp.where(blocks_ref[6] == 0, sums[0:4], sums[4:8])
        for i in range(12):
            value = sums[i // 3 : i // 3 + 1, (i % 3) * 256 : (i % 3) * 256 + 256]
            if i < 8:
                vectors[i][...] = value
            else:
                vectors[8][:, (i - 8) * 256 : (i - 8) * 256 + 256] = value

    wide = ((BLOCK, 1024), f32)
    outs = [((BLOCK, 3, 256), f32), ((BLOCK, 256), f32), wide, wide, *[((1, 256), f32)] * 8, ((1, 1024), f32)]
    return call(kernel, outs, (blocks, *parts))


def body(
    tokens,
    seg_ids,
    qkv_weight,
    q_bias,
    v_bias,
    out_weight,
    out_bias,
    gain_attn,
    shift_attn,
    up_weight,
    up_bias,
    down_weight,
    down_bias,
    gain_ffn,
    shift_ffn,
    out_grad,
):
    length = seg_ids.shape[1]
    cols = tokens.shape[1]
    xh = lax.axis_index("xh")
    core = lax.axis_index("core")
    place = {
        "x": xh * 2 + lax.axis_index("xl"),
        "y": lax.axis_index("y"),
        "z": lax.axis_index("z"),
        "core": core,
    }
    tables = {group: block_table(GATHER, group, place) for group in GATHER}
    back_tables = {group: block_table(SCATTER, group, place) for group in SCATTER}
    blocks = jnp.stack(
        [xh * 2 + core, 2 - xh * 2 + core, xh * 2 + 1 - core, 3 - xh * 2 - core, core, 2 + core, xh]
    ).astype(jnp.int32)

    def one_sequence(local, flip, wait=None):
        pair = local.reshape(2, length, cols)
        own = lax.dynamic_index_in_dim(pair, xh, 0, keepdims=False)
        away = lax.dynamic_index_in_dim(pair, 1 - xh, 0, keepdims=False)
        if wait is not None:
            away = after(away, wait)
        partner = swap_xh(away)
        return collect_tokens(blocks, own, partner, swap_core(jnp.stack([own, partner])), flip)

    def two_sequences(own, partner):
        partner = partner.astype(f32)
        return jnp.where(xh == 0, jnp.stack([own, partner]), jnp.stack([partner, own])).reshape(2 * length, cols)

    first = gather_direct(round_weights(qkv_weight, out_weight, up_weight, down_weight), SHARED)
    level = dict(zip(("attn", "up", "down"), part_groups(first)))
    attn_second = gather_direct(level["attn"], stage_axes(GATHER, "attn", 1))
    token_rows, token_flip = one_sequence(tokens, True)
    attn_pieces = gather_direct(stack_four(attn_second), stage_axes(GATHER, "attn", 2))
    level["down"] = after(level["down"], attn_second[1])
    down_second = stack_four(gather_direct(level["down"], stage_axes(GATHER, "down", 1)))
    down_piece = lax.all_gather(down_second, "y", axis=0, tiled=True)
    level["up"] = after(level["up"], *attn_second[1:])
    up_second = stack_four(gather_direct(level["up"], stage_axes(GATHER, "up", 1)))
    up_pieces = gather_direct(up_second, stage_axes(GATHER, "up", 2))

    vectors = stack_vectors(
        (q_bias, v_bias, out_bias, gain_attn, shift_attn, down_bias, gain_ffn, shift_ffn), up_bias
    )
    vectors = after(vectors, *attn_second[1:])
    partner = swap_xh(vectors)
    rows, mine = collect_vectors(blocks, vectors, partner, swap_core(jnp.stack([vectors, partner])))
    segment = lax.dynamic_index_in_dim(seg_ids, xh, 0, keepdims=False)

    attn_full, queries, keys, values, context, probs, attn_part = attention_forward(
        tables["attn"], token_rows, attn_pieces, mine, segment[:, None], segment[None, :]
    )
    (cot_rows,) = one_sequence(out_grad.astype(bf16), False, attn_pieces[3])
    up_full, down_full, normed_attn, inverse_attn, hidden_low, activated, slope, ffn_part = ffn_forward(
        tables["up"], tables["down"], token_rows, attn_part, swap_core(attn_part), rows, mine, up_pieces, down_piece
    )
    (
        layer_own,
        layer_away,
        grad_resid_ffn,
        ffn_grad_low,
        ffn_sums,
        hidden_sums,
        pre_grad_low,
        hidden_part,
        down_blocks,
    ) = ffn_backward(
        back_tables["down"], blocks, normed_attn, ffn_part, swap_core(ffn_part), rows, cot_rows, activated,
        down_full, slope, up_full,
    )
    del ffn_grad_low
    up_grad = up_backward(hidden_low, pre_grad_low)
    grad_resid_attn, context_grad, attn_sums, *up_parts = out_backward(
        back_tables["up"], grad_resid_ffn, hidden_part, swap_core(hidden_part), normed_attn, inverse_attn,
        rows, attn_full, context, up_grad,
    )
    input_own, input_away, *attn_parts = attention_backward(
        back_tables["attn"], blocks, queries, keys, values, context_grad, probs, token_flip, attn_full,
        grad_resid_attn, attn_sums, ffn_sums, hidden_sums,
    )
    down_part = lax.psum_scatter(down_blocks, "y", scatter_dimension=0, tiled=True)
    up_parts = scatter_direct(up_parts, stage_axes(SCATTER, "up", 2))
    attn_parts = lax.optimization_barrier((*attn_parts, *up_parts[1:]))[:4]
    input_away = after(input_away, attn_parts[0])
    attn_parts = scatter_direct(attn_parts, stage_axes(SCATTER, "attn", 2))
    up_parts = scatter_direct(add_split(up_parts, 0), stage_axes(SCATTER, "up", 1))
    input_own = input_own + swap_core(input_away).astype(f32)
    attn_parts = add_split(attn_parts, VECTOR_ROWS)
    attn_parts = lax.optimization_barrier((*attn_parts, *up_parts[1:], down_part))
    down_part = attn_parts[7]
    attn_parts = scatter_direct(attn_parts[:4], stage_axes(SCATTER, "attn", 1))
    down_parts = scatter_direct(quarters(down_part), stage_axes(SCATTER, "down", 1))
    input_away = after(input_own[1].astype(bf16), attn_parts[1])
    input_grad = two_sequences(input_own[0], swap_xh(input_away))
    layer_out = two_sequences(layer_own, swap_xh(after(layer_away, attn_parts[1])))
    last = scatter_direct(merge_groups(attn_parts, up_parts, down_parts), SHARED)
    qkv_grad, out_grad_rows, up_rows, down_rows, *sums = final_sums(blocks, last)
    (
        q_bias_grad,
        v_bias_grad,
        out_bias_grad,
        gain_attn_grad,
        shift_attn_grad,
        down_bias_grad,
        gain_ffn_grad,
        shift_ffn_grad,
        up_bias_grad,
    ) = (value.reshape(-1) for value in sums)
    return (
        layer_out,
        input_grad,
        qkv_grad,
        q_bias_grad,
        v_bias_grad,
        out_grad_rows,
        out_bias_grad,
        gain_attn_grad,
        shift_attn_grad,
        up_rows,
        up_bias_grad,
        down_rows,
        down_bias_grad,
        gain_ffn_grad,
        shift_ffn_grad,
    )


def solution(mesh):
    placed_mesh = Mesh(mesh.devices.reshape(4, 4, 2, 2, 2), AXES)
    placed = (
        P(ROW, COL),
        P(ROW, None),
        P(ROW, None, COL),
        P(COL),
        P(COL),
        P(ROW, COL),
        P(COL),
        P(COL),
        P(COL),
        P(ROW, COL),
        P(COL),
        P(ROW, COL),
        P(COL),
        P(COL),
        P(COL),
        P(ROW, COL),
    )
    return jax.shard_map(
        body,
        mesh=placed_mesh,
        in_specs=placed,
        out_specs=(
            P(ROW, COL),
            P(ROW, COL),
            P(ROW, None, COL),
            P(COL),
            P(COL),
            P(ROW, COL),
            P(COL),
            P(COL),
            P(COL),
            P(ROW, COL),
            P(COL),
            P(ROW, COL),
            P(COL),
            P(COL),
            P(COL),
        ),
        check_vma=False,
    )
```

```python
import itertools

import jax
import jax.numpy as jnp
from jax import lax
from jax.experimental import pallas as pl
from jax.experimental.pallas import tpu as pltpu
from jax.sharding import Mesh, PartitionSpec as P

HD = 64
AXES = ("z", "y", "xl", "xh", "core")
ROW = ("z", "y", "xl")
COL = ("xh", "core")
CHIPS = ("z", "y", "xl", "xh")
lowest = -1e30
epsilon = 1e-06
bf16 = jnp.bfloat16
f32 = jnp.float32

STAGES = (("x", "z"), ("y", "y"), ("z", "x"))
DOWN_STAGES = (("x", "z"), ("z", "x"), ("y", "y"))


def device_at(x, y, z, core):
    return ((z * 4 + y) * 2 + x % 2) * 4 + (x // 2) * 2 + core


def shifts(axes, step):
    pairs = []
    for x, y, z, core in itertools.product(range(4), range(4), range(4), range(2)):
        to = {"x": x, "y": y, "z": z}
        axis = axes[core]
        to[axis] = (to[axis] + (step if core == 0 else -step)) % 4
        pairs.append((device_at(x, y, z, core), device_at(to["x"], to["y"], to["z"], core)))
    return pairs


def send(value, axes, step):
    return lax.ppermute(value, AXES, shifts(axes, step))


def swap_core(value):
    return lax.ppermute(value, "core", [(0, 1), (1, 0)])


def swap_xh(value):
    return lax.ppermute(value, "xh", [(0, 1), (1, 0)])


def gather_direct(value, axes):
    return value, send(value, axes, -1), send(value, axes, 2), send(value, axes, 1)


def gather_halves(first, second, axes):
    down = [send(first, axes, 1)]
    up = [send(second, axes, -1)]
    far = send(down[0], axes, 1), send(up[0], axes, -1)
    down.append(send(second, axes, 1))
    up.insert(0, send(first, axes, -1))
    return first, second, *up, *far, *down


def scatter_direct(pieces, axes):
    own, near, far, back = pieces
    return own, send(near, axes, 1), send(far, axes, 2), send(back, axes, -1)


def after(value, *others):
    return lax.optimization_barrier((value, *others))[0]


def quarters(value):
    quarter = value.shape[0] // 4
    return [value[i * quarter : (i + 1) * quarter] for i in range(4)]


def block_table(stages, place):
    index = jnp.arange(64, dtype=jnp.int32)
    offset = (index % 4, (index // 4) % 4, index // 16)
    tables = []
    for core in range(2):
        at = {}
        for stage in range(3):
            axis = stages[stage][core]
            at[axis] = (place[axis] + (1 - 2 * core) * offset[stage] + 4) % 4
        tables.append((((at["x"] // 2) * 4 + at["z"]) * 4 + at["y"]) * 2 + at["x"] % 2)
    return jnp.where(place["core"] == 0, tables[0], tables[1])


MIB = 1024 * 1024
BLOCK = 32
VECTOR_ROWS = 16
LANES = 128


class Late:
    def __init__(self, source, target, sems, count, cols):
        rows = target.shape[0] // count
        if cols is not None:
            source = source.at[:, cols]
        self.target, self.copies = target, []
        for i in range(count):
            part = pl.ds(i * rows, rows)
            self.copies.append(pltpu.make_async_copy(source.at[part], target.at[part], sems.at[i]))
        for copy in self.copies:
            copy.start()

    def part(self, upto):
        while len(self.copies) and upto >= 0:
            self.copies.pop(0).wait()
            upto -= 1
        return self.target

    @property
    def ref(self):
        return self.part(len(self.copies))


class Far:
    def __init__(self, target, source, sems, count):
        rows = source.shape[0] // count
        self.ref, self.target, self.started, self.waiting = source, target, [], []
        for i in range(count):
            part = pl.ds(i * rows, rows)
            self.waiting.append(pltpu.make_async_copy(source.at[part], target.at[part], sems.at[i]))

    def push(self, count=None):
        for _ in range(len(self.waiting) if count is None else count):
            copy = self.waiting.pop(0)
            copy.start()
            self.started.append(copy)

    def finish(self):
        self.push()
        for copy in self.started:
            copy.wait()


def late(value, count=1, cols=None):
    return ("late", value, count, cols)


def far(shape, dtype, count=1):
    return ("far", shape, dtype, count)


def call(body, outs, args, scratch=(), flops=1 << 20, limit=12):
    in_specs, values, extra, lates = [], [], [], {}
    for i, arg in enumerate(args):
        if not isinstance(arg, tuple):
            scalar = arg.ndim == 1 and arg.dtype == jnp.int32
            in_specs.append(pl.BlockSpec(memory_space=pltpu.SMEM if scalar else pltpu.VMEM))
            values.append(arg)
            continue
        in_specs.append(pl.BlockSpec(memory_space=pltpu.HBM))
        values.append(arg[1])
        if arg[0] == "late":
            _, value, count, cols = arg
            shape = value.shape if cols is None else (value.shape[0], cols.stop - cols.start)
            lates[i] = (len(extra), count, cols)
            extra += [pltpu.VMEM(shape, value.dtype), pltpu.SemaphoreType.DMA((count,))]
    out_specs, shapes, fars = [], [], {}
    for i, out in enumerate(outs):
        if out[0] == "far":
            fars[i] = (len(extra), out[3])
            extra += [pltpu.VMEM(out[1], out[2]), pltpu.SemaphoreType.DMA((out[3],))]
        plain = out[0] not in ("far", "any")
        out_specs.append(pl.BlockSpec(memory_space=pltpu.VMEM if plain else pltpu.HBM))
        shapes.append(jax.ShapeDtypeStruct(*(out if plain else out[1:3])))

    def kernel(*refs):
        ins, rest = list(refs[: len(args)]), refs[len(args) :]
        results, rest = list(rest[: len(outs)]), rest[len(outs) :]
        own, rest = rest[: len(extra)], rest[len(extra) :]
        for i, (at, count, cols) in lates.items():
            ins[i] = Late(ins[i], own[at], own[at + 1], count, cols)
        for i, (at, count) in fars.items():
            results[i] = Far(results[i], own[at], own[at + 1], count)
        body(*ins, *results, *rest)
        for i in lates:
            ins[i].ref
        for i in fars:
            results[i].finish()

    return pl.pallas_call(
        kernel,
        out_shape=shapes,
        in_specs=in_specs,
        out_specs=out_specs,
        scratch_shapes=[*extra, *(s if not isinstance(s, tuple) else pltpu.VMEM(*s) for s in scratch)],
        compiler_params=pltpu.CompilerParams(vmem_limit_bytes=limit * MIB),
        cost_estimate=pl.CostEstimate(flops=flops, bytes_accessed=1 << 12, transcendentals=0),
    )(*values)


def nn(left, right):
    return lax.dot_general(left, right, (((1,), (0,)), ((), ())), preferred_element_type=f32)


def nt(left, right):
    return lax.dot_general(left, right, (((1,), (1,)), ((), ())), preferred_element_type=f32)


def chunks(count, size, step):
    for i in range(count):
        step(slice(i * size, i * size + size))


def narrow(total):
    return [slice(start, start + 256) for start in range(0, total, 256)]


def place_blocks(table_ref, pieces, group, groups, full_ref, sem):
    blocks = [(piece, row) for piece in pieces for row in range(0, piece.shape[0], 4 * BLOCK * groups)]
    for i, (piece, first) in enumerate(blocks):
        for j in range(4):
            row = first + (group * 4 + j) * BLOCK
            there = pl.ds(pl.multiple_of(table_ref[4 * i + j] * BLOCK, BLOCK), BLOCK)
            pltpu.make_async_copy(piece.at[pl.ds(row, BLOCK)], full_ref.at[there], sem).start()


DIRECT = tuple((i // 2, i % 2 * 256) for i in range(8))
RING = ((0, 0), (0, 256), (3, 0), (1, 256), (1, 0), (2, 0), (2, 256), (4, 0))
RING_ROWS = (512, 512, 512, 256, 256)


def split_blocks(table_ref, grad_ref, pieces, cols, layout=DIRECT):
    for block in range(64):
        piece, row = layout[block // 8]
        row += (block % 8) * BLOCK
        there = pl.multiple_of(table_ref[block] * BLOCK, BLOCK)
        pieces[piece].ref[row : row + BLOCK, cols] = grad_ref[pl.ds(there, BLOCK), :]


def weight_grad(left_ref, right_ref, grad_ref):
    half = right_ref.shape[1] // 2
    for xh in range(2):
        for cols in narrow(half):
            from_cols = slice(xh * half + cols.start, xh * half + cols.stop)
            grad_ref[xh * 1024 : xh * 1024 + 1024, cols] = nn(left_ref[...], right_ref[:, from_cols]).astype(bf16)


def row_mean(value):
    return jnp.mean(value, axis=-1, keepdims=True)


def norm_stats(residual):
    center = residual - row_mean(residual)
    inverse = lax.rsqrt(row_mean(center * center) + epsilon)
    return center * inverse, inverse


def norm_back(grad, normed, inverse, gain):
    scaled = grad * gain
    return inverse * (scaled - row_mean(scaled) - normed * row_mean(scaled * normed))


def both(own_ref, other_ref, rows):
    return own_ref[rows, :].astype(f32) + other_ref[rows, :].astype(f32)


def round_weights(qkv_weight, out_weight, up_weight, down_weight):
    def kernel(qkv, out, up, down, low_ref):
        for j in range(3):
            low_ref[0:32, j * 256 : j * 256 + 256] = qkv.ref[j].astype(bf16)
        low_ref[0:32, 768:] = out.ref[...].astype(bf16)
        low_ref[32:64, :] = up.ref[...].astype(bf16)
        low_ref[64:96, :] = down.ref[...].astype(bf16)

    weights = (qkv_weight.transpose(1, 0, 2), out_weight, up_weight, down_weight)
    return call(kernel, [((96, 1024), bf16)], [late(weight) for weight in weights])[0]


def part_groups(pieces):
    def kernel(*refs):
        for i in range(4):
            rows = slice(i * BLOCK, i * BLOCK + BLOCK)
            refs[4][rows, :] = refs[i][0:BLOCK, :]
            refs[5][rows, :] = refs[i][BLOCK : 2 * BLOCK, :]
            refs[5][128 + rows.start : 128 + rows.stop, :] = refs[i][2 * BLOCK :, :]

    return call(kernel, [((128, 1024), bf16), ((256, 1024), bf16)], pieces)


def stack(pieces, count=1, awaited=()):
    rows = pieces[0].shape[0]
    each = 4 // count

    def kernel(*refs):
        outs = refs[-count:]
        for i in range(4):
            outs[i // each][(i % each) * rows : (i % each) * rows + rows, :] = refs[i][...]

    return call(kernel, [((each * rows, 1024), bf16)] * count, (*pieces, *(("any", value) for value in awaited)))


def collect_tokens(blocks, own, partner, across, flip):
    def kernel(blocks_ref, own_ref, partner_ref, across_ref, out, *flipped):
        parts = (own_ref[...], partner_ref[...], across_ref[0], across_ref[1])
        for i in range(4):
            out.ref[:, pl.ds(pl.multiple_of(blocks_ref[i] * 256, 256), 256)] = parts[i]
        out.push()
        if flip:
            flipped[0].ref[...] = out.ref[...].T

    outs = [far((512, 1024), bf16)] + ([far((1024, 512), bf16)] if flip else [])
    return call(kernel, outs, (blocks, own, partner, across))


def stack_vectors(vectors, up_bias):
    def kernel(*refs):
        for i in range(8):
            refs[9][i : i + 1, :] = refs[i][...]
        for i in range(4):
            refs[9][8 + i : 9 + i, :] = refs[8][:, i * 256 : i * 256 + 256]
        refs[9][12:16, :] = jnp.zeros((4, 256), f32)

    args = [vector.reshape(1, -1) for vector in (*vectors, up_bias)]
    return call(kernel, [((16, 256), f32)], args)[0]


def collect_vectors(blocks, own, partner, across):
    def kernel(blocks_ref, own_ref, partner_ref, across_ref, rows_ref, mine_ref):
        parts = (own_ref[...], partner_ref[...], across_ref[0], across_ref[1])
        for i in range(4):
            rows_ref[:, pl.ds(pl.multiple_of(blocks_ref[i] * 256, 256), 256)] = parts[i][0:8, :]
        mine_ref[blocks_ref[6]] = parts[0]
        mine_ref[1 - blocks_ref[6]] = parts[1]

    return call(kernel, [((8, 1024), f32), ((2, 16, 256), f32)], (blocks, own, partner, across))


def attention_forward(table, tokens, pieces, mine, seg_col, seg_row):
    def kernel(table_ref, x, p0, p1, p2, p3, mine_ref, sc_ref, sr_ref, weights, q, k, v, ctx, probs, part_ref, mask_ref, sem):
        place_blocks(table_ref, (p0, p1, p2, p3), 0, 1, weights.ref, sem)
        mask_ref[...] = jnp.where(sc_ref[...] == sr_ref[...], 0.0, lowest)
        x_ref = x.ref
        pltpu.make_async_copy(weights.target, weights.ref, sem).wait()
        weights.push()
        for xh in range(2):
            cols = slice(xh * 256, xh * 256 + 256)
            w = weights.ref.at[xh * 1024 : xh * 1024 + 1024]
            q.ref[:, cols] = (nn(x_ref[...], w[:, :256]) + mine_ref[xh, 0:1, :]).astype(bf16)
            k.ref[:, cols] = nn(x_ref[...], w[:, 256:512]).astype(bf16)
            v.ref[:, cols] = (nn(x_ref[...], w[:, 512:768]) + mine_ref[xh, 1:2, :]).astype(bf16)
        for result in (q, k, v):
            result.push()
        for pair in range(4):
            lanes = slice(pair * LANES, pair * LANES + LANES)
            for start in range(0, 512, 256):
                rows = slice(start, start + 256)
                query = q.ref[rows, lanes]
                low_half = lax.broadcasted_iota(jnp.int32, query.shape, 1) < HD
                parts = []
                for h in range(2):
                    one = jnp.where(low_half == (h == 0), query, jnp.zeros_like(query)) * HD**-0.5
                    scores = nt(one.astype(bf16), k.ref[:, lanes]) + mask_ref[rows, :]
                    shifted = jnp.exp(scores - jnp.max(scores, axis=-1, keepdims=True))
                    inverse = 1.0 / jnp.sum(shifted, axis=-1, keepdims=True)
                    probs_low = (shifted * inverse).astype(bf16)
                    probs.ref[2 * pair + h, rows, :] = probs_low
                    parts.append(nn(probs_low, v.ref[:, lanes]))
                ctx.ref[rows, lanes] = jnp.where(low_half, parts[0], parts[1]).astype(bf16)
            probs.push(1)
        ctx.push()
        for out in narrow(1024):
            low = slice(out.start + 1024, out.stop + 1024)
            part_ref[:, out] = (
                nt(ctx.ref[:, :256], weights.ref[out, 768:]) + nt(ctx.ref[:, 256:], weights.ref[low, 768:])
            ).astype(bf16)

    return call(
        kernel,
        [far((2048, 1024), bf16), *[far((512, 512), bf16)] * 4, far((8, 512, 512), bf16, 4), ((512, 1024), bf16)],
        (table, late(tokens), *(("any", piece) for piece in pieces), mine, seg_col, seg_row),
        scratch=[((512, 512), f32), pltpu.SemaphoreType.DMA],
        limit=44,
    )


def up_forward(table, tokens, own, other, vectors, mine, pieces):
    def kernel(table_ref, x, own_ref, other_ref, vec_ref, mine_ref, p0, p1, p2, p3, p4, p5, p6, p7, up, down, normed, inv_ref, hidden, act, slope, up_sem, down_sem):
        place_blocks(table_ref, (p0, p1, p2, p3, p4, p5, p6, p7), 0, 2, up.ref, up_sem)
        place_blocks(table_ref, (p0, p1, p2, p3, p4, p5, p6, p7), 1, 2, down.ref, down_sem)
        x_ref = x.ref

        def norm(rows):
            residual = x_ref[rows, :].astype(f32) + both(own_ref, other_ref, rows) + vec_ref[2:3, :]
            centered, inverse = norm_stats(residual)
            normed.ref[rows, :] = centered
            inv_ref[rows, :] = jnp.broadcast_to(inverse, (inverse.shape[0], LANES))
            hidden.ref[rows, :] = (centered * vec_ref[3:4, :] + vec_ref[4:5, :]).astype(bf16)

        chunks(4, 128, norm)
        normed.push()
        hidden.push()
        pltpu.make_async_copy(up.target, up.ref, up_sem).wait()
        up.push()
        for xh in range(2):
            for i, out in enumerate(narrow(1024)):
                cols = slice(xh * 1024 + out.start, xh * 1024 + out.stop)
                pre_act = nn(hidden.ref[...], up.ref[xh * 1024 : xh * 1024 + 1024, out]) + mine_ref[xh, 8 + i : 9 + i, :]
                cumulative = 0.5 * (1.0 + lax.erf(pre_act * 0.7071067811865476))
                density = jnp.exp(-0.5 * pre_act * pre_act) * 0.3989422804014327
                act.ref[:, cols] = (pre_act * cumulative).astype(bf16)
                slope.ref[:, cols] = (cumulative + pre_act * density).astype(bf16)
            if xh == 0:
                pltpu.make_async_copy(down.target, down.ref, down_sem).wait()
                down.push()

    return call(
        kernel,
        [
            far((2048, 1024), bf16),
            far((2048, 1024), bf16),
            far((512, 1024), f32),
            ((512, LANES), f32),
            far((512, 1024), bf16),
            far((512, 2048), bf16),
            far((512, 2048), bf16),
        ],
        (table, late(tokens), own, other, vectors, mine, *(("any", piece) for piece in pieces)),
        scratch=[pltpu.SemaphoreType.DMA, pltpu.SemaphoreType.DMA],
        limit=44,
    )


def down_forward(act, down):
    def kernel(act, down, part_ref):
        down_ref, act_ref = down.ref, act.ref
        for out in narrow(1024):
            low = slice(out.start + 1024, out.stop + 1024)
            part_ref[:, out] = (
                nt(act_ref[:, :1024], down_ref[out, :]) + nt(act_ref[:, 1024:], down_ref[low, :])
            ).astype(bf16)

    return call(kernel, [((512, 1024), bf16)], (late(act), late(down)), limit=12)[0]


def ffn_backward(blocks, normed_in, own, other, vectors, cot, down, slope, up):
    def kernel(blocks_ref, ni, own_ref, other_ref, vec_ref, cot_late, down, slope, up, keep_ref, away_ref, grad, low_ref, sums_ref, hidden_sums_ref, pre, part_ref, layer_ref):
        sums_ref[...] = jnp.zeros_like(sums_ref)
        hidden_sums_ref[...] = jnp.zeros_like(hidden_sums_ref)
        ni_ref, cot_ref = ni.ref, cot_late.ref

        def norm(rows):
            hidden = ni_ref[rows, :] * vec_ref[3:4, :] + vec_ref[4:5, :]
            residual = hidden + both(own_ref, other_ref, rows) + vec_ref[5:6, :]
            normed, inverse = norm_stats(residual)
            layer_ref[rows, :] = normed * vec_ref[6:7, :] + vec_ref[7:8, :]
            cot_rows = cot_ref[rows, :].astype(f32)
            grad_rows = norm_back(cot_rows, normed, inverse, vec_ref[6:7, :])
            grad.ref[rows, :] = grad_rows
            low_ref[rows, :] = grad_rows.astype(bf16)
            sums_ref[0:1, :] += jnp.sum(grad_rows, axis=0, keepdims=True)
            sums_ref[1:2, :] += jnp.sum(cot_rows * normed, axis=0, keepdims=True)
            sums_ref[2:3, :] += jnp.sum(cot_rows, axis=0, keepdims=True)

        chunks(4, 128, norm)
        grad.push()
        slope_ref = slope.ref
        for xh in range(2):
            down_ref = down.part(0)
            for out in narrow(1024):
                cols = slice(xh * 1024 + out.start, xh * 1024 + out.stop)
                act_grad = nn(low_ref[...], down_ref[xh * 1024 : xh * 1024 + 1024, out]).astype(bf16)
                pre_grad = act_grad.astype(f32) * slope_ref[:, cols].astype(f32)
                hidden_sums_ref[xh : xh + 1, out] = jnp.sum(pre_grad, axis=0, keepdims=True)
                pre.ref[:, cols] = pre_grad.astype(bf16)
        pre.push()
        up_ref = up.ref
        for out in narrow(1024):
            low = slice(out.start + 1024, out.stop + 1024)
            part_ref[:, out] = (
                nt(pre.ref[:, :1024], up_ref[out, :]) + nt(pre.ref[:, 1024:], up_ref[low, :])
            ).astype(bf16)
        keep_ref[...] = layer_ref[:, pl.ds(pl.multiple_of(blocks_ref[0] * 256, 256), 256)]
        away_ref[...] = layer_ref[:, pl.ds(pl.multiple_of(blocks_ref[1] * 256, 256), 256)].astype(bf16)

    return call(
        kernel,
        [((512, 256), f32), ((512, 256), bf16), far((512, 1024), f32), ((512, 1024), bf16), ((8, 1024), f32), ((8, 1024), f32), far((512, 2048), bf16), ((512, 1024), bf16)],
        (blocks, late(normed_in), own, other, vectors, late(cot), late(down, 2), late(slope), late(up)),
        scratch=[((512, 1024), f32)],
        limit=44,
    )


def up_backward(table, hidden_low, pre_low):
    def kernel(table_ref, hidden, pre, *rest):
        pieces, (flip_ref, full_ref) = rest[:4], rest[4:]
        flip_ref[...] = hidden.ref[...].T
        weight_grad(flip_ref, pre.ref, full_ref)
        split_blocks(table_ref, full_ref, pieces, slice(None))
        for piece in pieces:
            piece.push()

    return call(
        kernel,
        [far((512, 1024), bf16)] * 4,
        (table, late(hidden_low), late(pre_low)),
        scratch=[((1024, 512), bf16), ((2048, 1024), bf16)],
        limit=44,
    )


def out_backward(down_table, grad_ffn, own, other, normed_in, inverse, vectors, weights, context, low, act, awaited):
    def kernel(table_ref, gf, own_ref, other_ref, ni, inv_ref, vec_ref, w, ctx, ffn_low_ref, act, _, ga, cg_ref, sums_ref, out_grad, o0, o1, o2, o3, o4, low_ref, flip_ref, full_ref):
        pieces = (o0, o1, o2, o3, o4)
        sums_ref[...] = jnp.zeros_like(sums_ref)
        gf_ref, n_ref = gf.ref, ni.ref

        def norm(rows):
            hidden_grad = gf_ref[rows, :] + both(own_ref, other_ref, rows)
            normed = n_ref[rows, :]
            grad = norm_back(hidden_grad, normed, inv_ref[rows, :1], vec_ref[3:4, :])
            ga.ref[rows, :] = grad
            low_ref[rows, :] = grad.astype(bf16)
            sums_ref[0:1, :] += jnp.sum(grad, axis=0, keepdims=True)
            sums_ref[1:2, :] += jnp.sum(hidden_grad * normed, axis=0, keepdims=True)
            sums_ref[2:3, :] += jnp.sum(hidden_grad, axis=0, keepdims=True)

        chunks(4, 128, norm)
        ga.push()
        flip_ref[...] = ffn_low_ref[...].T
        weight_grad(flip_ref, act.ref, full_ref)
        split_blocks(table_ref, full_ref, pieces, slice(None), RING)
        for piece in pieces:
            piece.push()
        flip_ref[...] = low_ref[...].T
        weight_grad(flip_ref, ctx.ref, out_grad.ref)
        out_grad.push()
        w_ref = w.ref
        for xh in range(2):
            cg_ref[:, xh * 256 : xh * 256 + 256] = nn(low_ref[...], w_ref[xh * 1024 : xh * 1024 + 1024, :]).astype(bf16)

    return call(
        kernel,
        [far((512, 1024), f32), ((512, 512), bf16), ((8, 1024), f32), far((2048, 256), bf16), *[far((count, 1024), bf16) for count in RING_ROWS]],
        (down_table, late(grad_ffn), own, other, late(normed_in), inverse, vectors, late(weights, 1, slice(768, 1024)), late(context), low, late(act), ("any", awaited)),
        scratch=[((512, 1024), bf16), ((1024, 512), bf16), ((2048, 1024), bf16)],
        limit=44,
    )


def attention_backward(table, blocks, queries, keys, values, context_grad, probs, flip, weights, grad_attn, attn_sums, ffn_sums, hidden_sums, out_grad, awaited):
    def kernel(table_ref, blocks_ref, q, k, v, cg_ref, probs, flip, w, ga, as_ref, fs_ref, hs_ref, out_late, _, keep_ref, away_ref, o0, o1, o2, o3, full_ref, d_ref, part_ref, bias_ref, vec_ref):
        pieces = (o0, o1, o2, o3)
        bias_ref[...] = jnp.zeros_like(bias_ref)
        q_ref, k_ref, v_ref = q.ref, k.ref, v.ref
        for pair in range(4):
            lanes = slice(pair * LANES, pair * LANES + LANES)
            base = (pair // 2) * 768 + (pair % 2) * LANES
            p_ref = probs.part(0)
            key_flips, value_flips = [0.0, 0.0], [0.0, 0.0]
            for start in range(0, 512, 256):
                rows = slice(start, start + 256)
                grad = cg_ref[rows, lanes]
                grad_flip = grad.T
                query_flip = q_ref[rows, lanes].T
                low_half = lax.broadcasted_iota(jnp.int32, grad.shape, 1) < HD
                query_grads = []
                for h in range(2):
                    one = slice(h * HD, h * HD + HD)
                    grad_one = jnp.where(low_half == (h == 0), grad, jnp.zeros_like(grad))
                    probs_low = p_ref[2 * pair + h, rows, :]
                    attn = probs_low.astype(f32)
                    prob_grad = nt(grad_one, v_ref[:, lanes])
                    row_dot = jnp.sum(attn * prob_grad, axis=-1, keepdims=True)
                    score_low = (attn * (prob_grad - row_dot) * HD**-0.5).astype(bf16)
                    query_grads.append(nn(score_low, k_ref[:, lanes]))
                    key_flips[h] = key_flips[h] + nn(query_flip[one], score_low)
                    value_flips[h] = value_flips[h] + nn(grad_flip[one], probs_low)
                query_grad = jnp.where(low_half, query_grads[0], query_grads[1])
                bias_ref[0:1, lanes] += jnp.sum(query_grad, axis=0, keepdims=True)
                d_ref[rows, base : base + LANES] = query_grad.astype(bf16)
            key_grad = jnp.concatenate(key_flips, 0).T
            value_grad = jnp.concatenate(value_flips, 0).T
            bias_ref[1:2, lanes] = jnp.sum(value_grad, axis=0, keepdims=True)
            d_ref[:, base + 256 : base + 256 + LANES] = key_grad.astype(bf16)
            d_ref[:, base + 512 : base + 512 + LANES] = value_grad.astype(bf16)
        for xh in range(2):
            own = pl.ds(pl.multiple_of(blocks_ref[4 + xh] * 256, 256), 256)
            here = slice(xh * 256, xh * 256 + 256)
            parts = [bias_ref[0:1, here], bias_ref[1:2, here]]
            parts += [ref[i : i + 1, own] for ref in (as_ref, fs_ref) for i in range(3)]
            parts += [hs_ref[xh : xh + 1, out] for out in narrow(1024)]
            for i, part in enumerate(parts):
                vec_ref[xh * 4 + i // 3 : xh * 4 + i // 3 + 1, (i % 3) * 256 : (i % 3) * 256 + 256] = part
        vec_ref[8:16, :] = jnp.zeros((8, 768), f32)
        for piece in pieces:
            piece.ref[512:528, 0:768] = vec_ref[...].astype(bf16)
            piece.ref[512:528, 768:] = jnp.zeros((VECTOR_ROWS, 256), bf16)
        weight_grad(flip.ref, d_ref, full_ref)
        split_blocks(table_ref, full_ref, pieces, slice(0, 768))
        split_blocks(table_ref, out_late.ref, pieces, slice(768, 1024))
        for piece in pieces:
            piece.push()
        w_ref, ga_ref = w.ref, ga.ref
        for out in narrow(1024):
            low = slice(out.start + 1024, out.stop + 1024)
            part_ref[:, out] = nt(d_ref[:, :768], w_ref[out, :]) + nt(d_ref[:, 768:], w_ref[low, :])
        for i in range(2):
            own = pl.ds(pl.multiple_of(blocks_ref[i] * 256, 256), 256)
            across = pl.ds(pl.multiple_of(blocks_ref[2 + i] * 256, 256), 256)
            keep_ref[i, :, :] = part_ref[:, own] + ga_ref[:, own]
            away_ref[i, :, :] = part_ref[:, across].astype(bf16)

    return call(
        kernel,
        [((2, 512, 256), f32), ((2, 512, 256), bf16), *[far((528, 1024), bf16)] * 4],
        (table, blocks, late(queries), late(keys), late(values), context_grad, late(probs, 4), late(flip), late(weights, 1, slice(0, 768)), late(grad_attn), attn_sums, ffn_sums, hidden_sums, late(out_grad), ("any", awaited)),
        scratch=[((2048, 768), bf16), ((512, 1536), bf16), ((512, 1024), f32), ((8, 512), f32), ((16, 768), f32)],
        limit=44,
    )


def add_refs(refs, rows, cols=slice(None)):
    total = refs[0][rows, cols].astype(f32)
    for ref in refs[1:]:
        total = total + ref[rows, cols].astype(f32)
    return total


def add_split(parts, tail, fetch, awaited=()):
    rows, width = parts[0].shape
    quarter = (rows - tail) // 4

    def kernel(*refs):
        ins, outs = [ref.ref if fetch else ref for ref in refs[:4]], refs[-4:]
        for i in range(4):
            outs[i][0:quarter, :] = add_refs(ins, slice(i * quarter, i * quarter + quarter)).astype(bf16)
        if tail:
            vectors = add_refs(ins, slice(4 * quarter, rows)).astype(bf16)
            for i in range(4):
                outs[i][quarter : quarter + tail, :] = vectors

    args = [late(part) if fetch else part for part in parts] + [("any", value) for value in awaited]
    return call(kernel, [((quarter + tail, width), bf16)] * 4, args, limit=16)


def add_passing(near, back, plus, minus):
    def kernel(near, back, plus, minus, near_ref, back_ref):
        half = slice(0, 256)
        near_ref[...] = add_refs((near.ref, plus.ref), half).astype(bf16)
        back_ref[...] = add_refs((back.ref, minus.ref), half).astype(bf16)

    return call(kernel, [((256, 1024), bf16)] * 2, [late(part) for part in (near, back, plus, minus)])


def add_ring(own, plus, minus, near, back):
    def kernel(own, plus, minus, near, back, *outs):
        own_ref, plus_ref, minus_ref, near_ref, back_ref = own.ref, plus.ref, minus.ref, near.ref, back.ref
        for i in range(4):
            rows, here = slice(i * 128, i * 128 + 128), slice(i % 2 * 128, i % 2 * 128 + 128)
            behind = slice(256 + here.start, 256 + here.stop)
            total = own_ref[rows, :].astype(f32)
            if i < 2:
                total = total + near_ref[here, :].astype(f32) + minus_ref[behind, :].astype(f32)
            else:
                total = total + back_ref[here, :].astype(f32) + plus_ref[behind, :].astype(f32)
            outs[i][...] = total.astype(bf16)

    return call(kernel, [((128, 1024), bf16)] * 4, [late(part) for part in (own, plus, minus, near, back)])


def merge_groups(attn, up, down):
    def kernel(*refs):
        ready, outs = [ref.ref for ref in refs[:12]], refs[12:]
        vectors = add_refs(ready[:4], slice(128, 128 + VECTOR_ROWS)).astype(bf16)
        for i in range(4):
            rows = slice(i * BLOCK, i * BLOCK + BLOCK)
            for group in range(3):
                cols = slice(group * 1024, group * 1024 + 1024)
                outs[i][0:BLOCK, cols] = add_refs(ready[4 * group : 4 * group + 4], rows).astype(bf16)
            outs[i][BLOCK : BLOCK + VECTOR_ROWS, 0:1024] = vectors
            outs[i][BLOCK : BLOCK + VECTOR_ROWS, 1024:] = jnp.zeros((VECTOR_ROWS, 2048), bf16)

    return call(kernel, [((BLOCK + VECTOR_ROWS, 3072), bf16)] * 4, [late(part) for part in (*attn, *up, *down)])


def final_sums(blocks, parts):
    def kernel(blocks_ref, *refs):
        ins, (qkv_ref, out_ref, up_ref, down_ref, *vectors) = refs[:4], refs[4:]
        rows = slice(0, BLOCK)
        for j in range(3):
            qkv_ref[j] = add_refs(ins, rows, slice(j * 256, j * 256 + 256))
        out_ref[...] = add_refs(ins, rows, slice(768, 1024))
        up_ref[...] = add_refs(ins, rows, slice(1024, 2048))
        down_ref[...] = add_refs(ins, rows, slice(2048, 3072))
        sums = add_refs(ins, slice(BLOCK, BLOCK + VECTOR_ROWS), slice(0, 768))
        sums = jnp.where(blocks_ref[6] == 0, sums[0:4], sums[4:8])
        for i in range(12):
            value = sums[i // 3 : i // 3 + 1, (i % 3) * 256 : (i % 3) * 256 + 256]
            if i < 8:
                vectors[i][...] = value
            else:
                vectors[8][:, (i - 8) * 256 : (i - 8) * 256 + 256] = value

    wide = ((BLOCK, 1024), f32)
    outs = [((3, BLOCK, 256), f32), ((BLOCK, 256), f32), wide, wide, *[((1, 256), f32)] * 8, ((1, 1024), f32)]
    return call(kernel, outs, (blocks, *parts))


def body(
    tokens,
    seg_ids,
    qkv_weight,
    q_bias,
    v_bias,
    out_weight,
    out_bias,
    gain_attn,
    shift_attn,
    up_weight,
    up_bias,
    down_weight,
    down_bias,
    gain_ffn,
    shift_ffn,
    out_grad,
):
    length = seg_ids.shape[1]
    cols = tokens.shape[1]
    xh = lax.axis_index("xh")
    core = lax.axis_index("core")
    place = {
        "x": xh * 2 + lax.axis_index("xl"),
        "y": lax.axis_index("y"),
        "z": lax.axis_index("z"),
        "core": core,
    }
    table = block_table(STAGES, place)
    down_table = block_table(DOWN_STAGES, place)
    blocks = jnp.stack(
        [xh * 2 + core, 2 - xh * 2 + core, xh * 2 + 1 - core, 3 - xh * 2 - core, core, 2 + core, xh]
    ).astype(jnp.int32)

    def halves(local):
        pair = local.reshape(2, length, cols)
        own = lax.dynamic_index_in_dim(pair, xh, 0, keepdims=False)
        away = lax.dynamic_index_in_dim(pair, 1 - xh, 0, keepdims=False)
        return own, away

    def two_sequences(own, partner):
        partner = partner.astype(f32)
        return jnp.where(xh == 0, jnp.stack([own, partner]), jnp.stack([partner, own])).reshape(2 * length, cols)

    own_tokens, away_tokens = halves(tokens)
    token_partner = swap_xh(away_tokens)
    vectors = stack_vectors(
        (q_bias, v_bias, out_bias, gain_attn, shift_attn, down_bias, gain_ffn, shift_ffn), up_bias
    )
    vector_partner = swap_xh(vectors)
    first = gather_direct(round_weights(qkv_weight, out_weight, up_weight, down_weight), STAGES[0])
    first = lax.optimization_barrier((*first, token_partner))
    token_partner = first[4]
    attn_level, ffn_level = part_groups(first[:4])
    attn_second = gather_direct(attn_level, STAGES[1])
    token_across = swap_core(jnp.stack([own_tokens, token_partner]))
    vector_across = swap_core(jnp.stack([vectors, vector_partner]))
    attn_second = lax.optimization_barrier((*attn_second, token_across, vector_across))
    token_across, vector_across = attn_second[4:]
    attn_pieces = gather_direct(*stack(attn_second[:4]), STAGES[2])
    token_rows, token_flip = collect_tokens(blocks, own_tokens, token_partner, token_across, True)
    rows, mine = collect_vectors(blocks, vectors, vector_partner, vector_across)
    ffn_second = gather_direct(after(ffn_level, *attn_second[1:4]), STAGES[1])
    ffn_pieces = gather_halves(*stack(ffn_second, 2, attn_pieces[1:]), STAGES[2])
    segment = lax.dynamic_index_in_dim(seg_ids, xh, 0, keepdims=False)

    attn_full, queries, keys, values, context, probs, attn_part = attention_forward(
        table, token_rows, attn_pieces, mine, segment[:, None], segment[None, :]
    )
    up_full, down_full, normed_attn, inverse_attn, hidden_low, activated, slope = up_forward(
        table, token_rows, attn_part, swap_core(attn_part), rows, mine, ffn_pieces
    )
    own_cot, away_cot = halves(out_grad.astype(bf16))
    cot_partner = swap_xh(after(away_cot, *ffn_pieces[2:]))
    ffn_part = down_forward(after(activated, cot_partner), down_full)
    cot_rows = collect_tokens(blocks, own_cot, cot_partner, swap_core(jnp.stack([own_cot, cot_partner])), False)[0]
    layer_own, layer_away, grad_resid_ffn, ffn_grad_low, ffn_sums, hidden_sums, pre_grad_low, hidden_part = ffn_backward(
        blocks, normed_attn, ffn_part, swap_core(ffn_part), rows, cot_rows, down_full, slope, up_full
    )
    layer_partner = swap_xh(layer_away)
    up_own, up_near, up_far, up_back = up_backward(table, hidden_low, pre_grad_low)
    up_near = send(after(up_near, layer_partner), STAGES[2], 1)
    up_back = send(up_back, STAGES[2], -1)
    grad_resid_attn, context_grad, attn_sums, out_weight_grad, *down_ring = out_backward(
        down_table, grad_resid_ffn, hidden_part, swap_core(hidden_part), normed_attn, inverse_attn,
        rows, attn_full, context, ffn_grad_low, activated, up_own,
    )
    up_parts = up_own, up_near, send(after(up_far, attn_sums), STAGES[2], 2), up_back
    down_own, down_plus, down_minus, down_near, down_back = down_ring
    down_plus, down_minus = send(down_plus, DOWN_STAGES[2], 1), send(down_minus, DOWN_STAGES[2], -1)
    input_own, input_away, *attn_parts = attention_backward(
        table, blocks, queries, keys, values, context_grad, probs, token_flip, attn_full,
        grad_resid_attn, attn_sums, ffn_sums, hidden_sums, out_weight_grad, up_parts[1],
    )
    attn_parts = lax.optimization_barrier((*attn_parts, *up_parts[1:], down_plus))[:4]
    attn_parts = scatter_direct(attn_parts, STAGES[2])
    up_parts = scatter_direct(add_split(up_parts, 0, True), STAGES[1])
    down_near, down_back = add_passing(down_near, down_back, down_plus, down_minus)
    down_near, down_back = send(down_near, DOWN_STAGES[2], 1), send(down_back, DOWN_STAGES[2], -1)
    down_parts = add_ring(down_own, down_plus, down_minus, down_near, down_back)
    down_parts = scatter_direct(down_parts, DOWN_STAGES[1])
    attn_parts = add_split(attn_parts, VECTOR_ROWS, False)
    input_own = input_own + swap_core(after(input_away, attn_parts[0])).astype(f32)
    attn_parts = scatter_direct(lax.optimization_barrier((*attn_parts, *up_parts[1:], *down_parts[1:]))[:4], STAGES[1])
    input_away = after(input_own[1].astype(bf16), attn_parts[1])
    input_grad = two_sequences(input_own[0], swap_xh(input_away))
    layer_out = two_sequences(layer_own, layer_partner)
    last = scatter_direct(merge_groups(attn_parts, up_parts, down_parts), STAGES[0])
    qkv_grad, out_grad_rows, up_rows, down_rows, *sums = final_sums(blocks, last)
    (
        q_bias_grad,
        v_bias_grad,
        out_bias_grad,
        gain_attn_grad,
        shift_attn_grad,
        down_bias_grad,
        gain_ffn_grad,
        shift_ffn_grad,
        up_bias_grad,
    ) = (value.reshape(-1) for value in sums)
    return (
        layer_out,
        input_grad,
        qkv_grad.transpose(1, 0, 2),
        q_bias_grad,
        v_bias_grad,
        out_grad_rows,
        out_bias_grad,
        gain_attn_grad,
        shift_attn_grad,
        up_rows,
        up_bias_grad,
        down_rows,
        down_bias_grad,
        gain_ffn_grad,
        shift_ffn_grad,
    )


def solution(mesh):
    placed_mesh = Mesh(mesh.devices.reshape(4, 4, 2, 2, 2), AXES)
    placed = (
        P(ROW, COL),
        P(ROW, None),
        P(ROW, None, COL),
        P(COL),
        P(COL),
        P(ROW, COL),
        P(COL),
        P(COL),
        P(COL),
        P(ROW, COL),
        P(COL),
        P(ROW, COL),
        P(COL),
        P(COL),
        P(COL),
        P(ROW, COL),
    )
    return jax.shard_map(
        body,
        mesh=placed_mesh,
        in_specs=placed,
        out_specs=(
            P(ROW, COL),
            P(ROW, COL),
            P(ROW, None, COL),
            P(COL),
            P(COL),
            P(ROW, COL),
            P(COL),
            P(COL),
            P(COL),
            P(ROW, COL),
            P(COL),
            P(ROW, COL),
            P(COL),
            P(COL),
            P(COL),
        ),
        check_vma=False,
    )
```

```python
import itertools

import jax
import jax.numpy as jnp
from jax import lax
from jax.experimental import pallas as pl
from jax.experimental.pallas import tpu as pltpu
from jax.sharding import Mesh, PartitionSpec as P

HD = 64
AXES = ("z", "y", "xl", "xh", "core")
ROW = ("z", "y", "xl")
COL = ("xh", "core")
CHIPS = ("z", "y", "xl", "xh")
lowest = -1e30
epsilon = 1e-06
bf16 = jnp.bfloat16
f32 = jnp.float32

STAGES = (("x", "z"), ("y", "y"), ("z", "x"))
DOWN_STAGES = (("x", "z"), ("z", "x"), ("y", "y"))


def device_at(x, y, z, core):
    return ((z * 4 + y) * 2 + x % 2) * 4 + (x // 2) * 2 + core


def shifts(axes, step):
    pairs = []
    for x, y, z, core in itertools.product(range(4), range(4), range(4), range(2)):
        to = {"x": x, "y": y, "z": z}
        axis = axes[core]
        to[axis] = (to[axis] + (step if core == 0 else -step)) % 4
        pairs.append((device_at(x, y, z, core), device_at(to["x"], to["y"], to["z"], core)))
    return pairs


def send(value, axes, step):
    return lax.ppermute(value, AXES, shifts(axes, step))


def swap_core(value):
    return lax.ppermute(value, "core", [(0, 1), (1, 0)])


def swap_xh(value):
    return lax.ppermute(value, "xh", [(0, 1), (1, 0)])


def gather_direct(value, axes):
    return value, send(value, axes, -1), send(value, axes, 2), send(value, axes, 1)


def gather_halves(first, second, axes):
    down = [send(first, axes, 1)]
    up = [send(second, axes, -1)]
    far = send(down[0], axes, 1), send(up[0], axes, -1)
    down.append(send(second, axes, 1))
    up.insert(0, send(first, axes, -1))
    return first, second, *up, *far, *down


def scatter_direct(pieces, axes):
    own, near, far, back = pieces
    return own, send(near, axes, 1), send(far, axes, 2), send(back, axes, -1)


def after(value, *others):
    return lax.optimization_barrier((value, *others))[0]


def quarters(value):
    quarter = value.shape[0] // 4
    return [value[i * quarter : (i + 1) * quarter] for i in range(4)]


def block_table(stages, place):
    index = jnp.arange(64, dtype=jnp.int32)
    offset = (index % 4, (index // 4) % 4, index // 16)
    tables = []
    for core in range(2):
        at = {}
        for stage in range(3):
            axis = stages[stage][core]
            at[axis] = (place[axis] + (1 - 2 * core) * offset[stage] + 4) % 4
        tables.append((((at["x"] // 2) * 4 + at["z"]) * 4 + at["y"]) * 2 + at["x"] % 2)
    return jnp.where(place["core"] == 0, tables[0], tables[1])


MIB = 1024 * 1024
BLOCK = 32
VECTOR_ROWS = 16
LANES = 128


class Late:
    def __init__(self, source, target, sems, count, cols):
        rows = target.shape[0] // count
        if cols is not None:
            source = source.at[:, cols]
        self.target, self.copies = target, []
        for i in range(count):
            part = pl.ds(i * rows, rows)
            self.copies.append(pltpu.make_async_copy(source.at[part], target.at[part], sems.at[i]))
        for copy in self.copies:
            copy.start()

    def part(self, upto):
        while len(self.copies) and upto >= 0:
            self.copies.pop(0).wait()
            upto -= 1
        return self.target

    @property
    def ref(self):
        return self.part(len(self.copies))


class Far:
    def __init__(self, target, source, sems, count):
        rows = source.shape[0] // count
        self.ref, self.target, self.started, self.waiting = source, target, [], []
        for i in range(count):
            part = pl.ds(i * rows, rows)
            self.waiting.append(pltpu.make_async_copy(source.at[part], target.at[part], sems.at[i]))

    def push(self, count=None):
        for _ in range(len(self.waiting) if count is None else count):
            copy = self.waiting.pop(0)
            copy.start()
            self.started.append(copy)

    def finish(self):
        self.push()
        for copy in self.started:
            copy.wait()


def late(value, count=1, cols=None):
    return ("late", value, count, cols)


def far(shape, dtype, count=1):
    return ("far", shape, dtype, count)


def call(body, outs, args, scratch=(), flops=1 << 20, limit=12):
    in_specs, values, extra, lates = [], [], [], {}
    for i, arg in enumerate(args):
        if not isinstance(arg, tuple):
            scalar = arg.ndim == 1 and arg.dtype == jnp.int32
            in_specs.append(pl.BlockSpec(memory_space=pltpu.SMEM if scalar else pltpu.VMEM))
            values.append(arg)
            continue
        in_specs.append(pl.BlockSpec(memory_space=pltpu.HBM))
        values.append(arg[1])
        if arg[0] == "late":
            _, value, count, cols = arg
            shape = value.shape if cols is None else (value.shape[0], cols.stop - cols.start)
            lates[i] = (len(extra), count, cols)
            extra += [pltpu.VMEM(shape, value.dtype), pltpu.SemaphoreType.DMA((count,))]
    out_specs, shapes, fars = [], [], {}
    for i, out in enumerate(outs):
        if out[0] == "far":
            fars[i] = (len(extra), out[3])
            extra += [pltpu.VMEM(out[1], out[2]), pltpu.SemaphoreType.DMA((out[3],))]
        plain = out[0] not in ("far", "any")
        out_specs.append(pl.BlockSpec(memory_space=pltpu.VMEM if plain else pltpu.HBM))
        shapes.append(jax.ShapeDtypeStruct(*(out if plain else out[1:3])))

    def kernel(*refs):
        ins, rest = list(refs[: len(args)]), refs[len(args) :]
        results, rest = list(rest[: len(outs)]), rest[len(outs) :]
        own, rest = rest[: len(extra)], rest[len(extra) :]
        for i, (at, count, cols) in lates.items():
            ins[i] = Late(ins[i], own[at], own[at + 1], count, cols)
        for i, (at, count) in fars.items():
            results[i] = Far(results[i], own[at], own[at + 1], count)
        body(*ins, *results, *rest)
        for i in lates:
            ins[i].ref
        for i in fars:
            results[i].finish()

    return pl.pallas_call(
        kernel,
        out_shape=shapes,
        in_specs=in_specs,
        out_specs=out_specs,
        scratch_shapes=[*extra, *(s if not isinstance(s, tuple) else pltpu.VMEM(*s) for s in scratch)],
        compiler_params=pltpu.CompilerParams(vmem_limit_bytes=limit * MIB),
        cost_estimate=pl.CostEstimate(flops=flops, bytes_accessed=1 << 12, transcendentals=0),
    )(*values)


def nn(left, right):
    return lax.dot_general(left, right, (((1,), (0,)), ((), ())), preferred_element_type=f32)


def nt(left, right):
    return lax.dot_general(left, right, (((1,), (1,)), ((), ())), preferred_element_type=f32)


def chunks(count, size, step):
    for i in range(count):
        step(slice(i * size, i * size + size))


def narrow(total):
    return [slice(start, start + 256) for start in range(0, total, 256)]


def place_blocks(table_ref, pieces, group, groups, full_ref, sem):
    blocks = [(piece, row) for piece in pieces for row in range(0, piece.shape[0], 4 * BLOCK * groups)]
    for i, (piece, first) in enumerate(blocks):
        for j in range(4):
            row = first + (group * 4 + j) * BLOCK
            there = pl.ds(pl.multiple_of(table_ref[4 * i + j] * BLOCK, BLOCK), BLOCK)
            pltpu.make_async_copy(piece.at[pl.ds(row, BLOCK)], full_ref.at[there], sem).start()


DIRECT = tuple((i // 2, i % 2 * 256) for i in range(8))
RING = ((0, 0), (0, 256), (3, 0), (1, 256), (1, 0), (2, 0), (2, 256), (4, 0))
RING_ROWS = (512, 512, 512, 256, 256)


def split_blocks(table_ref, grad_ref, pieces, cols, layout=DIRECT):
    for block in range(64):
        piece, row = layout[block // 8]
        row += (block % 8) * BLOCK
        there = pl.multiple_of(table_ref[block] * BLOCK, BLOCK)
        pieces[piece].ref[row : row + BLOCK, cols] = grad_ref[pl.ds(there, BLOCK), :]


def weight_grad(left_ref, right_ref, grad_ref):
    half = right_ref.shape[1] // 2
    for xh in range(2):
        for cols in narrow(half):
            from_cols = slice(xh * half + cols.start, xh * half + cols.stop)
            grad_ref[xh * 1024 : xh * 1024 + 1024, cols] = nn(left_ref[...], right_ref[:, from_cols]).astype(bf16)


def row_mean(value):
    return jnp.mean(value, axis=-1, keepdims=True)


def norm_stats(residual):
    center = residual - row_mean(residual)
    inverse = lax.rsqrt(row_mean(center * center) + epsilon)
    return center * inverse, inverse


def norm_back(grad, normed, inverse, gain):
    scaled = grad * gain
    return inverse * (scaled - row_mean(scaled) - normed * row_mean(scaled * normed))


def both(own_ref, other_ref, rows):
    return own_ref[rows, :].astype(f32) + other_ref[rows, :].astype(f32)


def round_weights(qkv_weight, out_weight, up_weight, down_weight):
    def kernel(qkv, out, up, down, low_ref):
        for j in range(3):
            low_ref[0:32, j * 256 : j * 256 + 256] = qkv.ref[j].astype(bf16)
        low_ref[0:32, 768:] = out.ref[...].astype(bf16)
        low_ref[32:64, :] = up.ref[...].astype(bf16)
        low_ref[64:96, :] = down.ref[...].astype(bf16)

    weights = (qkv_weight.transpose(1, 0, 2), out_weight, up_weight, down_weight)
    return call(kernel, [((96, 1024), bf16)], [late(weight) for weight in weights])[0]


def part_groups(pieces):
    def kernel(*refs):
        for i in range(4):
            rows = slice(i * BLOCK, i * BLOCK + BLOCK)
            refs[4][rows, :] = refs[i][0:BLOCK, :]
            refs[5][rows, :] = refs[i][BLOCK : 2 * BLOCK, :]
            refs[5][128 + rows.start : 128 + rows.stop, :] = refs[i][2 * BLOCK :, :]

    return call(kernel, [((128, 1024), bf16), ((256, 1024), bf16)], pieces)


def stack(pieces, count=1, awaited=()):
    rows = pieces[0].shape[0]
    each = 4 // count

    def kernel(*refs):
        outs = refs[-count:]
        for i in range(4):
            outs[i // each][(i % each) * rows : (i % each) * rows + rows, :] = refs[i][...]

    return call(kernel, [((each * rows, 1024), bf16)] * count, (*pieces, *(("any", value) for value in awaited)))


def collect_tokens(blocks, own, partner, across, flip):
    def kernel(blocks_ref, own_ref, partner_ref, across_ref, out, *flipped):
        parts = (own_ref[...], partner_ref[...], across_ref[0], across_ref[1])
        for i in range(4):
            out.ref[:, pl.ds(pl.multiple_of(blocks_ref[i] * 256, 256), 256)] = parts[i]
        out.push()
        if flip:
            flipped[0].ref[...] = out.ref[...].T

    outs = [far((512, 1024), bf16)] + ([far((1024, 512), bf16)] if flip else [])
    return call(kernel, outs, (blocks, own, partner, across))


def stack_vectors(vectors, up_bias):
    def kernel(*refs):
        for i in range(8):
            refs[9][i : i + 1, :] = refs[i][...]
        for i in range(4):
            refs[9][8 + i : 9 + i, :] = refs[8][:, i * 256 : i * 256 + 256]
        refs[9][12:16, :] = jnp.zeros((4, 256), f32)

    args = [vector.reshape(1, -1) for vector in (*vectors, up_bias)]
    return call(kernel, [((16, 256), f32)], args)[0]


def collect_vectors(blocks, own, partner, across):
    def kernel(blocks_ref, own_ref, partner_ref, across_ref, rows_ref, mine_ref):
        parts = (own_ref[...], partner_ref[...], across_ref[0], across_ref[1])
        for i in range(4):
            rows_ref[:, pl.ds(pl.multiple_of(blocks_ref[i] * 256, 256), 256)] = parts[i][0:8, :]
        mine_ref[blocks_ref[6]] = parts[0]
        mine_ref[1 - blocks_ref[6]] = parts[1]

    return call(kernel, [((8, 1024), f32), ((2, 16, 256), f32)], (blocks, own, partner, across))


def attention_forward(table, tokens, pieces, mine, seg_col, seg_row):
    def kernel(table_ref, x, p0, p1, p2, p3, mine_ref, sc_ref, sr_ref, weights, q, k, v, ctx, probs, part_ref, mask_ref, sem):
        place_blocks(table_ref, (p0, p1, p2, p3), 0, 1, weights.ref, sem)
        mask_ref[...] = jnp.where(sc_ref[...] == sr_ref[...], 0.0, lowest)
        x_ref = x.ref
        pltpu.make_async_copy(weights.target, weights.ref, sem).wait()
        weights.push()
        for xh in range(2):
            cols = slice(xh * 256, xh * 256 + 256)
            w = weights.ref.at[xh * 1024 : xh * 1024 + 1024]
            q.ref[:, cols] = (nn(x_ref[...], w[:, :256]) + mine_ref[xh, 0:1, :]).astype(bf16)
            k.ref[:, cols] = nn(x_ref[...], w[:, 256:512]).astype(bf16)
            v.ref[:, cols] = (nn(x_ref[...], w[:, 512:768]) + mine_ref[xh, 1:2, :]).astype(bf16)
        for result in (q, k, v):
            result.push()
        for pair in range(4):
            lanes = slice(pair * LANES, pair * LANES + LANES)
            for start in range(0, 512, 256):
                rows = slice(start, start + 256)
                query = q.ref[rows, lanes]
                low_half = lax.broadcasted_iota(jnp.int32, query.shape, 1) < HD
                parts = []
                for h in range(2):
                    one = jnp.where(low_half == (h == 0), query, jnp.zeros_like(query)) * HD**-0.5
                    scores = nt(one.astype(bf16), k.ref[:, lanes]) + mask_ref[rows, :]
                    shifted = jnp.exp(scores - jnp.max(scores, axis=-1, keepdims=True))
                    inverse = 1.0 / jnp.sum(shifted, axis=-1, keepdims=True)
                    probs_low = (shifted * inverse).astype(bf16)
                    probs.ref[2 * pair + h, rows, :] = probs_low
                    parts.append(nn(probs_low, v.ref[:, lanes]))
                ctx.ref[rows, lanes] = jnp.where(low_half, parts[0], parts[1]).astype(bf16)
            probs.push(1)
        ctx.push()
        for out in narrow(1024):
            low = slice(out.start + 1024, out.stop + 1024)
            part_ref[:, out] = (
                nt(ctx.ref[:, :256], weights.ref[out, 768:]) + nt(ctx.ref[:, 256:], weights.ref[low, 768:])
            ).astype(bf16)

    return call(
        kernel,
        [far((2048, 1024), bf16), *[far((512, 512), bf16)] * 4, far((8, 512, 512), bf16, 4), ((512, 1024), bf16)],
        (table, late(tokens), *(("any", piece) for piece in pieces), mine, seg_col, seg_row),
        scratch=[((512, 512), f32), pltpu.SemaphoreType.DMA],
        limit=44,
    )


def up_forward(table, tokens, own, other, vectors, mine, pieces):
    def kernel(table_ref, x, own_ref, other_ref, vec_ref, mine_ref, p0, p1, p2, p3, p4, p5, p6, p7, up, down, normed, inv_ref, hidden, act, slope, up_sem, down_sem):
        place_blocks(table_ref, (p0, p1, p2, p3, p4, p5, p6, p7), 0, 2, up.ref, up_sem)
        place_blocks(table_ref, (p0, p1, p2, p3, p4, p5, p6, p7), 1, 2, down, down_sem)
        x_ref = x.ref

        def norm(rows):
            residual = x_ref[rows, :].astype(f32) + both(own_ref, other_ref, rows) + vec_ref[2:3, :]
            centered, inverse = norm_stats(residual)
            normed.ref[rows, :] = centered
            inv_ref[rows, :] = jnp.broadcast_to(inverse, (inverse.shape[0], LANES))
            hidden.ref[rows, :] = (centered * vec_ref[3:4, :] + vec_ref[4:5, :]).astype(bf16)

        chunks(4, 128, norm)
        normed.push()
        hidden.push()
        pltpu.make_async_copy(up.target, up.ref, up_sem).wait()
        up.push()
        for xh in range(2):
            for i, out in enumerate(narrow(1024)):
                cols = slice(xh * 1024 + out.start, xh * 1024 + out.stop)
                pre_act = nn(hidden.ref[...], up.ref[xh * 1024 : xh * 1024 + 1024, out]) + mine_ref[xh, 8 + i : 9 + i, :]
                cumulative = 0.5 * (1.0 + lax.erf(pre_act * 0.7071067811865476))
                density = jnp.exp(-0.5 * pre_act * pre_act) * 0.3989422804014327
                act[:, cols] = (pre_act * cumulative).astype(bf16)
                slope.ref[:, cols] = (cumulative + pre_act * density).astype(bf16)
            if xh == 0:
                pltpu.make_async_copy(down, down, down_sem).wait()

    return call(
        kernel,
        [
            far((2048, 1024), bf16),
            ((2048, 1024), bf16),
            far((512, 1024), f32),
            ((512, LANES), f32),
            far((512, 1024), bf16),
            ((512, 2048), bf16),
            far((512, 2048), bf16),
        ],
        (table, late(tokens), own, other, vectors, mine, *(("any", piece) for piece in pieces)),
        scratch=[pltpu.SemaphoreType.DMA, pltpu.SemaphoreType.DMA],
        limit=44,
    )


def down_forward(act, down):
    def kernel(act_ref, down_ref, part_ref):
        for out in narrow(1024):
            low = slice(out.start + 1024, out.stop + 1024)
            part_ref[:, out] = (
                nt(act_ref[:, :1024], down_ref[out, :]) + nt(act_ref[:, 1024:], down_ref[low, :])
            ).astype(bf16)

    return call(kernel, [((512, 1024), bf16)], (act, down), limit=12)[0]


def ffn_backward(blocks, normed_in, own, other, vectors, cot, down, slope, up):
    def kernel(blocks_ref, ni, own_ref, other_ref, vec_ref, cot_late, down, slope, up, keep_ref, away_ref, grad, low_ref, sums_ref, hidden_sums_ref, pre, part_ref, layer_ref):
        sums_ref[...] = jnp.zeros_like(sums_ref)
        hidden_sums_ref[...] = jnp.zeros_like(hidden_sums_ref)
        ni_ref, cot_ref = ni.ref, cot_late.ref

        def norm(rows):
            hidden = ni_ref[rows, :] * vec_ref[3:4, :] + vec_ref[4:5, :]
            residual = hidden + both(own_ref, other_ref, rows) + vec_ref[5:6, :]
            normed, inverse = norm_stats(residual)
            layer_ref[rows, :] = normed * vec_ref[6:7, :] + vec_ref[7:8, :]
            cot_rows = cot_ref[rows, :].astype(f32)
            grad_rows = norm_back(cot_rows, normed, inverse, vec_ref[6:7, :])
            grad.ref[rows, :] = grad_rows
            low_ref[rows, :] = grad_rows.astype(bf16)
            sums_ref[0:1, :] += jnp.sum(grad_rows, axis=0, keepdims=True)
            sums_ref[1:2, :] += jnp.sum(cot_rows * normed, axis=0, keepdims=True)
            sums_ref[2:3, :] += jnp.sum(cot_rows, axis=0, keepdims=True)

        chunks(4, 128, norm)
        grad.push()
        slope_ref = slope.ref
        for xh in range(2):
            down_ref = down.part(0)
            for out in narrow(1024):
                cols = slice(xh * 1024 + out.start, xh * 1024 + out.stop)
                act_grad = nn(low_ref[...], down_ref[xh * 1024 : xh * 1024 + 1024, out]).astype(bf16)
                pre_grad = act_grad.astype(f32) * slope_ref[:, cols].astype(f32)
                hidden_sums_ref[xh : xh + 1, out] = jnp.sum(pre_grad, axis=0, keepdims=True)
                pre.ref[:, cols] = pre_grad.astype(bf16)
        pre.push()
        up_ref = up.ref
        for out in narrow(1024):
            low = slice(out.start + 1024, out.stop + 1024)
            part_ref[:, out] = (
                nt(pre.ref[:, :1024], up_ref[out, :]) + nt(pre.ref[:, 1024:], up_ref[low, :])
            ).astype(bf16)
        keep_ref[...] = layer_ref[:, pl.ds(pl.multiple_of(blocks_ref[0] * 256, 256), 256)]
        away_ref[...] = layer_ref[:, pl.ds(pl.multiple_of(blocks_ref[1] * 256, 256), 256)].astype(bf16)

    return call(
        kernel,
        [((512, 256), f32), ((512, 256), bf16), far((512, 1024), f32), ((512, 1024), bf16), ((8, 1024), f32), ((8, 1024), f32), far((512, 2048), bf16), ((512, 1024), bf16)],
        (blocks, late(normed_in), own, other, vectors, late(cot), late(down, 2), late(slope), late(up)),
        scratch=[((512, 1024), f32)],
        limit=44,
    )


def up_backward(table, hidden_low, pre_low):
    def kernel(table_ref, hidden, pre, *rest):
        pieces, (flip_ref, full_ref) = rest[:4], rest[4:]
        flip_ref[...] = hidden.ref[...].T
        weight_grad(flip_ref, pre.ref, full_ref)
        split_blocks(table_ref, full_ref, pieces, slice(None))
        for piece in pieces:
            piece.push()

    return call(
        kernel,
        [far((512, 1024), bf16)] * 4,
        (table, late(hidden_low), late(pre_low)),
        scratch=[((1024, 512), bf16), ((2048, 1024), bf16)],
        limit=44,
    )


def out_backward(down_table, grad_ffn, own, other, normed_in, inverse, vectors, weights, context, low, act, awaited):
    def kernel(table_ref, gf, own_ref, other_ref, ni, inv_ref, vec_ref, w, ctx, ffn_low_ref, act, _, ga, cg_ref, sums_ref, out_grad, o0, o1, o2, o3, o4, low_ref, flip_ref, full_ref):
        pieces = (o0, o1, o2, o3, o4)
        sums_ref[...] = jnp.zeros_like(sums_ref)
        gf_ref, n_ref = gf.ref, ni.ref

        def norm(rows):
            hidden_grad = gf_ref[rows, :] + both(own_ref, other_ref, rows)
            normed = n_ref[rows, :]
            grad = norm_back(hidden_grad, normed, inv_ref[rows, :1], vec_ref[3:4, :])
            ga.ref[rows, :] = grad
            low_ref[rows, :] = grad.astype(bf16)
            sums_ref[0:1, :] += jnp.sum(grad, axis=0, keepdims=True)
            sums_ref[1:2, :] += jnp.sum(hidden_grad * normed, axis=0, keepdims=True)
            sums_ref[2:3, :] += jnp.sum(hidden_grad, axis=0, keepdims=True)

        chunks(4, 128, norm)
        ga.push()
        flip_ref[...] = ffn_low_ref[...].T
        weight_grad(flip_ref, act.ref, full_ref)
        split_blocks(table_ref, full_ref, pieces, slice(None), RING)
        for piece in pieces:
            piece.push()
        flip_ref[...] = low_ref[...].T
        weight_grad(flip_ref, ctx.ref, out_grad.ref)
        out_grad.push()
        w_ref = w.ref
        for xh in range(2):
            cg_ref[:, xh * 256 : xh * 256 + 256] = nn(low_ref[...], w_ref[xh * 1024 : xh * 1024 + 1024, :]).astype(bf16)

    return call(
        kernel,
        [far((512, 1024), f32), ((512, 512), bf16), ((8, 1024), f32), far((2048, 256), bf16), *[far((count, 1024), bf16) for count in RING_ROWS]],
        (down_table, late(grad_ffn), own, other, late(normed_in), inverse, vectors, late(weights, 1, slice(768, 1024)), late(context), low, late(act), ("any", awaited)),
        scratch=[((512, 1024), bf16), ((1024, 512), bf16), ((2048, 1024), bf16)],
        limit=44,
    )


def attention_backward(table, blocks, queries, keys, values, context_grad, probs, flip, weights, grad_attn, attn_sums, ffn_sums, hidden_sums, out_grad, awaited):
    def kernel(table_ref, blocks_ref, q, k, v, cg_ref, probs, flip, w, ga, as_ref, fs_ref, hs_ref, out_late, _, keep_ref, away_ref, o0, o1, o2, o3, full_ref, d_ref, part_ref, bias_ref, vec_ref):
        pieces = (o0, o1, o2, o3)
        bias_ref[...] = jnp.zeros_like(bias_ref)
        q_ref, k_ref, v_ref = q.ref, k.ref, v.ref
        for pair in range(4):
            lanes = slice(pair * LANES, pair * LANES + LANES)
            base = (pair // 2) * 768 + (pair % 2) * LANES
            p_ref = probs.part(0)
            key_flips, value_flips = [0.0, 0.0], [0.0, 0.0]
            for start in range(0, 512, 256):
                rows = slice(start, start + 256)
                grad = cg_ref[rows, lanes]
                grad_flip = grad.T
                query_flip = q_ref[rows, lanes].T
                low_half = lax.broadcasted_iota(jnp.int32, grad.shape, 1) < HD
                query_grads = []
                for h in range(2):
                    one = slice(h * HD, h * HD + HD)
                    grad_one = jnp.where(low_half == (h == 0), grad, jnp.zeros_like(grad))
                    probs_low = p_ref[2 * pair + h, rows, :]
                    attn = probs_low.astype(f32)
                    prob_grad = nt(grad_one, v_ref[:, lanes])
                    row_dot = jnp.sum(attn * prob_grad, axis=-1, keepdims=True)
                    score_low = (attn * (prob_grad - row_dot) * HD**-0.5).astype(bf16)
                    query_grads.append(nn(score_low, k_ref[:, lanes]))
                    key_flips[h] = key_flips[h] + nn(query_flip[one], score_low)
                    value_flips[h] = value_flips[h] + nn(grad_flip[one], probs_low)
                query_grad = jnp.where(low_half, query_grads[0], query_grads[1])
                bias_ref[0:1, lanes] += jnp.sum(query_grad, axis=0, keepdims=True)
                d_ref[rows, base : base + LANES] = query_grad.astype(bf16)
            key_grad = jnp.concatenate(key_flips, 0).T
            value_grad = jnp.concatenate(value_flips, 0).T
            bias_ref[1:2, lanes] = jnp.sum(value_grad, axis=0, keepdims=True)
            d_ref[:, base + 256 : base + 256 + LANES] = key_grad.astype(bf16)
            d_ref[:, base + 512 : base + 512 + LANES] = value_grad.astype(bf16)
        for xh in range(2):
            own = pl.ds(pl.multiple_of(blocks_ref[4 + xh] * 256, 256), 256)
            here = slice(xh * 256, xh * 256 + 256)
            parts = [bias_ref[0:1, here], bias_ref[1:2, here]]
            parts += [ref[i : i + 1, own] for ref in (as_ref, fs_ref) for i in range(3)]
            parts += [hs_ref[xh : xh + 1, out] for out in narrow(1024)]
            for i, part in enumerate(parts):
                vec_ref[xh * 4 + i // 3 : xh * 4 + i // 3 + 1, (i % 3) * 256 : (i % 3) * 256 + 256] = part
        vec_ref[8:16, :] = jnp.zeros((8, 768), f32)
        for piece in pieces:
            piece.ref[512:528, 0:768] = vec_ref[...].astype(bf16)
            piece.ref[512:528, 768:] = jnp.zeros((VECTOR_ROWS, 256), bf16)
        weight_grad(flip.ref, d_ref, full_ref)
        split_blocks(table_ref, full_ref, pieces, slice(0, 768))
        split_blocks(table_ref, out_late.ref, pieces, slice(768, 1024))
        for piece in pieces:
            piece.push()
        w_ref, ga_ref = w.ref, ga.ref
        for out in narrow(1024):
            low = slice(out.start + 1024, out.stop + 1024)
            part_ref[:, out] = nt(d_ref[:, :768], w_ref[out, :]) + nt(d_ref[:, 768:], w_ref[low, :])
        for i in range(2):
            own = pl.ds(pl.multiple_of(blocks_ref[i] * 256, 256), 256)
            across = pl.ds(pl.multiple_of(blocks_ref[2 + i] * 256, 256), 256)
            keep_ref[i, :, :] = part_ref[:, own] + ga_ref[:, own]
            away_ref[i, :, :] = part_ref[:, across].astype(bf16)

    return call(
        kernel,
        [((2, 512, 256), f32), ((2, 512, 256), bf16), *[far((528, 1024), bf16)] * 4],
        (table, blocks, late(queries), late(keys), late(values), context_grad, late(probs, 4), late(flip), late(weights, 1, slice(0, 768)), late(grad_attn), attn_sums, ffn_sums, hidden_sums, late(out_grad), ("any", awaited)),
        scratch=[((2048, 768), bf16), ((512, 1536), bf16), ((512, 1024), f32), ((8, 512), f32), ((16, 768), f32)],
        limit=44,
    )


def add_refs(refs, rows, cols=slice(None)):
    total = refs[0][rows, cols].astype(f32)
    for ref in refs[1:]:
        total = total + ref[rows, cols].astype(f32)
    return total


def add_split(parts, tail, fetch):
    rows, width = parts[0].shape
    quarter = (rows - tail) // 4

    def kernel(*refs):
        ins, outs = [ref.ref if fetch else ref for ref in refs[:4]], refs[4:]
        for i in range(4):
            outs[i][0:quarter, :] = add_refs(ins, slice(i * quarter, i * quarter + quarter)).astype(bf16)
        if tail:
            vectors = add_refs(ins, slice(4 * quarter, rows)).astype(bf16)
            for i in range(4):
                outs[i][quarter : quarter + tail, :] = vectors

    return call(kernel, [((quarter + tail, width), bf16)] * 4, [late(part) if fetch else part for part in parts], limit=16)


def add_passing(near, back, plus, minus):
    def kernel(near, back, plus, minus, near_ref, back_ref):
        half = slice(0, 256)
        near_ref[...] = add_refs((near.ref, plus.ref), half).astype(bf16)
        back_ref[...] = add_refs((back.ref, minus.ref), half).astype(bf16)

    return call(kernel, [((256, 1024), bf16)] * 2, [late(part) for part in (near, back, plus, minus)])


def add_ring(own, plus, minus, near, back):
    def kernel(own, plus, minus, near, back, *outs):
        own_ref, plus_ref, minus_ref, near_ref, back_ref = own.ref, plus.ref, minus.ref, near.ref, back.ref
        for i in range(4):
            rows, here = slice(i * 128, i * 128 + 128), slice(i % 2 * 128, i % 2 * 128 + 128)
            behind = slice(256 + here.start, 256 + here.stop)
            total = own_ref[rows, :].astype(f32)
            if i < 2:
                total = total + near_ref[here, :].astype(f32) + minus_ref[behind, :].astype(f32)
            else:
                total = total + back_ref[here, :].astype(f32) + plus_ref[behind, :].astype(f32)
            outs[i][...] = total.astype(bf16)

    return call(kernel, [((128, 1024), bf16)] * 4, [late(part) for part in (own, plus, minus, near, back)])


def merge_groups(attn, up, down):
    def kernel(*refs):
        ready, outs = [ref.ref for ref in refs[:12]], refs[12:]
        vectors = add_refs(ready[:4], slice(128, 128 + VECTOR_ROWS)).astype(bf16)
        for i in range(4):
            rows = slice(i * BLOCK, i * BLOCK + BLOCK)
            for group in range(3):
                cols = slice(group * 1024, group * 1024 + 1024)
                outs[i][0:BLOCK, cols] = add_refs(ready[4 * group : 4 * group + 4], rows).astype(bf16)
            outs[i][BLOCK : BLOCK + VECTOR_ROWS, 0:1024] = vectors
            outs[i][BLOCK : BLOCK + VECTOR_ROWS, 1024:] = jnp.zeros((VECTOR_ROWS, 2048), bf16)

    return call(kernel, [((BLOCK + VECTOR_ROWS, 3072), bf16)] * 4, [late(part) for part in (*attn, *up, *down)])


def final_sums(blocks, parts):
    def kernel(blocks_ref, *refs):
        ins, (qkv_ref, out_ref, up_ref, down_ref, *vectors) = refs[:4], refs[4:]
        rows = slice(0, BLOCK)
        for j in range(3):
            qkv_ref[j] = add_refs(ins, rows, slice(j * 256, j * 256 + 256))
        out_ref[...] = add_refs(ins, rows, slice(768, 1024))
        up_ref[...] = add_refs(ins, rows, slice(1024, 2048))
        down_ref[...] = add_refs(ins, rows, slice(2048, 3072))
        sums = add_refs(ins, slice(BLOCK, BLOCK + VECTOR_ROWS), slice(0, 768))
        sums = jnp.where(blocks_ref[6] == 0, sums[0:4], sums[4:8])
        for i in range(12):
            value = sums[i // 3 : i // 3 + 1, (i % 3) * 256 : (i % 3) * 256 + 256]
            if i < 8:
                vectors[i][...] = value
            else:
                vectors[8][:, (i - 8) * 256 : (i - 8) * 256 + 256] = value

    wide = ((BLOCK, 1024), f32)
    outs = [((3, BLOCK, 256), f32), ((BLOCK, 256), f32), wide, wide, *[((1, 256), f32)] * 8, ((1, 1024), f32)]
    return call(kernel, outs, (blocks, *parts))


def body(
    tokens,
    seg_ids,
    qkv_weight,
    q_bias,
    v_bias,
    out_weight,
    out_bias,
    gain_attn,
    shift_attn,
    up_weight,
    up_bias,
    down_weight,
    down_bias,
    gain_ffn,
    shift_ffn,
    out_grad,
):
    length = seg_ids.shape[1]
    cols = tokens.shape[1]
    xh = lax.axis_index("xh")
    core = lax.axis_index("core")
    place = {
        "x": xh * 2 + lax.axis_index("xl"),
        "y": lax.axis_index("y"),
        "z": lax.axis_index("z"),
        "core": core,
    }
    table = block_table(STAGES, place)
    down_table = block_table(DOWN_STAGES, place)
    blocks = jnp.stack(
        [xh * 2 + core, 2 - xh * 2 + core, xh * 2 + 1 - core, 3 - xh * 2 - core, core, 2 + core, xh]
    ).astype(jnp.int32)

    def halves(local):
        pair = local.reshape(2, length, cols)
        own = lax.dynamic_index_in_dim(pair, xh, 0, keepdims=False)
        away = lax.dynamic_index_in_dim(pair, 1 - xh, 0, keepdims=False)
        return own, away

    def two_sequences(own, partner):
        partner = partner.astype(f32)
        return jnp.where(xh == 0, jnp.stack([own, partner]), jnp.stack([partner, own])).reshape(2 * length, cols)

    own_tokens, away_tokens = halves(tokens)
    token_partner = swap_xh(away_tokens)
    vectors = stack_vectors(
        (q_bias, v_bias, out_bias, gain_attn, shift_attn, down_bias, gain_ffn, shift_ffn), up_bias
    )
    vector_partner = swap_xh(vectors)
    first = gather_direct(round_weights(qkv_weight, out_weight, up_weight, down_weight), STAGES[0])
    first = lax.optimization_barrier((*first, token_partner))
    token_partner = first[4]
    attn_level, ffn_level = part_groups(first[:4])
    attn_second = gather_direct(attn_level, STAGES[1])
    token_across = swap_core(jnp.stack([own_tokens, token_partner]))
    vector_across = swap_core(jnp.stack([vectors, vector_partner]))
    attn_second = lax.optimization_barrier((*attn_second, token_across, vector_across))
    token_across, vector_across = attn_second[4:]
    attn_pieces = gather_direct(*stack(attn_second[:4]), STAGES[2])
    token_rows, token_flip = collect_tokens(blocks, own_tokens, token_partner, token_across, True)
    rows, mine = collect_vectors(blocks, vectors, vector_partner, vector_across)
    ffn_second = gather_direct(after(ffn_level, *attn_second[1:4]), STAGES[1])
    ffn_pieces = gather_halves(*stack(ffn_second, 2, attn_pieces[1:]), STAGES[2])
    segment = lax.dynamic_index_in_dim(seg_ids, xh, 0, keepdims=False)

    attn_full, queries, keys, values, context, probs, attn_part = attention_forward(
        table, token_rows, attn_pieces, mine, segment[:, None], segment[None, :]
    )
    up_full, down_full, normed_attn, inverse_attn, hidden_low, activated, slope = up_forward(
        table, token_rows, attn_part, swap_core(attn_part), rows, mine, ffn_pieces
    )
    own_cot, away_cot = halves(out_grad.astype(bf16))
    cot_partner = swap_xh(after(away_cot, *ffn_pieces[2:]))
    ffn_part = down_forward(after(activated, cot_partner), down_full)
    cot_rows = collect_tokens(blocks, own_cot, cot_partner, swap_core(jnp.stack([own_cot, cot_partner])), False)[0]
    layer_own, layer_away, grad_resid_ffn, ffn_grad_low, ffn_sums, hidden_sums, pre_grad_low, hidden_part = ffn_backward(
        blocks, normed_attn, ffn_part, swap_core(ffn_part), rows, cot_rows, down_full, slope, up_full
    )
    layer_partner = swap_xh(layer_away)
    up_own, up_near, up_far, up_back = up_backward(table, hidden_low, pre_grad_low)
    up_near = send(after(up_near, layer_partner), STAGES[2], 1)
    up_far = send(up_far, STAGES[2], 2)
    grad_resid_attn, context_grad, attn_sums, out_weight_grad, *down_ring = out_backward(
        down_table, grad_resid_ffn, hidden_part, swap_core(hidden_part), normed_attn, inverse_attn,
        rows, attn_full, context, ffn_grad_low, activated, up_own,
    )
    up_parts = up_own, up_near, up_far, send(after(up_back, attn_sums), STAGES[2], -1)
    down_own, down_plus, down_minus, down_near, down_back = down_ring
    down_plus, down_minus = send(down_plus, DOWN_STAGES[2], 1), send(down_minus, DOWN_STAGES[2], -1)
    input_own, input_away, *attn_parts = attention_backward(
        table, blocks, queries, keys, values, context_grad, probs, token_flip, attn_full,
        grad_resid_attn, attn_sums, ffn_sums, hidden_sums, out_weight_grad, up_parts[0],
    )
    attn_parts = lax.optimization_barrier((*attn_parts, *up_parts[1:], down_plus))[:4]
    attn_parts = scatter_direct(attn_parts, STAGES[2])
    up_parts = scatter_direct(add_split(up_parts, 0, True), STAGES[1])
    down_near, down_back = add_passing(down_near, down_back, down_plus, down_minus)
    down_near, down_back = send(down_near, DOWN_STAGES[2], 1), send(down_back, DOWN_STAGES[2], -1)
    down_parts = add_ring(down_own, down_plus, down_minus, down_near, down_back)
    down_parts = scatter_direct(down_parts, DOWN_STAGES[1])
    attn_parts = add_split(attn_parts, VECTOR_ROWS, False)
    input_own = input_own + swap_core(after(input_away, attn_parts[0])).astype(f32)
    attn_parts = scatter_direct(lax.optimization_barrier((*attn_parts, *up_parts[1:], *down_parts[1:]))[:4], STAGES[1])
    input_away = after(input_own[1].astype(bf16), attn_parts[1])
    input_grad = two_sequences(input_own[0], swap_xh(input_away))
    layer_out = two_sequences(layer_own, layer_partner)
    last = scatter_direct(merge_groups(attn_parts, up_parts, down_parts), STAGES[0])
    qkv_grad, out_grad_rows, up_rows, down_rows, *sums = final_sums(blocks, last)
    (
        q_bias_grad,
        v_bias_grad,
        out_bias_grad,
        gain_attn_grad,
        shift_attn_grad,
        down_bias_grad,
        gain_ffn_grad,
        shift_ffn_grad,
        up_bias_grad,
    ) = (value.reshape(-1) for value in sums)
    return (
        layer_out,
        input_grad,
        qkv_grad.transpose(1, 0, 2),
        q_bias_grad,
        v_bias_grad,
        out_grad_rows,
        out_bias_grad,
        gain_attn_grad,
        shift_attn_grad,
        up_rows,
        up_bias_grad,
        down_rows,
        down_bias_grad,
        gain_ffn_grad,
        shift_ffn_grad,
    )


def solution(mesh):
    placed_mesh = Mesh(mesh.devices.reshape(4, 4, 2, 2, 2), AXES)
    placed = (
        P(ROW, COL),
        P(ROW, None),
        P(ROW, None, COL),
        P(COL),
        P(COL),
        P(ROW, COL),
        P(COL),
        P(COL),
        P(COL),
        P(ROW, COL),
        P(COL),
        P(ROW, COL),
        P(COL),
        P(COL),
        P(COL),
        P(ROW, COL),
    )
    return jax.shard_map(
        body,
        mesh=placed_mesh,
        in_specs=placed,
        out_specs=(
            P(ROW, COL),
            P(ROW, COL),
            P(ROW, None, COL),
            P(COL),
            P(COL),
            P(ROW, COL),
            P(COL),
            P(COL),
            P(COL),
            P(ROW, COL),
            P(COL),
            P(ROW, COL),
            P(COL),
            P(COL),
            P(COL),
        ),
        check_vma=False,
    )
```

```python
import itertools

import jax
import jax.numpy as jnp
from jax import lax
from jax.experimental import pallas as pl
from jax.experimental.pallas import tpu as pltpu
from jax.sharding import Mesh, PartitionSpec as P

HD = 64
AXES = ("z", "y", "xl", "xh", "core")
ROW = ("z", "y", "xl")
COL = ("xh", "core")
CHIPS = ("z", "y", "xl", "xh")
lowest = -1e30
epsilon = 1e-06
bf16 = jnp.bfloat16
f32 = jnp.float32

STAGES = (("x", "z"), ("y", "y"), ("z", "x"))
DOWN_STAGES = (("x", "z"), ("z", "x"), ("y", "y"))


def device_at(x, y, z, core):
    return ((z * 4 + y) * 2 + x % 2) * 4 + (x // 2) * 2 + core


def shifts(axes, step):
    pairs = []
    for x, y, z, core in itertools.product(range(4), range(4), range(4), range(2)):
        to = {"x": x, "y": y, "z": z}
        axis = axes[core]
        to[axis] = (to[axis] + (step if core == 0 else -step)) % 4
        pairs.append((device_at(x, y, z, core), device_at(to["x"], to["y"], to["z"], core)))
    return pairs


def send(value, axes, step):
    return lax.ppermute(value, AXES, shifts(axes, step))


def swap_core(value):
    return lax.ppermute(value, "core", [(0, 1), (1, 0)])


def swap_xh(value):
    return lax.ppermute(value, "xh", [(0, 1), (1, 0)])


def gather_direct(value, axes):
    return value, send(value, axes, -1), send(value, axes, 2), send(value, axes, 1)


def gather_halves(first, second, axes):
    down = send(first, axes, 1), send(second, axes, 1)
    up = send(first, axes, -1), send(second, axes, -1)
    return first, second, up, down


def gather_beyond(up, down, axes):
    return send(down[0], axes, 1), send(up[1], axes, -1)


def scatter_direct(pieces, axes):
    own, near, far, back = pieces
    return own, send(near, axes, 1), send(far, axes, 2), send(back, axes, -1)


def after(value, *others):
    return lax.optimization_barrier((value, *others))[0]


def quarters(value):
    quarter = value.shape[0] // 4
    return [value[i * quarter : (i + 1) * quarter] for i in range(4)]


def block_table(stages, place):
    index = jnp.arange(64, dtype=jnp.int32)
    offset = (index % 4, (index // 4) % 4, index // 16)
    tables = []
    for core in range(2):
        at = {}
        for stage in range(3):
            axis = stages[stage][core]
            at[axis] = (place[axis] + (1 - 2 * core) * offset[stage] + 4) % 4
        tables.append((((at["x"] // 2) * 4 + at["z"]) * 4 + at["y"]) * 2 + at["x"] % 2)
    return jnp.where(place["core"] == 0, tables[0], tables[1])


MIB = 1024 * 1024
BLOCK = 32
VECTOR_ROWS = 16
LANES = 128


class Late:
    def __init__(self, source, target, sems, count, cols):
        rows = target.shape[0] // count
        if cols is not None:
            source = source.at[:, cols]
        self.target, self.copies = target, []
        for i in range(count):
            part = pl.ds(i * rows, rows)
            self.copies.append(pltpu.make_async_copy(source.at[part], target.at[part], sems.at[i]))
        for copy in self.copies:
            copy.start()

    def part(self, upto):
        while len(self.copies) and upto >= 0:
            self.copies.pop(0).wait()
            upto -= 1
        return self.target

    @property
    def ref(self):
        return self.part(len(self.copies))


class Far:
    def __init__(self, target, source, sems, count):
        rows = source.shape[0] // count
        self.ref, self.target, self.started, self.waiting = source, target, [], []
        for i in range(count):
            part = pl.ds(i * rows, rows)
            self.waiting.append(pltpu.make_async_copy(source.at[part], target.at[part], sems.at[i]))

    def push(self, count=None):
        for _ in range(len(self.waiting) if count is None else count):
            copy = self.waiting.pop(0)
            copy.start()
            self.started.append(copy)

    def finish(self):
        self.push()
        for copy in self.started:
            copy.wait()


def late(value, count=1, cols=None):
    return ("late", value, count, cols)


def far(shape, dtype, count=1):
    return ("far", shape, dtype, count)


def call(body, outs, args, scratch=(), flops=1 << 20, limit=12):
    in_specs, values, extra, lates = [], [], [], {}
    for i, arg in enumerate(args):
        if not isinstance(arg, tuple):
            scalar = arg.ndim == 1 and arg.dtype == jnp.int32
            in_specs.append(pl.BlockSpec(memory_space=pltpu.SMEM if scalar else pltpu.VMEM))
            values.append(arg)
            continue
        in_specs.append(pl.BlockSpec(memory_space=pltpu.HBM))
        values.append(arg[1])
        if arg[0] == "late":
            _, value, count, cols = arg
            shape = value.shape if cols is None else (value.shape[0], cols.stop - cols.start)
            lates[i] = (len(extra), count, cols)
            extra += [pltpu.VMEM(shape, value.dtype), pltpu.SemaphoreType.DMA((count,))]
    out_specs, shapes, fars = [], [], {}
    for i, out in enumerate(outs):
        if out[0] == "far":
            fars[i] = (len(extra), out[3])
            extra += [pltpu.VMEM(out[1], out[2]), pltpu.SemaphoreType.DMA((out[3],))]
        plain = out[0] not in ("far", "any")
        out_specs.append(pl.BlockSpec(memory_space=pltpu.VMEM if plain else pltpu.HBM))
        shapes.append(jax.ShapeDtypeStruct(*(out if plain else out[1:3])))

    def kernel(*refs):
        ins, rest = list(refs[: len(args)]), refs[len(args) :]
        results, rest = list(rest[: len(outs)]), rest[len(outs) :]
        own, rest = rest[: len(extra)], rest[len(extra) :]
        for i, (at, count, cols) in lates.items():
            ins[i] = Late(ins[i], own[at], own[at + 1], count, cols)
        for i, (at, count) in fars.items():
            results[i] = Far(results[i], own[at], own[at + 1], count)
        body(*ins, *results, *rest)
        for i in lates:
            ins[i].ref
        for i in fars:
            results[i].finish()

    return pl.pallas_call(
        kernel,
        out_shape=shapes,
        in_specs=in_specs,
        out_specs=out_specs,
        scratch_shapes=[*extra, *(s if not isinstance(s, tuple) else pltpu.VMEM(*s) for s in scratch)],
        compiler_params=pltpu.CompilerParams(vmem_limit_bytes=limit * MIB),
        cost_estimate=pl.CostEstimate(flops=flops, bytes_accessed=1 << 12, transcendentals=0),
    )(*values)


def nn(left, right):
    return lax.dot_general(left, right, (((1,), (0,)), ((), ())), preferred_element_type=f32)


def nt(left, right):
    return lax.dot_general(left, right, (((1,), (1,)), ((), ())), preferred_element_type=f32)


def chunks(count, size, step):
    for i in range(count):
        step(slice(i * size, i * size + size))


def narrow(total):
    return [slice(start, start + 256) for start in range(0, total, 256)]


def place_blocks(table_ref, pieces, group, groups, full_ref, sem):
    blocks = [(piece, row) for piece in pieces for row in range(0, piece.shape[0], 4 * BLOCK * groups)]
    for i, (piece, first) in enumerate(blocks):
        for j in range(4):
            row = first + (group * 4 + j) * BLOCK
            there = pl.ds(pl.multiple_of(table_ref[4 * i + j] * BLOCK, BLOCK), BLOCK)
            pltpu.make_async_copy(piece.at[pl.ds(row, BLOCK)], full_ref.at[there], sem).start()


DIRECT = tuple((i // 2, i % 2 * 256) for i in range(8))
RING = ((0, 0), (0, 256), (3, 0), (1, 256), (1, 0), (2, 0), (2, 256), (4, 0))
RING_ROWS = (512, 512, 512, 256, 256)


def split_blocks(table_ref, grad_ref, pieces, cols, layout=DIRECT):
    for block in range(64):
        piece, row = layout[block // 8]
        row += (block % 8) * BLOCK
        there = pl.multiple_of(table_ref[block] * BLOCK, BLOCK)
        pieces[piece].ref[row : row + BLOCK, cols] = grad_ref[pl.ds(there, BLOCK), :]


def weight_grad(left_ref, right_ref, grad_ref):
    half = right_ref.shape[1] // 2
    for xh in range(2):
        for cols in narrow(half):
            from_cols = slice(xh * half + cols.start, xh * half + cols.stop)
            grad_ref[xh * 1024 : xh * 1024 + 1024, cols] = nn(left_ref[...], right_ref[:, from_cols]).astype(bf16)


def row_mean(value):
    return jnp.mean(value, axis=-1, keepdims=True)


def norm_stats(residual):
    center = residual - row_mean(residual)
    inverse = lax.rsqrt(row_mean(center * center) + epsilon)
    return center * inverse, inverse


def norm_back(grad, normed, inverse, gain):
    scaled = grad * gain
    return inverse * (scaled - row_mean(scaled) - normed * row_mean(scaled * normed))


def both(own_ref, other_ref, rows):
    return own_ref[rows, :].astype(f32) + other_ref[rows, :].astype(f32)


def round_weights(qkv_weight, out_weight, up_weight, down_weight):
    def kernel(qkv, out, up, down, low_ref):
        for j in range(3):
            low_ref[0:32, j * 256 : j * 256 + 256] = qkv.ref[j].astype(bf16)
        low_ref[0:32, 768:] = out.ref[...].astype(bf16)
        low_ref[32:64, :] = up.ref[...].astype(bf16)
        low_ref[64:96, :] = down.ref[...].astype(bf16)

    weights = (qkv_weight.transpose(1, 0, 2), out_weight, up_weight, down_weight)
    return call(kernel, [((96, 1024), bf16)], [late(weight) for weight in weights])[0]


def part_groups(pieces):
    def kernel(*refs):
        for i in range(4):
            rows = slice(i * BLOCK, i * BLOCK + BLOCK)
            refs[4][rows, :] = refs[i][0:BLOCK, :]
            refs[5][rows, :] = refs[i][BLOCK : 2 * BLOCK, :]
            refs[5][128 + rows.start : 128 + rows.stop, :] = refs[i][2 * BLOCK :, :]

    return call(kernel, [((128, 1024), bf16), ((256, 1024), bf16)], pieces)


def stack(pieces, count=1, awaited=()):
    rows = pieces[0].shape[0]
    each = 4 // count

    def kernel(*refs):
        outs = refs[-count:]
        for i in range(4):
            outs[i // each][(i % each) * rows : (i % each) * rows + rows, :] = refs[i][...]

    return call(kernel, [((each * rows, 1024), bf16)] * count, (*pieces, *(("any", value) for value in awaited)))


def collect_tokens(blocks, own, partner, across, flip):
    def kernel(blocks_ref, own_ref, partner_ref, across_ref, out, *flipped):
        parts = (own_ref[...], partner_ref[...], across_ref[0], across_ref[1])
        for i in range(4):
            out.ref[:, pl.ds(pl.multiple_of(blocks_ref[i] * 256, 256), 256)] = parts[i]
        out.push()
        if flip:
            flipped[0].ref[...] = out.ref[...].T

    outs = [far((512, 1024), bf16)] + ([far((1024, 512), bf16)] if flip else [])
    return call(kernel, outs, (blocks, own, partner, across))


def stack_vectors(vectors, up_bias):
    def kernel(*refs):
        for i in range(8):
            refs[9][i : i + 1, :] = refs[i][...]
        for i in range(4):
            refs[9][8 + i : 9 + i, :] = refs[8][:, i * 256 : i * 256 + 256]
        refs[9][12:16, :] = jnp.zeros((4, 256), f32)

    args = [vector.reshape(1, -1) for vector in (*vectors, up_bias)]
    return call(kernel, [((16, 256), f32)], args)[0]


def collect_vectors(blocks, own, partner, across):
    def kernel(blocks_ref, own_ref, partner_ref, across_ref, rows_ref, mine_ref):
        parts = (own_ref[...], partner_ref[...], across_ref[0], across_ref[1])
        for i in range(4):
            rows_ref[:, pl.ds(pl.multiple_of(blocks_ref[i] * 256, 256), 256)] = parts[i][0:8, :]
        mine_ref[blocks_ref[6]] = parts[0]
        mine_ref[1 - blocks_ref[6]] = parts[1]

    return call(kernel, [((8, 1024), f32), ((2, 16, 256), f32)], (blocks, own, partner, across))


def attention_forward(table, tokens, pieces, mine, seg_col, seg_row):
    def kernel(table_ref, x, p0, p1, p2, p3, mine_ref, sc_ref, sr_ref, weights, q, k, v, ctx, probs, part_ref, mask_ref):
        for block in range(64):
            there = pl.ds(pl.multiple_of(table_ref[block] * BLOCK, BLOCK), BLOCK)
            row = block % 16 * BLOCK
            weights.ref[there, :] = (p0, p1, p2, p3)[block // 16][row : row + BLOCK, :]
        mask_ref[...] = jnp.where(sc_ref[...] == sr_ref[...], 0.0, lowest)
        x_ref = x.ref
        weights.push()
        for xh in range(2):
            cols = slice(xh * 256, xh * 256 + 256)
            w = weights.ref.at[xh * 1024 : xh * 1024 + 1024]
            q.ref[:, cols] = (nn(x_ref[...], w[:, :256]) + mine_ref[xh, 0:1, :]).astype(bf16)
            k.ref[:, cols] = nn(x_ref[...], w[:, 256:512]).astype(bf16)
            v.ref[:, cols] = (nn(x_ref[...], w[:, 512:768]) + mine_ref[xh, 1:2, :]).astype(bf16)
        for result in (q, k, v):
            result.push()
        for pair in range(4):
            lanes = slice(pair * LANES, pair * LANES + LANES)
            for start in range(0, 512, 256):
                rows = slice(start, start + 256)
                query = q.ref[rows, lanes]
                low_half = lax.broadcasted_iota(jnp.int32, query.shape, 1) < HD
                parts = []
                for h in range(2):
                    one = jnp.where(low_half == (h == 0), query, jnp.zeros_like(query)) * HD**-0.5
                    scores = nt(one.astype(bf16), k.ref[:, lanes]) + mask_ref[rows, :]
                    shifted = jnp.exp(scores - jnp.max(scores, axis=-1, keepdims=True))
                    inverse = 1.0 / jnp.sum(shifted, axis=-1, keepdims=True)
                    probs_low = (shifted * inverse).astype(bf16)
                    probs.ref[2 * pair + h, rows, :] = probs_low
                    parts.append(nn(probs_low, v.ref[:, lanes]))
                ctx.ref[rows, lanes] = jnp.where(low_half, parts[0], parts[1]).astype(bf16)
            probs.push(1)
        ctx.push()
        for out in narrow(1024):
            low = slice(out.start + 1024, out.stop + 1024)
            part_ref[:, out] = (
                nt(ctx.ref[:, :256], weights.ref[out, 768:]) + nt(ctx.ref[:, 256:], weights.ref[low, 768:])
            ).astype(bf16)

    return call(
        kernel,
        [far((2048, 1024), bf16), *[far((512, 512), bf16)] * 4, far((8, 512, 512), bf16, 4), ((512, 1024), bf16)],
        (table, late(tokens), *pieces, mine, seg_col, seg_row),
        scratch=[((512, 512), f32)],
        limit=44,
    )


def up_forward(table, tokens, own, other, vectors, mine, pieces):
    def kernel(table_ref, x, own_ref, other_ref, vec_ref, mine_ref, p0, p1, p2, p3, p4, p5, p6, p7, up, down, normed, inv_ref, hidden, act, slope, up_sem, down_sem):
        place_blocks(table_ref, (p0, p1, p2, p3, p4, p5, p6, p7), 0, 2, up.ref, up_sem)
        place_blocks(table_ref, (p0, p1, p2, p3, p4, p5, p6, p7), 1, 2, down, down_sem)
        x_ref = x.ref

        def norm(rows):
            residual = x_ref[rows, :].astype(f32) + both(own_ref, other_ref, rows) + vec_ref[2:3, :]
            centered, inverse = norm_stats(residual)
            normed.ref[rows, :] = centered
            inv_ref[rows, :] = jnp.broadcast_to(inverse, (inverse.shape[0], LANES))
            hidden.ref[rows, :] = (centered * vec_ref[3:4, :] + vec_ref[4:5, :]).astype(bf16)

        chunks(4, 128, norm)
        normed.push()
        hidden.push()
        pltpu.make_async_copy(up.target, up.ref, up_sem).wait()
        up.push()
        for xh in range(2):
            for i, out in enumerate(narrow(1024)):
                cols = slice(xh * 1024 + out.start, xh * 1024 + out.stop)
                pre_act = nn(hidden.ref[...], up.ref[xh * 1024 : xh * 1024 + 1024, out]) + mine_ref[xh, 8 + i : 9 + i, :]
                cumulative = 0.5 * (1.0 + lax.erf(pre_act * 0.7071067811865476))
                density = jnp.exp(-0.5 * pre_act * pre_act) * 0.3989422804014327
                act[:, cols] = (pre_act * cumulative).astype(bf16)
                slope.ref[:, cols] = (cumulative + pre_act * density).astype(bf16)
            if xh == 0:
                pltpu.make_async_copy(down, down, down_sem).wait()

    return call(
        kernel,
        [
            far((2048, 1024), bf16),
            ((2048, 1024), bf16),
            far((512, 1024), f32),
            ((512, LANES), f32),
            far((512, 1024), bf16),
            ((512, 2048), bf16),
            far((512, 2048), bf16),
        ],
        (table, late(tokens), own, other, vectors, mine, *(("any", piece) for piece in pieces)),
        scratch=[pltpu.SemaphoreType.DMA, pltpu.SemaphoreType.DMA],
        limit=44,
    )


def down_forward(act, down):
    def kernel(act_ref, down_ref, part_ref):
        for out in narrow(1024):
            low = slice(out.start + 1024, out.stop + 1024)
            part_ref[:, out] = (
                nt(act_ref[:, :1024], down_ref[out, :]) + nt(act_ref[:, 1024:], down_ref[low, :])
            ).astype(bf16)

    return call(kernel, [((512, 1024), bf16)], (act, down), limit=12)[0]


def ffn_backward(blocks, normed_in, own, other, vectors, cot, down, slope, up):
    def kernel(blocks_ref, ni, own_ref, other_ref, vec_ref, cot_late, down, slope, up, keep_ref, away_ref, grad, low_ref, sums_ref, hidden_sums_ref, pre, part_ref, layer_ref):
        sums_ref[...] = jnp.zeros_like(sums_ref)
        hidden_sums_ref[...] = jnp.zeros_like(hidden_sums_ref)
        ni_ref, cot_ref = ni.ref, cot_late.ref

        def norm(rows):
            hidden = ni_ref[rows, :] * vec_ref[3:4, :] + vec_ref[4:5, :]
            residual = hidden + both(own_ref, other_ref, rows) + vec_ref[5:6, :]
            normed, inverse = norm_stats(residual)
            layer_ref[rows, :] = normed * vec_ref[6:7, :] + vec_ref[7:8, :]
            cot_rows = cot_ref[rows, :].astype(f32)
            grad_rows = norm_back(cot_rows, normed, inverse, vec_ref[6:7, :])
            grad.ref[rows, :] = grad_rows
            low_ref[rows, :] = grad_rows.astype(bf16)
            sums_ref[0:1, :] += jnp.sum(grad_rows, axis=0, keepdims=True)
            sums_ref[1:2, :] += jnp.sum(cot_rows * normed, axis=0, keepdims=True)
            sums_ref[2:3, :] += jnp.sum(cot_rows, axis=0, keepdims=True)

        chunks(4, 128, norm)
        grad.push()
        slope_ref = slope.ref
        for xh in range(2):
            down_ref = down.part(0)
            for out in narrow(1024):
                cols = slice(xh * 1024 + out.start, xh * 1024 + out.stop)
                act_grad = nn(low_ref[...], down_ref[xh * 1024 : xh * 1024 + 1024, out]).astype(bf16)
                pre_grad = act_grad.astype(f32) * slope_ref[:, cols].astype(f32)
                hidden_sums_ref[xh : xh + 1, out] = jnp.sum(pre_grad, axis=0, keepdims=True)
                pre.ref[:, cols] = pre_grad.astype(bf16)
        pre.push()
        up_ref = up.ref
        for out in narrow(1024):
            low = slice(out.start + 1024, out.stop + 1024)
            part_ref[:, out] = (
                nt(pre.ref[:, :1024], up_ref[out, :]) + nt(pre.ref[:, 1024:], up_ref[low, :])
            ).astype(bf16)
        keep_ref[...] = layer_ref[:, pl.ds(pl.multiple_of(blocks_ref[0] * 256, 256), 256)]
        away_ref[...] = layer_ref[:, pl.ds(pl.multiple_of(blocks_ref[1] * 256, 256), 256)].astype(bf16)

    return call(
        kernel,
        [((512, 256), f32), ((512, 256), bf16), far((512, 1024), f32), ((512, 1024), bf16), ((8, 1024), f32), ((8, 1024), f32), far((512, 2048), bf16), ((512, 1024), bf16)],
        (blocks, late(normed_in), own, other, vectors, late(cot), late(down, 2), late(slope), late(up)),
        scratch=[((512, 1024), f32)],
        limit=44,
    )


def up_backward(table, hidden_low, pre_low):
    def kernel(table_ref, hidden, pre, *rest):
        pieces, (flip_ref, full_ref) = rest[:4], rest[4:]
        flip_ref[...] = hidden.ref[...].T
        weight_grad(flip_ref, pre.ref, full_ref)
        split_blocks(table_ref, full_ref, pieces, slice(None))
        for piece in pieces:
            piece.push()

    return call(
        kernel,
        [far((512, 1024), bf16)] * 4,
        (table, late(hidden_low), late(pre_low)),
        scratch=[((1024, 512), bf16), ((2048, 1024), bf16)],
        limit=44,
    )


def out_backward(down_table, grad_ffn, own, other, normed_in, inverse, vectors, weights, context, low, act, awaited):
    def kernel(table_ref, gf, own_ref, other_ref, ni, inv_ref, vec_ref, w, ctx, ffn_low_ref, act, _, ga, cg_ref, sums_ref, out_grad, o0, o1, o2, o3, o4, low_ref, flip_ref, full_ref):
        pieces = (o0, o1, o2, o3, o4)
        sums_ref[...] = jnp.zeros_like(sums_ref)
        gf_ref, n_ref = gf.ref, ni.ref

        def norm(rows):
            hidden_grad = gf_ref[rows, :] + both(own_ref, other_ref, rows)
            normed = n_ref[rows, :]
            grad = norm_back(hidden_grad, normed, inv_ref[rows, :1], vec_ref[3:4, :])
            ga.ref[rows, :] = grad
            low_ref[rows, :] = grad.astype(bf16)
            sums_ref[0:1, :] += jnp.sum(grad, axis=0, keepdims=True)
            sums_ref[1:2, :] += jnp.sum(hidden_grad * normed, axis=0, keepdims=True)
            sums_ref[2:3, :] += jnp.sum(hidden_grad, axis=0, keepdims=True)

        chunks(4, 128, norm)
        ga.push()
        flip_ref[...] = ffn_low_ref[...].T
        weight_grad(flip_ref, act.ref, full_ref)
        split_blocks(table_ref, full_ref, pieces, slice(None), RING)
        for piece in pieces:
            piece.push()
        flip_ref[...] = low_ref[...].T
        weight_grad(flip_ref, ctx.ref, out_grad.ref)
        out_grad.push()
        w_ref = w.ref
        for xh in range(2):
            cg_ref[:, xh * 256 : xh * 256 + 256] = nn(low_ref[...], w_ref[xh * 1024 : xh * 1024 + 1024, :]).astype(bf16)

    return call(
        kernel,
        [far((512, 1024), f32), ((512, 512), bf16), ((8, 1024), f32), far((2048, 256), bf16), *[far((count, 1024), bf16) for count in RING_ROWS]],
        (down_table, late(grad_ffn), own, other, late(normed_in), inverse, vectors, late(weights, 1, slice(768, 1024)), late(context), low, late(act), ("any", awaited)),
        scratch=[((512, 1024), bf16), ((1024, 512), bf16), ((2048, 1024), bf16)],
        limit=44,
    )


def attention_backward(table, blocks, queries, keys, values, context_grad, probs, flip, weights, grad_attn, attn_sums, ffn_sums, hidden_sums, out_grad, awaited):
    def kernel(table_ref, blocks_ref, q, k, v, cg_ref, probs, flip, w, ga, as_ref, fs_ref, hs_ref, out_late, _, keep_ref, away_ref, o0, o1, o2, o3, full_ref, d_ref, part_ref, bias_ref, vec_ref):
        pieces = (o0, o1, o2, o3)
        bias_ref[...] = jnp.zeros_like(bias_ref)
        q_ref, k_ref, v_ref = q.ref, k.ref, v.ref
        for pair in range(4):
            lanes = slice(pair * LANES, pair * LANES + LANES)
            base = (pair // 2) * 768 + (pair % 2) * LANES
            p_ref = probs.part(0)
            key_flips, value_flips = [0.0, 0.0], [0.0, 0.0]
            for start in range(0, 512, 256):
                rows = slice(start, start + 256)
                grad = cg_ref[rows, lanes]
                grad_flip = grad.T
                query_flip = q_ref[rows, lanes].T
                low_half = lax.broadcasted_iota(jnp.int32, grad.shape, 1) < HD
                query_grads = []
                for h in range(2):
                    one = slice(h * HD, h * HD + HD)
                    grad_one = jnp.where(low_half == (h == 0), grad, jnp.zeros_like(grad))
                    probs_low = p_ref[2 * pair + h, rows, :]
                    attn = probs_low.astype(f32)
                    prob_grad = nt(grad_one, v_ref[:, lanes])
                    row_dot = jnp.sum(attn * prob_grad, axis=-1, keepdims=True)
                    score_low = (attn * (prob_grad - row_dot) * HD**-0.5).astype(bf16)
                    query_grads.append(nn(score_low, k_ref[:, lanes]))
                    key_flips[h] = key_flips[h] + nn(query_flip[one], score_low)
                    value_flips[h] = value_flips[h] + nn(grad_flip[one], probs_low)
                query_grad = jnp.where(low_half, query_grads[0], query_grads[1])
                bias_ref[0:1, lanes] += jnp.sum(query_grad, axis=0, keepdims=True)
                d_ref[rows, base : base + LANES] = query_grad.astype(bf16)
            key_grad = jnp.concatenate(key_flips, 0).T
            value_grad = jnp.concatenate(value_flips, 0).T
            bias_ref[1:2, lanes] = jnp.sum(value_grad, axis=0, keepdims=True)
            d_ref[:, base + 256 : base + 256 + LANES] = key_grad.astype(bf16)
            d_ref[:, base + 512 : base + 512 + LANES] = value_grad.astype(bf16)
        for xh in range(2):
            own = pl.ds(pl.multiple_of(blocks_ref[4 + xh] * 256, 256), 256)
            here = slice(xh * 256, xh * 256 + 256)
            parts = [bias_ref[0:1, here], bias_ref[1:2, here]]
            parts += [ref[i : i + 1, own] for ref in (as_ref, fs_ref) for i in range(3)]
            parts += [hs_ref[xh : xh + 1, out] for out in narrow(1024)]
            for i, part in enumerate(parts):
                vec_ref[xh * 4 + i // 3 : xh * 4 + i // 3 + 1, (i % 3) * 256 : (i % 3) * 256 + 256] = part
        vec_ref[8:16, :] = jnp.zeros((8, 768), f32)
        for piece in pieces:
            piece.ref[512:528, 0:768] = vec_ref[...].astype(bf16)
            piece.ref[512:528, 768:] = jnp.zeros((VECTOR_ROWS, 256), bf16)
        weight_grad(flip.ref, d_ref, full_ref)
        split_blocks(table_ref, full_ref, pieces, slice(0, 768))
        split_blocks(table_ref, out_late.ref, pieces, slice(768, 1024))
        for piece in pieces:
            piece.push()
        w_ref, ga_ref = w.ref, ga.ref
        for out in narrow(1024):
            low = slice(out.start + 1024, out.stop + 1024)
            part_ref[:, out] = nt(d_ref[:, :768], w_ref[out, :]) + nt(d_ref[:, 768:], w_ref[low, :])
        for i in range(2):
            own = pl.ds(pl.multiple_of(blocks_ref[i] * 256, 256), 256)
            across = pl.ds(pl.multiple_of(blocks_ref[2 + i] * 256, 256), 256)
            keep_ref[i, :, :] = part_ref[:, own] + ga_ref[:, own]
            away_ref[i, :, :] = part_ref[:, across].astype(bf16)

    return call(
        kernel,
        [((2, 512, 256), f32), ((2, 512, 256), bf16), *[far((528, 1024), bf16)] * 4],
        (table, blocks, late(queries), late(keys), late(values), context_grad, late(probs, 4), late(flip), late(weights, 1, slice(0, 768)), late(grad_attn), attn_sums, ffn_sums, hidden_sums, late(out_grad), ("any", awaited)),
        scratch=[((2048, 768), bf16), ((512, 1536), bf16), ((512, 1024), f32), ((8, 512), f32), ((16, 768), f32)],
        limit=44,
    )


def add_refs(refs, rows, cols=slice(None)):
    total = refs[0][rows, cols].astype(f32)
    for ref in refs[1:]:
        total = total + ref[rows, cols].astype(f32)
    return total


def add_split(parts, tail, fetch):
    rows, width = parts[0].shape
    quarter = (rows - tail) // 4

    def kernel(*refs):
        ins, outs = [ref.ref if fetch else ref for ref in refs[:4]], refs[4:]
        for i in range(4):
            outs[i][0:quarter, :] = add_refs(ins, slice(i * quarter, i * quarter + quarter)).astype(bf16)
        if tail:
            vectors = add_refs(ins, slice(4 * quarter, rows)).astype(bf16)
            for i in range(4):
                outs[i][quarter : quarter + tail, :] = vectors

    return call(kernel, [((quarter + tail, width), bf16)] * 4, [late(part) if fetch else part for part in parts], limit=16)


def add_passing(near, back, plus, minus):
    def kernel(near, back, plus, minus, near_ref, back_ref):
        half = slice(0, 256)
        near_ref[...] = add_refs((near.ref, plus.ref), half).astype(bf16)
        back_ref[...] = add_refs((back.ref, minus.ref), half).astype(bf16)

    return call(kernel, [((256, 1024), bf16)] * 2, [late(part) for part in (near, back, plus, minus)])


def add_ring(own, plus, minus, near, back):
    def kernel(own, plus, minus, near, back, *outs):
        own_ref, plus_ref, minus_ref, near_ref, back_ref = own.ref, plus.ref, minus.ref, near.ref, back.ref
        for i in range(4):
            rows, here = slice(i * 128, i * 128 + 128), slice(i % 2 * 128, i % 2 * 128 + 128)
            behind = slice(256 + here.start, 256 + here.stop)
            total = own_ref[rows, :].astype(f32)
            if i < 2:
                total = total + near_ref[here, :].astype(f32) + minus_ref[behind, :].astype(f32)
            else:
                total = total + back_ref[here, :].astype(f32) + plus_ref[behind, :].astype(f32)
            outs[i][...] = total.astype(bf16)

    return call(kernel, [((128, 1024), bf16)] * 4, [late(part) for part in (own, plus, minus, near, back)])


def merge_groups(attn, up, down):
    def kernel(*refs):
        ready, outs = [ref.ref for ref in refs[:12]], refs[12:]
        vectors = add_refs(ready[:4], slice(128, 128 + VECTOR_ROWS)).astype(bf16)
        for i in range(4):
            rows = slice(i * BLOCK, i * BLOCK + BLOCK)
            for group in range(3):
                cols = slice(group * 1024, group * 1024 + 1024)
                outs[i][0:BLOCK, cols] = add_refs(ready[4 * group : 4 * group + 4], rows).astype(bf16)
            outs[i][BLOCK : BLOCK + VECTOR_ROWS, 0:1024] = vectors
            outs[i][BLOCK : BLOCK + VECTOR_ROWS, 1024:] = jnp.zeros((VECTOR_ROWS, 2048), bf16)

    return call(kernel, [((BLOCK + VECTOR_ROWS, 3072), bf16)] * 4, [late(part) for part in (*attn, *up, *down)])


def final_sums(blocks, parts):
    def kernel(blocks_ref, *refs):
        ins, (qkv_ref, out_ref, up_ref, down_ref, *vectors) = refs[:4], refs[4:]
        rows = slice(0, BLOCK)
        for j in range(3):
            qkv_ref[j] = add_refs(ins, rows, slice(j * 256, j * 256 + 256))
        out_ref[...] = add_refs(ins, rows, slice(768, 1024))
        up_ref[...] = add_refs(ins, rows, slice(1024, 2048))
        down_ref[...] = add_refs(ins, rows, slice(2048, 3072))
        sums = add_refs(ins, slice(BLOCK, BLOCK + VECTOR_ROWS), slice(0, 768))
        sums = jnp.where(blocks_ref[6] == 0, sums[0:4], sums[4:8])
        for i in range(12):
            value = sums[i // 3 : i // 3 + 1, (i % 3) * 256 : (i % 3) * 256 + 256]
            if i < 8:
                vectors[i][...] = value
            else:
                vectors[8][:, (i - 8) * 256 : (i - 8) * 256 + 256] = value

    wide = ((BLOCK, 1024), f32)
    outs = [((3, BLOCK, 256), f32), ((BLOCK, 256), f32), wide, wide, *[((1, 256), f32)] * 8, ((1, 1024), f32)]
    return call(kernel, outs, (blocks, *parts))


def body(
    tokens,
    seg_ids,
    qkv_weight,
    q_bias,
    v_bias,
    out_weight,
    out_bias,
    gain_attn,
    shift_attn,
    up_weight,
    up_bias,
    down_weight,
    down_bias,
    gain_ffn,
    shift_ffn,
    out_grad,
):
    length = seg_ids.shape[1]
    cols = tokens.shape[1]
    xh = lax.axis_index("xh")
    core = lax.axis_index("core")
    place = {
        "x": xh * 2 + lax.axis_index("xl"),
        "y": lax.axis_index("y"),
        "z": lax.axis_index("z"),
        "core": core,
    }
    table = block_table(STAGES, place)
    down_table = block_table(DOWN_STAGES, place)
    blocks = jnp.stack(
        [xh * 2 + core, 2 - xh * 2 + core, xh * 2 + 1 - core, 3 - xh * 2 - core, core, 2 + core, xh]
    ).astype(jnp.int32)

    def halves(local):
        pair = local.reshape(2, length, cols)
        own = lax.dynamic_index_in_dim(pair, xh, 0, keepdims=False)
        away = lax.dynamic_index_in_dim(pair, 1 - xh, 0, keepdims=False)
        return own, away

    def two_sequences(own, partner):
        partner = partner.astype(f32)
        return jnp.where(xh == 0, jnp.stack([own, partner]), jnp.stack([partner, own])).reshape(2 * length, cols)

    own_tokens, away_tokens = halves(tokens)
    token_partner = swap_xh(away_tokens)
    vectors = stack_vectors(
        (q_bias, v_bias, out_bias, gain_attn, shift_attn, down_bias, gain_ffn, shift_ffn), up_bias
    )
    vector_partner = swap_xh(vectors)
    first = gather_direct(round_weights(qkv_weight, out_weight, up_weight, down_weight), STAGES[0])
    first = lax.optimization_barrier((*first, token_partner))
    token_partner = first[4]
    attn_level, ffn_level = part_groups(first[:4])
    attn_second = gather_direct(attn_level, STAGES[1])
    token_across = swap_core(jnp.stack([own_tokens, token_partner]))
    vector_across = swap_core(jnp.stack([vectors, vector_partner]))
    attn_second = lax.optimization_barrier((*attn_second, token_across, vector_across))
    token_across, vector_across = attn_second[4:]
    attn_pieces = gather_direct(*stack(attn_second[:4]), STAGES[2])
    token_rows, token_flip = collect_tokens(blocks, own_tokens, token_partner, token_across, True)
    rows, mine = collect_vectors(blocks, vectors, vector_partner, vector_across)
    ffn_second = gather_direct(after(ffn_level, *attn_second[1:4]), STAGES[1])
    ffn_first, ffn_last, ffn_up, ffn_down = gather_halves(*stack(ffn_second, 2, (*attn_pieces[1:], token_flip, mine)), STAGES[2])
    segment = lax.dynamic_index_in_dim(seg_ids, xh, 0, keepdims=False)

    attn_full, queries, keys, values, context, probs, attn_part = attention_forward(
        table, token_rows, attn_pieces, mine, segment[:, None], segment[None, :]
    )
    ffn_beyond = gather_beyond(
        (ffn_up[0], after(ffn_up[1], attn_part)), (after(ffn_down[0], attn_part), ffn_down[1]), STAGES[2]
    )
    ffn_pieces = ffn_first, ffn_last, *ffn_up, *ffn_beyond, *ffn_down
    up_full, down_full, normed_attn, inverse_attn, hidden_low, activated, slope = up_forward(
        table, token_rows, attn_part, swap_core(attn_part), rows, mine, ffn_pieces
    )
    own_cot, away_cot = halves(out_grad.astype(bf16))
    cot_partner = swap_xh(after(away_cot, *ffn_pieces[2:]))
    ffn_part = down_forward(after(activated, cot_partner), down_full)
    cot_rows = collect_tokens(blocks, own_cot, cot_partner, swap_core(jnp.stack([own_cot, cot_partner])), False)[0]
    layer_own, layer_away, grad_resid_ffn, ffn_grad_low, ffn_sums, hidden_sums, pre_grad_low, hidden_part = ffn_backward(
        blocks, normed_attn, ffn_part, swap_core(ffn_part), rows, cot_rows, down_full, slope, up_full
    )
    layer_partner = swap_xh(layer_away)
    up_own, up_near, up_far, up_back = up_backward(table, hidden_low, pre_grad_low)
    up_near = send(after(up_near, layer_partner), STAGES[2], 1)
    up_far = send(up_far, STAGES[2], 2)
    grad_resid_attn, context_grad, attn_sums, out_weight_grad, *down_ring = out_backward(
        down_table, grad_resid_ffn, hidden_part, swap_core(hidden_part), normed_attn, inverse_attn,
        rows, attn_full, context, ffn_grad_low, activated, up_own,
    )
    up_parts = up_own, up_near, up_far, send(after(up_back, attn_sums), STAGES[2], -1)
    down_own, down_plus, down_minus, down_near, down_back = down_ring
    down_plus, down_minus = send(down_plus, DOWN_STAGES[2], 1), send(down_minus, DOWN_STAGES[2], -1)
    input_own, input_away, *attn_parts = attention_backward(
        table, blocks, queries, keys, values, context_grad, probs, token_flip, attn_full,
        grad_resid_attn, attn_sums, ffn_sums, hidden_sums, out_weight_grad, up_parts[0],
    )
    attn_parts = lax.optimization_barrier((*attn_parts, *up_parts[1:], down_plus))[:4]
    attn_parts = scatter_direct(attn_parts, STAGES[2])
    up_parts = scatter_direct(add_split(up_parts, 0, True), STAGES[1])
    down_near, down_back = add_passing(down_near, down_back, down_plus, down_minus)
    down_near, down_back = send(down_near, DOWN_STAGES[2], 1), send(down_back, DOWN_STAGES[2], -1)
    down_parts = add_ring(down_own, down_plus, down_minus, down_near, down_back)
    down_parts = scatter_direct(down_parts, DOWN_STAGES[1])
    attn_parts = add_split(attn_parts, VECTOR_ROWS, False)
    input_own = input_own + swap_core(after(input_away, attn_parts[0])).astype(f32)
    attn_parts = scatter_direct(lax.optimization_barrier((*attn_parts, up_parts[1], up_parts[3]))[:4], STAGES[1])
    input_away = after(input_own[1].astype(bf16), attn_parts[1])
    input_grad = two_sequences(input_own[0], swap_xh(input_away))
    layer_out = two_sequences(layer_own, layer_partner)
    last = scatter_direct(merge_groups(attn_parts, up_parts, down_parts), STAGES[0])
    qkv_grad, out_grad_rows, up_rows, down_rows, *sums = final_sums(blocks, last)
    (
        q_bias_grad,
        v_bias_grad,
        out_bias_grad,
        gain_attn_grad,
        shift_attn_grad,
        down_bias_grad,
        gain_ffn_grad,
        shift_ffn_grad,
        up_bias_grad,
    ) = (value.reshape(-1) for value in sums)
    return (
        layer_out,
        input_grad,
        qkv_grad.transpose(1, 0, 2),
        q_bias_grad,
        v_bias_grad,
        out_grad_rows,
        out_bias_grad,
        gain_attn_grad,
        shift_attn_grad,
        up_rows,
        up_bias_grad,
        down_rows,
        down_bias_grad,
        gain_ffn_grad,
        shift_ffn_grad,
    )


def solution(mesh):
    placed_mesh = Mesh(mesh.devices.reshape(4, 4, 2, 2, 2), AXES)
    placed = (
        P(ROW, COL),
        P(ROW, None),
        P(ROW, None, COL),
        P(COL),
        P(COL),
        P(ROW, COL),
        P(COL),
        P(COL),
        P(COL),
        P(ROW, COL),
        P(COL),
        P(ROW, COL),
        P(COL),
        P(COL),
        P(COL),
        P(ROW, COL),
    )
    return jax.shard_map(
        body,
        mesh=placed_mesh,
        in_specs=placed,
        out_specs=(
            P(ROW, COL),
            P(ROW, COL),
            P(ROW, None, COL),
            P(COL),
            P(COL),
            P(ROW, COL),
            P(COL),
            P(COL),
            P(COL),
            P(ROW, COL),
            P(COL),
            P(ROW, COL),
            P(COL),
            P(COL),
            P(COL),
        ),
        check_vma=False,
    )
```

```python
import itertools

import jax
import jax.numpy as jnp
from jax import lax
from jax.experimental import pallas as pl
from jax.experimental.pallas import tpu as pltpu
from jax.sharding import Mesh, PartitionSpec as P

HD = 64
AXES = ("z", "y", "xl", "xh", "core")
ROW = ("z", "y", "xl")
COL = ("xh", "core")
CHIPS = ("z", "y", "xl", "xh")
lowest = -1e30
epsilon = 1e-06
bf16 = jnp.bfloat16
f32 = jnp.float32

STAGES = (("x", "z"), ("y", "y"), ("z", "x"))
DOWN_STAGES = (("x", "z"), ("z", "x"), ("y", "y"))


def device_at(x, y, z, core):
    return ((z * 4 + y) * 2 + x % 2) * 4 + (x // 2) * 2 + core


def shifts(axes, step):
    pairs = []
    for x, y, z, core in itertools.product(range(4), range(4), range(4), range(2)):
        to = {"x": x, "y": y, "z": z}
        axis = axes[core]
        to[axis] = (to[axis] + (step if core == 0 else -step)) % 4
        pairs.append((device_at(x, y, z, core), device_at(to["x"], to["y"], to["z"], core)))
    return pairs


def send(value, axes, step):
    return lax.ppermute(value, AXES, shifts(axes, step))


def swap_core(value):
    return lax.ppermute(value, "core", [(0, 1), (1, 0)])


def swap_xh(value):
    return lax.ppermute(value, "xh", [(0, 1), (1, 0)])


def gather_direct(value, axes):
    return value, send(value, axes, -1), send(value, axes, 2), send(value, axes, 1)


def gather_halves(first, second, axes):
    down = send(first, axes, 1), send(second, axes, 1)
    up = send(first, axes, -1), send(second, axes, -1)
    return first, second, up, down


def gather_beyond(up, down, axes):
    return send(down[0], axes, 1), send(up[1], axes, -1)


def scatter_direct(pieces, axes):
    own, near, far, back = pieces
    return own, send(near, axes, 1), send(far, axes, 2), send(back, axes, -1)


def after(value, *others):
    return lax.optimization_barrier((value, *others))[0]


def quarters(value):
    quarter = value.shape[0] // 4
    return [value[i * quarter : (i + 1) * quarter] for i in range(4)]


def block_table(stages, place):
    index = jnp.arange(64, dtype=jnp.int32)
    offset = (index % 4, (index // 4) % 4, index // 16)
    tables = []
    for core in range(2):
        at = {}
        for stage in range(3):
            axis = stages[stage][core]
            at[axis] = (place[axis] + (1 - 2 * core) * offset[stage] + 4) % 4
        tables.append((((at["x"] // 2) * 4 + at["z"]) * 4 + at["y"]) * 2 + at["x"] % 2)
    return jnp.where(place["core"] == 0, tables[0], tables[1])


MIB = 1024 * 1024
BLOCK = 32
VECTOR_ROWS = 16
LANES = 128


class Late:
    def __init__(self, source, target, sems, count, cols):
        rows = target.shape[0] // count
        if cols is not None:
            source = source.at[:, cols]
        self.target, self.copies = target, []
        for i in range(count):
            part = pl.ds(i * rows, rows)
            self.copies.append(pltpu.make_async_copy(source.at[part], target.at[part], sems.at[i]))
        for copy in self.copies:
            copy.start()

    def part(self, upto):
        while len(self.copies) and upto >= 0:
            self.copies.pop(0).wait()
            upto -= 1
        return self.target

    @property
    def ref(self):
        return self.part(len(self.copies))


class Far:
    def __init__(self, target, source, sems, count):
        rows = source.shape[0] // count
        self.ref, self.target, self.started, self.waiting = source, target, [], []
        for i in range(count):
            part = pl.ds(i * rows, rows)
            self.waiting.append(pltpu.make_async_copy(source.at[part], target.at[part], sems.at[i]))

    def push(self, count=None):
        for _ in range(len(self.waiting) if count is None else count):
            copy = self.waiting.pop(0)
            copy.start()
            self.started.append(copy)

    def finish(self):
        self.push()
        for copy in self.started:
            copy.wait()


def late(value, count=1, cols=None):
    return ("late", value, count, cols)


def far(shape, dtype, count=1):
    return ("far", shape, dtype, count)


def call(body, outs, args, scratch=(), flops=1 << 20, limit=12):
    in_specs, values, extra, lates = [], [], [], {}
    for i, arg in enumerate(args):
        if not isinstance(arg, tuple):
            scalar = arg.ndim == 1 and arg.dtype == jnp.int32
            in_specs.append(pl.BlockSpec(memory_space=pltpu.SMEM if scalar else pltpu.VMEM))
            values.append(arg)
            continue
        in_specs.append(pl.BlockSpec(memory_space=pltpu.HBM))
        values.append(arg[1])
        if arg[0] == "late":
            _, value, count, cols = arg
            shape = value.shape if cols is None else (value.shape[0], cols.stop - cols.start)
            lates[i] = (len(extra), count, cols)
            extra += [pltpu.VMEM(shape, value.dtype), pltpu.SemaphoreType.DMA((count,))]
    out_specs, shapes, fars = [], [], {}
    for i, out in enumerate(outs):
        if out[0] == "far":
            fars[i] = (len(extra), out[3])
            extra += [pltpu.VMEM(out[1], out[2]), pltpu.SemaphoreType.DMA((out[3],))]
        plain = out[0] not in ("far", "any")
        out_specs.append(pl.BlockSpec(memory_space=pltpu.VMEM if plain else pltpu.HBM))
        shapes.append(jax.ShapeDtypeStruct(*(out if plain else out[1:3])))

    def kernel(*refs):
        ins, rest = list(refs[: len(args)]), refs[len(args) :]
        results, rest = list(rest[: len(outs)]), rest[len(outs) :]
        own, rest = rest[: len(extra)], rest[len(extra) :]
        for i, (at, count, cols) in lates.items():
            ins[i] = Late(ins[i], own[at], own[at + 1], count, cols)
        for i, (at, count) in fars.items():
            results[i] = Far(results[i], own[at], own[at + 1], count)
        body(*ins, *results, *rest)
        for i in lates:
            ins[i].ref
        for i in fars:
            results[i].finish()

    return pl.pallas_call(
        kernel,
        out_shape=shapes,
        in_specs=in_specs,
        out_specs=out_specs,
        scratch_shapes=[*extra, *(s if not isinstance(s, tuple) else pltpu.VMEM(*s) for s in scratch)],
        compiler_params=pltpu.CompilerParams(vmem_limit_bytes=limit * MIB),
        cost_estimate=pl.CostEstimate(flops=flops, bytes_accessed=1 << 12, transcendentals=0),
    )(*values)


def nn(left, right):
    return lax.dot_general(left, right, (((1,), (0,)), ((), ())), preferred_element_type=f32)


def nt(left, right):
    return lax.dot_general(left, right, (((1,), (1,)), ((), ())), preferred_element_type=f32)


def chunks(count, size, step):
    for i in range(count):
        step(slice(i * size, i * size + size))


def narrow(total):
    return [slice(start, start + 256) for start in range(0, total, 256)]


def place_blocks(table_ref, pieces, group, groups, full_ref, sem):
    blocks = [(piece, row) for piece in pieces for row in range(0, piece.shape[0], 4 * BLOCK * groups)]
    for i, (piece, first) in enumerate(blocks):
        for j in range(4):
            row = first + (group * 4 + j) * BLOCK
            there = pl.ds(pl.multiple_of(table_ref[4 * i + j] * BLOCK, BLOCK), BLOCK)
            pltpu.make_async_copy(piece.at[pl.ds(row, BLOCK)], full_ref.at[there], sem).start()


DIRECT = tuple((i // 2, i % 2 * 256) for i in range(8))
RING = ((0, 0), (0, 256), (3, 0), (1, 256), (1, 0), (2, 0), (2, 256), (4, 0))
RING_ROWS = (512, 512, 512, 256, 256)


def split_blocks(table_ref, grad_ref, pieces, cols, layout=DIRECT):
    for block in range(64):
        piece, row = layout[block // 8]
        row += (block % 8) * BLOCK
        there = pl.multiple_of(table_ref[block] * BLOCK, BLOCK)
        pieces[piece].ref[row : row + BLOCK, cols] = grad_ref[pl.ds(there, BLOCK), :]


def weight_grad(left_ref, right_ref, grad_ref):
    half = right_ref.shape[1] // 2
    for xh in range(2):
        for cols in narrow(half):
            from_cols = slice(xh * half + cols.start, xh * half + cols.stop)
            grad_ref[xh * 1024 : xh * 1024 + 1024, cols] = nn(left_ref[...], right_ref[:, from_cols]).astype(bf16)


def row_mean(value):
    return jnp.mean(value, axis=-1, keepdims=True)


def norm_stats(residual):
    center = residual - row_mean(residual)
    inverse = lax.rsqrt(row_mean(center * center) + epsilon)
    return center * inverse, inverse


def norm_back(grad, normed, inverse, gain):
    scaled = grad * gain
    return inverse * (scaled - row_mean(scaled) - normed * row_mean(scaled * normed))


def both(own_ref, other_ref, rows):
    return own_ref[rows, :].astype(f32) + other_ref[rows, :].astype(f32)


def round_weights(qkv_weight, out_weight, up_weight, down_weight):
    def kernel(qkv, out, up, down, low_ref):
        for j in range(3):
            low_ref[0:32, j * 256 : j * 256 + 256] = qkv.ref[j].astype(bf16)
        low_ref[0:32, 768:] = out.ref[...].astype(bf16)
        low_ref[32:64, :] = up.ref[...].astype(bf16)
        low_ref[64:96, :] = down.ref[...].astype(bf16)

    weights = (qkv_weight.transpose(1, 0, 2), out_weight, up_weight, down_weight)
    return call(kernel, [((96, 1024), bf16)], [late(weight) for weight in weights])[0]


def part_groups(pieces):
    def kernel(*refs):
        for i in range(4):
            rows = slice(i * BLOCK, i * BLOCK + BLOCK)
            refs[4][rows, :] = refs[i][0:BLOCK, :]
            refs[5][rows, :] = refs[i][BLOCK : 2 * BLOCK, :]
            refs[5][128 + rows.start : 128 + rows.stop, :] = refs[i][2 * BLOCK :, :]

    return call(kernel, [((128, 1024), bf16), ((256, 1024), bf16)], pieces)


def stack(pieces, count=1, awaited=()):
    rows = pieces[0].shape[0]
    each = 4 // count

    def kernel(*refs):
        outs = refs[-count:]
        for i in range(4):
            outs[i // each][(i % each) * rows : (i % each) * rows + rows, :] = refs[i][...]

    return call(kernel, [((each * rows, 1024), bf16)] * count, (*pieces, *(("any", value) for value in awaited)))


def collect_tokens(blocks, own, partner, across, flip):
    def kernel(blocks_ref, own_ref, partner_ref, across_ref, out, *flipped):
        parts = (own_ref[...], partner_ref[...], across_ref[0], across_ref[1])
        for i in range(4):
            out.ref[:, pl.ds(pl.multiple_of(blocks_ref[i] * 256, 256), 256)] = parts[i]
        out.push()
        if flip:
            flipped[0].ref[...] = out.ref[...].T

    outs = [far((512, 1024), bf16)] + ([far((1024, 512), bf16)] if flip else [])
    return call(kernel, outs, (blocks, own, partner, across))


def stack_vectors(vectors, up_bias):
    def kernel(*refs):
        for i in range(8):
            refs[9][i : i + 1, :] = refs[i][...]
        for i in range(4):
            refs[9][8 + i : 9 + i, :] = refs[8][:, i * 256 : i * 256 + 256]
        refs[9][12:16, :] = jnp.zeros((4, 256), f32)

    args = [vector.reshape(1, -1) for vector in (*vectors, up_bias)]
    return call(kernel, [((16, 256), f32)], args)[0]


def collect_vectors(blocks, own, partner, across):
    def kernel(blocks_ref, own_ref, partner_ref, across_ref, rows_ref, mine_ref):
        parts = (own_ref[...], partner_ref[...], across_ref[0], across_ref[1])
        for i in range(4):
            rows_ref[:, pl.ds(pl.multiple_of(blocks_ref[i] * 256, 256), 256)] = parts[i][0:8, :]
        mine_ref[blocks_ref[6]] = parts[0]
        mine_ref[1 - blocks_ref[6]] = parts[1]

    return call(kernel, [((8, 1024), f32), ((2, 16, 256), f32)], (blocks, own, partner, across))


def attention_forward(table, tokens, pieces, mine, seg_col, seg_row):
    def kernel(table_ref, x, p0, p1, p2, p3, mine_ref, sc_ref, sr_ref, weights, q, k, v, ctx, probs, part_ref, mask_ref):
        for block in range(64):
            there = pl.ds(pl.multiple_of(table_ref[block] * BLOCK, BLOCK), BLOCK)
            row = block % 16 * BLOCK
            weights.ref[there, :] = (p0, p1, p2, p3)[block // 16][row : row + BLOCK, :]
        mask_ref[...] = jnp.where(sc_ref[...] == sr_ref[...], 0.0, lowest)
        x_ref = x.ref
        weights.push()
        for xh in range(2):
            cols = slice(xh * 256, xh * 256 + 256)
            w = weights.ref.at[xh * 1024 : xh * 1024 + 1024]
            q.ref[:, cols] = (nn(x_ref[...], w[:, :256]) + mine_ref[xh, 0:1, :]).astype(bf16)
            k.ref[:, cols] = nn(x_ref[...], w[:, 256:512]).astype(bf16)
            v.ref[:, cols] = (nn(x_ref[...], w[:, 512:768]) + mine_ref[xh, 1:2, :]).astype(bf16)
        for result in (q, k, v):
            result.push()
        for pair in range(4):
            lanes = slice(pair * LANES, pair * LANES + LANES)
            for start in range(0, 512, 256):
                rows = slice(start, start + 256)
                query = q.ref[rows, lanes]
                low_half = lax.broadcasted_iota(jnp.int32, query.shape, 1) < HD
                parts = []
                for h in range(2):
                    one = jnp.where(low_half == (h == 0), query, jnp.zeros_like(query)) * HD**-0.5
                    scores = nt(one.astype(bf16), k.ref[:, lanes]) + mask_ref[rows, :]
                    shifted = jnp.exp(scores - jnp.max(scores, axis=-1, keepdims=True))
                    inverse = 1.0 / jnp.sum(shifted, axis=-1, keepdims=True)
                    probs_low = (shifted * inverse).astype(bf16)
                    probs.ref[2 * pair + h, rows, :] = probs_low
                    parts.append(nn(probs_low, v.ref[:, lanes]))
                ctx.ref[rows, lanes] = jnp.where(low_half, parts[0], parts[1]).astype(bf16)
            probs.push(1)
        ctx.push()
        for out in narrow(1024):
            low = slice(out.start + 1024, out.stop + 1024)
            part_ref[:, out] = (
                nt(ctx.ref[:, :256], weights.ref[out, 768:]) + nt(ctx.ref[:, 256:], weights.ref[low, 768:])
            ).astype(bf16)

    return call(
        kernel,
        [far((2048, 1024), bf16), *[far((512, 512), bf16)] * 4, far((8, 512, 512), bf16, 4), ((512, 1024), bf16)],
        (table, late(tokens), *pieces, mine, seg_col, seg_row),
        scratch=[((512, 512), f32)],
        limit=44,
    )


def up_forward(table, tokens, own, other, vectors, mine, pieces):
    def kernel(table_ref, x, own_ref, other_ref, vec_ref, mine_ref, p0, p1, p2, p3, p4, p5, p6, p7, up, down, normed, inv_ref, hidden, act, slope, up_sem, down_sem):
        place_blocks(table_ref, (p0, p1, p2, p3, p4, p5, p6, p7), 0, 2, up.ref, up_sem)
        place_blocks(table_ref, (p0, p1, p2, p3, p4, p5, p6, p7), 1, 2, down, down_sem)
        x_ref = x.ref

        def norm(rows):
            residual = x_ref[rows, :].astype(f32) + both(own_ref, other_ref, rows) + vec_ref[2:3, :]
            centered, inverse = norm_stats(residual)
            normed.ref[rows, :] = centered
            inv_ref[rows, :] = jnp.broadcast_to(inverse, (inverse.shape[0], LANES))
            hidden.ref[rows, :] = (centered * vec_ref[3:4, :] + vec_ref[4:5, :]).astype(bf16)

        chunks(4, 128, norm)
        normed.push()
        hidden.push()
        pltpu.make_async_copy(up.target, up.ref, up_sem).wait()
        up.push()
        for xh in range(2):
            for i, out in enumerate(narrow(1024)):
                cols = slice(xh * 1024 + out.start, xh * 1024 + out.stop)
                pre_act = nn(hidden.ref[...], up.ref[xh * 1024 : xh * 1024 + 1024, out]) + mine_ref[xh, 8 + i : 9 + i, :]
                cumulative = 0.5 * (1.0 + lax.erf(pre_act * 0.7071067811865476))
                density = jnp.exp(-0.5 * pre_act * pre_act) * 0.3989422804014327
                act[:, cols] = (pre_act * cumulative).astype(bf16)
                slope.ref[:, cols] = (cumulative + pre_act * density).astype(bf16)
            if xh == 0:
                pltpu.make_async_copy(down, down, down_sem).wait()

    return call(
        kernel,
        [
            far((2048, 1024), bf16),
            ((2048, 1024), bf16),
            far((512, 1024), f32),
            ((512, LANES), f32),
            far((512, 1024), bf16),
            ((512, 2048), bf16),
            far((512, 2048), bf16),
        ],
        (table, late(tokens), own, other, vectors, mine, *(("any", piece) for piece in pieces)),
        scratch=[pltpu.SemaphoreType.DMA, pltpu.SemaphoreType.DMA],
        limit=44,
    )


def down_forward(act, down):
    def kernel(act_ref, down_ref, part_ref):
        for out in narrow(1024):
            low = slice(out.start + 1024, out.stop + 1024)
            part_ref[:, out] = (
                nt(act_ref[:, :1024], down_ref[out, :]) + nt(act_ref[:, 1024:], down_ref[low, :])
            ).astype(bf16)

    return call(kernel, [((512, 1024), bf16)], (act, down), limit=12)[0]


def ffn_backward(blocks, normed_in, own, other, vectors, cot, down, slope, up):
    def kernel(blocks_ref, ni, own_ref, other_ref, vec_ref, cot_late, down, slope, up, keep_ref, away_ref, grad, low_ref, sums_ref, hidden_sums_ref, pre, part_ref, layer_ref):
        sums_ref[...] = jnp.zeros_like(sums_ref)
        hidden_sums_ref[...] = jnp.zeros_like(hidden_sums_ref)
        ni_ref, cot_ref = ni.ref, cot_late.ref

        def norm(rows):
            hidden = ni_ref[rows, :] * vec_ref[3:4, :] + vec_ref[4:5, :]
            residual = hidden + both(own_ref, other_ref, rows) + vec_ref[5:6, :]
            normed, inverse = norm_stats(residual)
            layer_ref[rows, :] = normed * vec_ref[6:7, :] + vec_ref[7:8, :]
            cot_rows = cot_ref[rows, :].astype(f32)
            grad_rows = norm_back(cot_rows, normed, inverse, vec_ref[6:7, :])
            grad.ref[rows, :] = grad_rows
            low_ref[rows, :] = grad_rows.astype(bf16)
            sums_ref[0:1, :] += jnp.sum(grad_rows, axis=0, keepdims=True)
            sums_ref[1:2, :] += jnp.sum(cot_rows * normed, axis=0, keepdims=True)
            sums_ref[2:3, :] += jnp.sum(cot_rows, axis=0, keepdims=True)

        chunks(4, 128, norm)
        grad.push()
        slope_ref = slope.ref
        for xh in range(2):
            down_ref = down.part(0)
            for out in narrow(1024):
                cols = slice(xh * 1024 + out.start, xh * 1024 + out.stop)
                act_grad = nn(low_ref[...], down_ref[xh * 1024 : xh * 1024 + 1024, out]).astype(bf16)
                pre_grad = act_grad.astype(f32) * slope_ref[:, cols].astype(f32)
                hidden_sums_ref[xh : xh + 1, out] = jnp.sum(pre_grad, axis=0, keepdims=True)
                pre.ref[:, cols] = pre_grad.astype(bf16)
        pre.push()
        up_ref = up.ref
        for out in narrow(1024):
            low = slice(out.start + 1024, out.stop + 1024)
            part_ref[:, out] = (
                nt(pre.ref[:, :1024], up_ref[out, :]) + nt(pre.ref[:, 1024:], up_ref[low, :])
            ).astype(bf16)
        keep_ref[...] = layer_ref[:, pl.ds(pl.multiple_of(blocks_ref[0] * 256, 256), 256)]
        away_ref[...] = layer_ref[:, pl.ds(pl.multiple_of(blocks_ref[1] * 256, 256), 256)].astype(bf16)

    return call(
        kernel,
        [((512, 256), f32), ((512, 256), bf16), far((512, 1024), f32), ((512, 1024), bf16), ((8, 1024), f32), ((8, 1024), f32), far((512, 2048), bf16), ((512, 1024), bf16)],
        (blocks, late(normed_in), own, other, vectors, late(cot), late(down, 2), late(slope), late(up)),
        scratch=[((512, 1024), f32)],
        limit=44,
    )


def up_backward(table, hidden_low, pre_low):
    def kernel(table_ref, hidden, pre, *rest):
        pieces, (flip_ref, full_ref) = rest[:4], rest[4:]
        flip_ref[...] = hidden.ref[...].T
        weight_grad(flip_ref, pre.ref, full_ref)
        split_blocks(table_ref, full_ref, pieces, slice(None))
        for piece in pieces:
            piece.push()

    return call(
        kernel,
        [far((512, 1024), bf16)] * 4,
        (table, late(hidden_low), late(pre_low)),
        scratch=[((1024, 512), bf16), ((2048, 1024), bf16)],
        limit=44,
    )


def out_backward(down_table, grad_ffn, own, other, normed_in, inverse, vectors, weights, context, low, act, awaited):
    def kernel(table_ref, gf, own_ref, other_ref, ni, inv_ref, vec_ref, w, ctx, ffn_low_ref, act, _, ga, cg_ref, sums_ref, out_grad, o0, o1, o2, o3, o4, low_ref, flip_ref, full_ref):
        pieces = (o0, o1, o2, o3, o4)
        sums_ref[...] = jnp.zeros_like(sums_ref)
        gf_ref, n_ref = gf.ref, ni.ref

        def norm(rows):
            hidden_grad = gf_ref[rows, :] + both(own_ref, other_ref, rows)
            normed = n_ref[rows, :]
            grad = norm_back(hidden_grad, normed, inv_ref[rows, :1], vec_ref[3:4, :])
            ga.ref[rows, :] = grad
            low_ref[rows, :] = grad.astype(bf16)
            sums_ref[0:1, :] += jnp.sum(grad, axis=0, keepdims=True)
            sums_ref[1:2, :] += jnp.sum(hidden_grad * normed, axis=0, keepdims=True)
            sums_ref[2:3, :] += jnp.sum(hidden_grad, axis=0, keepdims=True)

        chunks(4, 128, norm)
        ga.push()
        flip_ref[...] = ffn_low_ref[...].T
        weight_grad(flip_ref, act.ref, full_ref)
        split_blocks(table_ref, full_ref, pieces, slice(None), RING)
        for piece in pieces:
            piece.push()
        flip_ref[...] = low_ref[...].T
        weight_grad(flip_ref, ctx.ref, out_grad.ref)
        out_grad.push()
        w_ref = w.ref
        for xh in range(2):
            cg_ref[:, xh * 256 : xh * 256 + 256] = nn(low_ref[...], w_ref[xh * 1024 : xh * 1024 + 1024, :]).astype(bf16)

    return call(
        kernel,
        [far((512, 1024), f32), ((512, 512), bf16), ((8, 1024), f32), far((2048, 256), bf16), *[far((count, 1024), bf16) for count in RING_ROWS]],
        (down_table, late(grad_ffn), own, other, late(normed_in), inverse, vectors, late(weights, 1, slice(768, 1024)), late(context), low, late(act), ("any", awaited)),
        scratch=[((512, 1024), bf16), ((1024, 512), bf16), ((2048, 1024), bf16)],
        limit=44,
    )


def attention_backward(table, blocks, queries, keys, values, context_grad, probs, flip, weights, grad_attn, attn_sums, ffn_sums, hidden_sums, out_grad, awaited):
    def kernel(table_ref, blocks_ref, q, k, v, cg_ref, probs, flip, w, ga, as_ref, fs_ref, hs_ref, out_late, _, keep_ref, away_ref, o0, o1, o2, o3, full_ref, d_ref, part_ref, bias_ref, vec_ref):
        pieces = (o0, o1, o2, o3)
        bias_ref[...] = jnp.zeros_like(bias_ref)
        q_ref, k_ref, v_ref = q.ref, k.ref, v.ref
        for pair in range(4):
            lanes = slice(pair * LANES, pair * LANES + LANES)
            base = (pair // 2) * 768 + (pair % 2) * LANES
            p_ref = probs.part(0)
            key_flips, value_flips = [0.0, 0.0], [0.0, 0.0]
            for start in range(0, 512, 256):
                rows = slice(start, start + 256)
                grad = cg_ref[rows, lanes]
                grad_flip = grad.T
                query_flip = q_ref[rows, lanes].T
                low_half = lax.broadcasted_iota(jnp.int32, grad.shape, 1) < HD
                query_grads = []
                for h in range(2):
                    one = slice(h * HD, h * HD + HD)
                    grad_one = jnp.where(low_half == (h == 0), grad, jnp.zeros_like(grad))
                    probs_low = p_ref[2 * pair + h, rows, :]
                    attn = probs_low.astype(f32)
                    prob_grad = nt(grad_one, v_ref[:, lanes])
                    row_dot = jnp.sum(attn * prob_grad, axis=-1, keepdims=True)
                    score_low = (attn * (prob_grad - row_dot) * HD**-0.5).astype(bf16)
                    query_grads.append(nn(score_low, k_ref[:, lanes]))
                    key_flips[h] = key_flips[h] + nn(query_flip[one], score_low)
                    value_flips[h] = value_flips[h] + nn(grad_flip[one], probs_low)
                query_grad = jnp.where(low_half, query_grads[0], query_grads[1])
                bias_ref[0:1, lanes] += jnp.sum(query_grad, axis=0, keepdims=True)
                d_ref[rows, base : base + LANES] = query_grad.astype(bf16)
            key_grad = jnp.concatenate(key_flips, 0).T
            value_grad = jnp.concatenate(value_flips, 0).T
            bias_ref[1:2, lanes] = jnp.sum(value_grad, axis=0, keepdims=True)
            d_ref[:, base + 256 : base + 256 + LANES] = key_grad.astype(bf16)
            d_ref[:, base + 512 : base + 512 + LANES] = value_grad.astype(bf16)
        for xh in range(2):
            own = pl.ds(pl.multiple_of(blocks_ref[4 + xh] * 256, 256), 256)
            here = slice(xh * 256, xh * 256 + 256)
            parts = [bias_ref[0:1, here], bias_ref[1:2, here]]
            parts += [ref[i : i + 1, own] for ref in (as_ref, fs_ref) for i in range(3)]
            parts += [hs_ref[xh : xh + 1, out] for out in narrow(1024)]
            for i, part in enumerate(parts):
                vec_ref[xh * 4 + i // 3 : xh * 4 + i // 3 + 1, (i % 3) * 256 : (i % 3) * 256 + 256] = part
        vec_ref[8:16, :] = jnp.zeros((8, 768), f32)
        for piece in pieces:
            piece.ref[512:528, 0:768] = vec_ref[...].astype(bf16)
            piece.ref[512:528, 768:] = jnp.zeros((VECTOR_ROWS, 256), bf16)
        weight_grad(flip.ref, d_ref, full_ref)
        split_blocks(table_ref, full_ref, pieces, slice(0, 768))
        split_blocks(table_ref, out_late.ref, pieces, slice(768, 1024))
        for piece in pieces:
            piece.push()
        w_ref, ga_ref = w.ref, ga.ref
        for out in narrow(1024):
            low = slice(out.start + 1024, out.stop + 1024)
            part_ref[:, out] = nt(d_ref[:, :768], w_ref[out, :]) + nt(d_ref[:, 768:], w_ref[low, :])
        for i in range(2):
            own = pl.ds(pl.multiple_of(blocks_ref[i] * 256, 256), 256)
            across = pl.ds(pl.multiple_of(blocks_ref[2 + i] * 256, 256), 256)
            keep_ref[i, :, :] = part_ref[:, own] + ga_ref[:, own]
            away_ref[i, :, :] = part_ref[:, across].astype(bf16)

    return call(
        kernel,
        [((2, 512, 256), f32), ((2, 512, 256), bf16), *[far((528, 1024), bf16)] * 4],
        (table, blocks, late(queries), late(keys), late(values), context_grad, late(probs, 4), late(flip), late(weights, 1, slice(0, 768)), late(grad_attn), attn_sums, ffn_sums, hidden_sums, late(out_grad), ("any", awaited)),
        scratch=[((2048, 768), bf16), ((512, 1536), bf16), ((512, 1024), f32), ((8, 512), f32), ((16, 768), f32)],
        limit=44,
    )


def add_refs(refs, rows, cols=slice(None)):
    total = refs[0][rows, cols].astype(f32)
    for ref in refs[1:]:
        total = total + ref[rows, cols].astype(f32)
    return total


def add_split(parts, tail, fetch):
    rows, width = parts[0].shape
    quarter = (rows - tail) // 4

    def kernel(*refs):
        ins, outs = [ref.ref if fetch else ref for ref in refs[:4]], refs[4:]
        for i in range(4):
            outs[i][0:quarter, :] = add_refs(ins, slice(i * quarter, i * quarter + quarter)).astype(bf16)
        if tail:
            vectors = add_refs(ins, slice(4 * quarter, rows)).astype(bf16)
            for i in range(4):
                outs[i][quarter : quarter + tail, :] = vectors

    return call(kernel, [((quarter + tail, width), bf16)] * 4, [late(part) if fetch else part for part in parts], limit=16)


def add_passing(near, back, plus, minus):
    def kernel(near, back, plus, minus, near_ref, back_ref):
        half = slice(0, 256)
        near_ref[...] = add_refs((near.ref, plus.ref), half).astype(bf16)
        back_ref[...] = add_refs((back.ref, minus.ref), half).astype(bf16)

    return call(kernel, [((256, 1024), bf16)] * 2, [late(part) for part in (near, back, plus, minus)])


def add_ring(own, plus, minus, near, back):
    def kernel(own, plus, minus, near, back, *outs):
        own_ref, plus_ref, minus_ref, near_ref, back_ref = own.ref, plus.ref, minus.ref, near.ref, back.ref
        for i in range(4):
            rows, here = slice(i * 128, i * 128 + 128), slice(i % 2 * 128, i % 2 * 128 + 128)
            behind = slice(256 + here.start, 256 + here.stop)
            total = own_ref[rows, :].astype(f32)
            if i < 2:
                total = total + near_ref[here, :].astype(f32) + minus_ref[behind, :].astype(f32)
            else:
                total = total + back_ref[here, :].astype(f32) + plus_ref[behind, :].astype(f32)
            outs[i][...] = total.astype(bf16)

    return call(kernel, [((128, 1024), bf16)] * 4, [late(part) for part in (own, plus, minus, near, back)])


def merge_groups(attn, up, down):
    def kernel(*refs):
        ready, outs = [ref.ref for ref in refs[:12]], refs[12:]
        vectors = add_refs(ready[:4], slice(128, 128 + VECTOR_ROWS)).astype(bf16)
        for i in range(4):
            rows = slice(i * BLOCK, i * BLOCK + BLOCK)
            for group in range(3):
                cols = slice(group * 1024, group * 1024 + 1024)
                outs[i][0:BLOCK, cols] = add_refs(ready[4 * group : 4 * group + 4], rows).astype(bf16)
            outs[i][BLOCK : BLOCK + VECTOR_ROWS, 0:1024] = vectors
            outs[i][BLOCK : BLOCK + VECTOR_ROWS, 1024:] = jnp.zeros((VECTOR_ROWS, 2048), bf16)

    return call(kernel, [((BLOCK + VECTOR_ROWS, 3072), bf16)] * 4, [late(part) for part in (*attn, *up, *down)])


def final_sums(blocks, parts):
    def kernel(blocks_ref, *refs):
        ins, (qkv_ref, out_ref, up_ref, down_ref, *vectors) = refs[:4], refs[4:]
        rows = slice(0, BLOCK)
        for j in range(3):
            qkv_ref[j] = add_refs(ins, rows, slice(j * 256, j * 256 + 256))
        out_ref[...] = add_refs(ins, rows, slice(768, 1024))
        up_ref[...] = add_refs(ins, rows, slice(1024, 2048))
        down_ref[...] = add_refs(ins, rows, slice(2048, 3072))
        sums = add_refs(ins, slice(BLOCK, BLOCK + VECTOR_ROWS), slice(0, 768))
        sums = jnp.where(blocks_ref[6] == 0, sums[0:4], sums[4:8])
        for i in range(12):
            value = sums[i // 3 : i // 3 + 1, (i % 3) * 256 : (i % 3) * 256 + 256]
            if i < 8:
                vectors[i][...] = value
            else:
                vectors[8][:, (i - 8) * 256 : (i - 8) * 256 + 256] = value

    wide = ((BLOCK, 1024), f32)
    outs = [((3, BLOCK, 256), f32), ((BLOCK, 256), f32), wide, wide, *[((1, 256), f32)] * 8, ((1, 1024), f32)]
    return call(kernel, outs, (blocks, *parts))


def body(
    tokens,
    seg_ids,
    qkv_weight,
    q_bias,
    v_bias,
    out_weight,
    out_bias,
    gain_attn,
    shift_attn,
    up_weight,
    up_bias,
    down_weight,
    down_bias,
    gain_ffn,
    shift_ffn,
    out_grad,
):
    length = seg_ids.shape[1]
    cols = tokens.shape[1]
    xh = lax.axis_index("xh")
    core = lax.axis_index("core")
    place = {
        "x": xh * 2 + lax.axis_index("xl"),
        "y": lax.axis_index("y"),
        "z": lax.axis_index("z"),
        "core": core,
    }
    table = block_table(STAGES, place)
    down_table = block_table(DOWN_STAGES, place)
    blocks = jnp.stack(
        [xh * 2 + core, 2 - xh * 2 + core, xh * 2 + 1 - core, 3 - xh * 2 - core, core, 2 + core, xh]
    ).astype(jnp.int32)

    def halves(local):
        pair = local.reshape(2, length, cols)
        own = lax.dynamic_index_in_dim(pair, xh, 0, keepdims=False)
        away = lax.dynamic_index_in_dim(pair, 1 - xh, 0, keepdims=False)
        return own, away

    def two_sequences(own, partner):
        partner = partner.astype(f32)
        return jnp.where(xh == 0, jnp.stack([own, partner]), jnp.stack([partner, own])).reshape(2 * length, cols)

    own_tokens, away_tokens = halves(tokens)
    token_partner = swap_xh(away_tokens)
    vectors = stack_vectors(
        (q_bias, v_bias, out_bias, gain_attn, shift_attn, down_bias, gain_ffn, shift_ffn), up_bias
    )
    vector_partner = swap_xh(vectors)
    first = gather_direct(round_weights(qkv_weight, out_weight, up_weight, down_weight), STAGES[0])
    first = lax.optimization_barrier((*first, token_partner))
    token_partner = first[4]
    attn_level, ffn_level = part_groups(first[:4])
    attn_second = gather_direct(attn_level, STAGES[1])
    token_across = swap_core(jnp.stack([own_tokens, token_partner]))
    vector_across = swap_core(jnp.stack([vectors, vector_partner]))
    attn_second = lax.optimization_barrier((*attn_second, token_across, vector_across))
    token_across, vector_across = attn_second[4:]
    attn_pieces = gather_direct(*stack(attn_second[:4]), STAGES[2])
    token_rows, token_flip = collect_tokens(blocks, own_tokens, token_partner, token_across, True)
    rows, mine = collect_vectors(blocks, vectors, vector_partner, vector_across)
    ffn_second = gather_direct(after(ffn_level, *attn_second[1:4]), STAGES[1])
    ffn_first, ffn_last, ffn_up, ffn_down = gather_halves(*stack(ffn_second, 2, (*attn_pieces[1:], token_flip, mine)), STAGES[2])
    segment = lax.dynamic_index_in_dim(seg_ids, xh, 0, keepdims=False)

    attn_full, queries, keys, values, context, probs, attn_part = attention_forward(
        table, token_rows, attn_pieces, mine, segment[:, None], segment[None, :]
    )
    ffn_beyond = gather_beyond(
        (ffn_up[0], after(ffn_up[1], attn_part)), (after(ffn_down[0], attn_part), ffn_down[1]), STAGES[2]
    )
    ffn_pieces = ffn_first, ffn_last, *ffn_up, *ffn_beyond, *ffn_down
    up_full, down_full, normed_attn, inverse_attn, hidden_low, activated, slope = up_forward(
        table, token_rows, attn_part, swap_core(attn_part), rows, mine, ffn_pieces
    )
    own_cot, away_cot = halves(out_grad.astype(bf16))
    cot_partner = swap_xh(after(away_cot, *ffn_pieces[2:]))
    ffn_part = down_forward(after(activated, cot_partner), down_full)
    cot_rows = collect_tokens(blocks, own_cot, cot_partner, swap_core(jnp.stack([own_cot, cot_partner])), False)[0]
    layer_own, layer_away, grad_resid_ffn, ffn_grad_low, ffn_sums, hidden_sums, pre_grad_low, hidden_part = ffn_backward(
        blocks, normed_attn, ffn_part, swap_core(ffn_part), rows, cot_rows, down_full, slope, up_full
    )
    layer_partner = swap_xh(layer_away)
    up_own, up_near, up_far, up_back = up_backward(table, hidden_low, pre_grad_low)
    up_near = send(after(up_near, layer_partner), STAGES[2], 1)
    up_far = send(up_far, STAGES[2], 2)
    grad_resid_attn, context_grad, attn_sums, out_weight_grad, *down_ring = out_backward(
        down_table, grad_resid_ffn, hidden_part, swap_core(hidden_part), normed_attn, inverse_attn,
        rows, attn_full, context, ffn_grad_low, activated, up_own,
    )
    up_parts = up_own, up_near, up_far, send(after(up_back, attn_sums), STAGES[2], -1)
    down_own, down_plus, down_minus, down_near, down_back = down_ring
    down_plus, down_minus = send(down_plus, DOWN_STAGES[2], 1), send(down_minus, DOWN_STAGES[2], -1)
    input_own, input_away, *attn_parts = attention_backward(
        table, blocks, queries, keys, values, context_grad, probs, token_flip, attn_full,
        grad_resid_attn, attn_sums, ffn_sums, hidden_sums, out_weight_grad, up_parts[0],
    )
    attn_own, attn_near, attn_far, attn_back = lax.optimization_barrier((*attn_parts, *up_parts[1:]))[:4]
    attn_back = after(attn_back, down_plus)
    attn_parts = scatter_direct((attn_own, attn_near, attn_far, attn_back), STAGES[2])
    up_parts = scatter_direct(add_split(up_parts, 0, True), STAGES[1])
    down_near, down_back = add_passing(down_near, down_back, down_plus, down_minus)
    down_near, down_back = send(down_near, DOWN_STAGES[2], 1), send(down_back, DOWN_STAGES[2], -1)
    down_parts = add_ring(down_own, down_plus, down_minus, down_near, down_back)
    down_parts = scatter_direct(down_parts, DOWN_STAGES[1])
    attn_parts = add_split(attn_parts, VECTOR_ROWS, False)
    input_own = input_own + swap_core(after(input_away, attn_parts[0])).astype(f32)
    attn_parts = scatter_direct(lax.optimization_barrier((*attn_parts, up_parts[1], up_parts[3]))[:4], STAGES[1])
    input_away = after(input_own[1].astype(bf16), attn_parts[1])
    input_grad = two_sequences(input_own[0], swap_xh(input_away))
    layer_out = two_sequences(layer_own, layer_partner)
    last = scatter_direct(merge_groups(attn_parts, up_parts, down_parts), STAGES[0])
    qkv_grad, out_grad_rows, up_rows, down_rows, *sums = final_sums(blocks, last)
    (
        q_bias_grad,
        v_bias_grad,
        out_bias_grad,
        gain_attn_grad,
        shift_attn_grad,
        down_bias_grad,
        gain_ffn_grad,
        shift_ffn_grad,
        up_bias_grad,
    ) = (value.reshape(-1) for value in sums)
    return (
        layer_out,
        input_grad,
        qkv_grad.transpose(1, 0, 2),
        q_bias_grad,
        v_bias_grad,
        out_grad_rows,
        out_bias_grad,
        gain_attn_grad,
        shift_attn_grad,
        up_rows,
        up_bias_grad,
        down_rows,
        down_bias_grad,
        gain_ffn_grad,
        shift_ffn_grad,
    )


def solution(mesh):
    placed_mesh = Mesh(mesh.devices.reshape(4, 4, 2, 2, 2), AXES)
    placed = (
        P(ROW, COL),
        P(ROW, None),
        P(ROW, None, COL),
        P(COL),
        P(COL),
        P(ROW, COL),
        P(COL),
        P(COL),
        P(COL),
        P(ROW, COL),
        P(COL),
        P(ROW, COL),
        P(COL),
        P(COL),
        P(COL),
        P(ROW, COL),
    )
    return jax.shard_map(
        body,
        mesh=placed_mesh,
        in_specs=placed,
        out_specs=(
            P(ROW, COL),
            P(ROW, COL),
            P(ROW, None, COL),
            P(COL),
            P(COL),
            P(ROW, COL),
            P(COL),
            P(COL),
            P(COL),
            P(ROW, COL),
            P(COL),
            P(ROW, COL),
            P(COL),
            P(COL),
            P(COL),
        ),
        check_vma=False,
    )
```

```python
import itertools

import jax
import jax.numpy as jnp
from jax import lax
from jax.experimental import pallas as pl
from jax.experimental.pallas import tpu as pltpu
from jax.sharding import Mesh, PartitionSpec as P

HD = 64
AXES = ("z", "y", "xl", "xh", "core")
ROW = ("z", "y", "xl")
COL = ("xh", "core")
CHIPS = ("z", "y", "xl", "xh")
lowest = -1e30
epsilon = 1e-06
bf16 = jnp.bfloat16
f32 = jnp.float32

STAGES = (("x", "z"), ("y", "y"), ("z", "x"))
DOWN_STAGES = (("x", "z"), ("z", "x"), ("y", "y"))


def device_at(x, y, z, core):
    return ((z * 4 + y) * 2 + x % 2) * 4 + (x // 2) * 2 + core


def shifts(axes, step):
    pairs = []
    for x, y, z, core in itertools.product(range(4), range(4), range(4), range(2)):
        to = {"x": x, "y": y, "z": z}
        axis = axes[core]
        to[axis] = (to[axis] + (step if core == 0 else -step)) % 4
        pairs.append((device_at(x, y, z, core), device_at(to["x"], to["y"], to["z"], core)))
    return pairs


def send(value, axes, step):
    return lax.ppermute(value, AXES, shifts(axes, step))


def swap_core(value):
    return lax.ppermute(value, "core", [(0, 1), (1, 0)])


def swap_xh(value):
    return lax.ppermute(value, "xh", [(0, 1), (1, 0)])


def gather_direct(value, axes):
    return value, send(value, axes, -1), send(value, axes, 2), send(value, axes, 1)


def gather_halves(first, second, axes):
    down = send(first, axes, 1), send(second, axes, 1)
    up = send(first, axes, -1), send(second, axes, -1)
    return first, second, up, down


def gather_beyond(up, down, axes):
    return send(down[0], axes, 1), send(up[1], axes, -1)


def scatter_direct(pieces, axes):
    own, near, far, back = pieces
    return own, send(near, axes, 1), send(far, axes, 2), send(back, axes, -1)


def after(value, *others):
    return lax.optimization_barrier((value, *others))[0]


def quarters(value):
    quarter = value.shape[0] // 4
    return [value[i * quarter : (i + 1) * quarter] for i in range(4)]


def block_table(stages, place):
    index = jnp.arange(64, dtype=jnp.int32)
    offset = (index % 4, (index // 4) % 4, index // 16)
    tables = []
    for core in range(2):
        at = {}
        for stage in range(3):
            axis = stages[stage][core]
            at[axis] = (place[axis] + (1 - 2 * core) * offset[stage] + 4) % 4
        tables.append((((at["x"] // 2) * 4 + at["z"]) * 4 + at["y"]) * 2 + at["x"] % 2)
    return jnp.where(place["core"] == 0, tables[0], tables[1])


MIB = 1024 * 1024
BLOCK = 32
VECTOR_ROWS = 16
LANES = 128


class Late:
    def __init__(self, source, target, sems, count, cols):
        rows = target.shape[0] // count
        if cols is not None:
            source = source.at[:, cols]
        self.target, self.copies = target, []
        for i in range(count):
            part = pl.ds(i * rows, rows)
            self.copies.append(pltpu.make_async_copy(source.at[part], target.at[part], sems.at[i]))
        for copy in self.copies:
            copy.start()

    def part(self, upto):
        while len(self.copies) and upto >= 0:
            self.copies.pop(0).wait()
            upto -= 1
        return self.target

    @property
    def ref(self):
        return self.part(len(self.copies))


class Far:
    def __init__(self, target, source, sems, count):
        rows = source.shape[0] // count
        self.ref, self.target, self.started, self.waiting = source, target, [], []
        for i in range(count):
            part = pl.ds(i * rows, rows)
            self.waiting.append(pltpu.make_async_copy(source.at[part], target.at[part], sems.at[i]))

    def push(self, count=None):
        for _ in range(len(self.waiting) if count is None else count):
            copy = self.waiting.pop(0)
            copy.start()
            self.started.append(copy)

    def finish(self):
        self.push()
        for copy in self.started:
            copy.wait()


def late(value, count=1, cols=None):
    return ("late", value, count, cols)


def far(shape, dtype, count=1):
    return ("far", shape, dtype, count)


def call(body, outs, args, scratch=(), flops=1 << 20, limit=12):
    in_specs, values, extra, lates = [], [], [], {}
    for i, arg in enumerate(args):
        if not isinstance(arg, tuple):
            scalar = arg.ndim == 1 and arg.dtype == jnp.int32
            in_specs.append(pl.BlockSpec(memory_space=pltpu.SMEM if scalar else pltpu.VMEM))
            values.append(arg)
            continue
        in_specs.append(pl.BlockSpec(memory_space=pltpu.HBM))
        values.append(arg[1])
        if arg[0] == "late":
            _, value, count, cols = arg
            shape = value.shape if cols is None else (value.shape[0], cols.stop - cols.start)
            lates[i] = (len(extra), count, cols)
            extra += [pltpu.VMEM(shape, value.dtype), pltpu.SemaphoreType.DMA((count,))]
    out_specs, shapes, fars = [], [], {}
    for i, out in enumerate(outs):
        if out[0] == "far":
            fars[i] = (len(extra), out[3])
            extra += [pltpu.VMEM(out[1], out[2]), pltpu.SemaphoreType.DMA((out[3],))]
        plain = out[0] not in ("far", "any")
        out_specs.append(pl.BlockSpec(memory_space=pltpu.VMEM if plain else pltpu.HBM))
        shapes.append(jax.ShapeDtypeStruct(*(out if plain else out[1:3])))

    def kernel(*refs):
        ins, rest = list(refs[: len(args)]), refs[len(args) :]
        results, rest = list(rest[: len(outs)]), rest[len(outs) :]
        own, rest = rest[: len(extra)], rest[len(extra) :]
        for i, (at, count, cols) in lates.items():
            ins[i] = Late(ins[i], own[at], own[at + 1], count, cols)
        for i, (at, count) in fars.items():
            results[i] = Far(results[i], own[at], own[at + 1], count)
        body(*ins, *results, *rest)
        for i in lates:
            ins[i].ref
        for i in fars:
            results[i].finish()

    return pl.pallas_call(
        kernel,
        out_shape=shapes,
        in_specs=in_specs,
        out_specs=out_specs,
        scratch_shapes=[*extra, *(s if not isinstance(s, tuple) else pltpu.VMEM(*s) for s in scratch)],
        compiler_params=pltpu.CompilerParams(vmem_limit_bytes=limit * MIB),
        cost_estimate=pl.CostEstimate(flops=flops, bytes_accessed=1 << 12, transcendentals=0),
    )(*values)


def nn(left, right):
    return lax.dot_general(left, right, (((1,), (0,)), ((), ())), preferred_element_type=f32)


def nt(left, right):
    return lax.dot_general(left, right, (((1,), (1,)), ((), ())), preferred_element_type=f32)


def chunks(count, size, step):
    for i in range(count):
        step(slice(i * size, i * size + size))


def narrow(total):
    return [slice(start, start + 256) for start in range(0, total, 256)]


def place_blocks(table_ref, pieces, group, groups, full_ref, sem):
    blocks = [(piece, row) for piece in pieces for row in range(0, piece.shape[0], 4 * BLOCK * groups)]
    for i, (piece, first) in enumerate(blocks):
        for j in range(4):
            row = first + (group * 4 + j) * BLOCK
            there = pl.ds(pl.multiple_of(table_ref[4 * i + j] * BLOCK, BLOCK), BLOCK)
            pltpu.make_async_copy(piece.at[pl.ds(row, BLOCK)], full_ref.at[there], sem).start()


DIRECT = tuple((i // 2, i % 2 * 256) for i in range(8))
RING = ((0, 0), (0, 256), (3, 0), (1, 256), (1, 0), (2, 0), (2, 256), (4, 0))
RING_ROWS = (512, 512, 512, 256, 256)


def split_blocks(table_ref, grad_ref, pieces, cols, layout=DIRECT):
    for block in range(64):
        piece, row = layout[block // 8]
        row += (block % 8) * BLOCK
        there = pl.multiple_of(table_ref[block] * BLOCK, BLOCK)
        pieces[piece].ref[row : row + BLOCK, cols] = grad_ref[pl.ds(there, BLOCK), :]


def weight_grad(left_ref, right_ref, grad_ref):
    half = right_ref.shape[1] // 2
    for xh in range(2):
        for cols in narrow(half):
            from_cols = slice(xh * half + cols.start, xh * half + cols.stop)
            grad_ref[xh * 1024 : xh * 1024 + 1024, cols] = nn(left_ref[...], right_ref[:, from_cols]).astype(bf16)


def row_mean(value):
    return jnp.mean(value, axis=-1, keepdims=True)


def norm_stats(residual):
    center = residual - row_mean(residual)
    inverse = lax.rsqrt(row_mean(center * center) + epsilon)
    return center * inverse, inverse


def norm_back(grad, normed, inverse, gain):
    scaled = grad * gain
    return inverse * (scaled - row_mean(scaled) - normed * row_mean(scaled * normed))


def both(own_ref, other_ref, rows):
    return own_ref[rows, :].astype(f32) + other_ref[rows, :].astype(f32)


def round_weights(qkv_weight, out_weight, up_weight, down_weight):
    def kernel(qkv, out, up, down, low_ref):
        for j in range(3):
            low_ref[0:32, j * 256 : j * 256 + 256] = qkv.ref[j].astype(bf16)
        low_ref[0:32, 768:] = out.ref[...].astype(bf16)
        low_ref[32:64, :] = up.ref[...].astype(bf16)
        low_ref[64:96, :] = down.ref[...].astype(bf16)

    weights = (qkv_weight.transpose(1, 0, 2), out_weight, up_weight, down_weight)
    return call(kernel, [((96, 1024), bf16)], [late(weight) for weight in weights])[0]


def part_groups(pieces):
    def kernel(*refs):
        for i in range(4):
            rows = slice(i * BLOCK, i * BLOCK + BLOCK)
            refs[4][rows, :] = refs[i][0:BLOCK, :]
            refs[5][rows, :] = refs[i][BLOCK : 2 * BLOCK, :]
            refs[5][128 + rows.start : 128 + rows.stop, :] = refs[i][2 * BLOCK :, :]

    return call(kernel, [((128, 1024), bf16), ((256, 1024), bf16)], pieces)


def stack(pieces, count=1, awaited=()):
    rows = pieces[0].shape[0]
    each = 4 // count

    def kernel(*refs):
        outs = refs[-count:]
        for i in range(4):
            outs[i // each][(i % each) * rows : (i % each) * rows + rows, :] = refs[i][...]

    return call(kernel, [((each * rows, 1024), bf16)] * count, (*pieces, *(("any", value) for value in awaited)))


def collect_tokens(blocks, own, partner, across, flip):
    def kernel(blocks_ref, own_ref, partner_ref, across_ref, out, *flipped):
        parts = (own_ref[...], partner_ref[...], across_ref[0], across_ref[1])
        for i in range(4):
            out.ref[:, pl.ds(pl.multiple_of(blocks_ref[i] * 256, 256), 256)] = parts[i]
        out.push()
        if flip:
            flipped[0].ref[...] = out.ref[...].T

    outs = [far((512, 1024), bf16)] + ([far((1024, 512), bf16)] if flip else [])
    return call(kernel, outs, (blocks, own, partner, across))


def stack_vectors(vectors, up_bias):
    def kernel(*refs):
        for i in range(8):
            refs[9][i : i + 1, :] = refs[i][...]
        for i in range(4):
            refs[9][8 + i : 9 + i, :] = refs[8][:, i * 256 : i * 256 + 256]
        refs[9][12:16, :] = jnp.zeros((4, 256), f32)

    args = [vector.reshape(1, -1) for vector in (*vectors, up_bias)]
    return call(kernel, [((16, 256), f32)], args)[0]


def collect_vectors(blocks, own, partner, across):
    def kernel(blocks_ref, own_ref, partner_ref, across_ref, rows_ref, mine_ref):
        parts = (own_ref[...], partner_ref[...], across_ref[0], across_ref[1])
        for i in range(4):
            rows_ref[:, pl.ds(pl.multiple_of(blocks_ref[i] * 256, 256), 256)] = parts[i][0:8, :]
        mine_ref[blocks_ref[6]] = parts[0]
        mine_ref[1 - blocks_ref[6]] = parts[1]

    return call(kernel, [((8, 1024), f32), ((2, 16, 256), f32)], (blocks, own, partner, across))


def attention_forward(table, tokens, pieces, mine, seg_col, seg_row):
    def kernel(table_ref, x, p0, p1, p2, p3, mine_ref, sc_ref, sr_ref, weights, q, k, v, ctx, probs, part_ref, mask_ref):
        for block in range(64):
            there = pl.ds(pl.multiple_of(table_ref[block] * BLOCK, BLOCK), BLOCK)
            row = block % 16 * BLOCK
            weights.ref[there, :] = (p0, p1, p2, p3)[block // 16][row : row + BLOCK, :]
        mask_ref[...] = jnp.where(sc_ref[...] == sr_ref[...], 0.0, lowest)
        x_ref = x.ref
        weights.push()
        for xh in range(2):
            cols = slice(xh * 256, xh * 256 + 256)
            w = weights.ref.at[xh * 1024 : xh * 1024 + 1024]
            q.ref[:, cols] = (nn(x_ref[...], w[:, :256]) + mine_ref[xh, 0:1, :]).astype(bf16)
            k.ref[:, cols] = nn(x_ref[...], w[:, 256:512]).astype(bf16)
            v.ref[:, cols] = (nn(x_ref[...], w[:, 512:768]) + mine_ref[xh, 1:2, :]).astype(bf16)
        for result in (q, k, v):
            result.push()
        for pair in range(4):
            lanes = slice(pair * LANES, pair * LANES + LANES)
            for start in range(0, 512, 256):
                rows = slice(start, start + 256)
                query = q.ref[rows, lanes]
                low_half = lax.broadcasted_iota(jnp.int32, query.shape, 1) < HD
                parts = []
                for h in range(2):
                    one = jnp.where(low_half == (h == 0), query, jnp.zeros_like(query)) * HD**-0.5
                    scores = nt(one.astype(bf16), k.ref[:, lanes]) + mask_ref[rows, :]
                    shifted = jnp.exp(scores - jnp.max(scores, axis=-1, keepdims=True))
                    inverse = 1.0 / jnp.sum(shifted, axis=-1, keepdims=True)
                    probs_low = (shifted * inverse).astype(bf16)
                    probs.ref[2 * pair + h, rows, :] = probs_low
                    parts.append(nn(probs_low, v.ref[:, lanes]))
                ctx.ref[rows, lanes] = jnp.where(low_half, parts[0], parts[1]).astype(bf16)
            probs.push(1)
        ctx.push()
        for out in narrow(1024):
            low = slice(out.start + 1024, out.stop + 1024)
            part_ref[:, out] = (
                nt(ctx.ref[:, :256], weights.ref[out, 768:]) + nt(ctx.ref[:, 256:], weights.ref[low, 768:])
            ).astype(bf16)

    return call(
        kernel,
        [far((2048, 1024), bf16), *[far((512, 512), bf16)] * 4, far((8, 512, 512), bf16, 4), ((512, 1024), bf16)],
        (table, late(tokens), *pieces, mine, seg_col, seg_row),
        scratch=[((512, 512), f32)],
        limit=44,
    )


def up_forward(table, tokens, own, other, vectors, mine, pieces):
    def kernel(table_ref, x, own_ref, other_ref, vec_ref, mine_ref, p0, p1, p2, p3, p4, p5, p6, p7, up, down, normed, inv_ref, hidden, act, slope, up_sem, down_sem):
        place_blocks(table_ref, (p0, p1, p2, p3, p4, p5, p6, p7), 0, 2, up.ref, up_sem)
        place_blocks(table_ref, (p0, p1, p2, p3, p4, p5, p6, p7), 1, 2, down, down_sem)
        x_ref = x.ref

        def norm(rows):
            residual = x_ref[rows, :].astype(f32) + both(own_ref, other_ref, rows) + vec_ref[2:3, :]
            centered, inverse = norm_stats(residual)
            normed.ref[rows, :] = centered
            inv_ref[rows, :] = jnp.broadcast_to(inverse, (inverse.shape[0], LANES))
            hidden.ref[rows, :] = (centered * vec_ref[3:4, :] + vec_ref[4:5, :]).astype(bf16)

        chunks(4, 128, norm)
        normed.push()
        hidden.push()
        pltpu.make_async_copy(up.target, up.ref, up_sem).wait()
        up.push()
        for xh in range(2):
            for i, out in enumerate(narrow(1024)):
                cols = slice(xh * 1024 + out.start, xh * 1024 + out.stop)
                pre_act = nn(hidden.ref[...], up.ref[xh * 1024 : xh * 1024 + 1024, out]) + mine_ref[xh, 8 + i : 9 + i, :]
                cumulative = 0.5 * (1.0 + lax.erf(pre_act * 0.7071067811865476))
                density = jnp.exp(-0.5 * pre_act * pre_act) * 0.3989422804014327
                act[:, cols] = (pre_act * cumulative).astype(bf16)
                slope.ref[:, cols] = (cumulative + pre_act * density).astype(bf16)
            if xh == 0:
                pltpu.make_async_copy(down, down, down_sem).wait()

    return call(
        kernel,
        [
            far((2048, 1024), bf16),
            ((2048, 1024), bf16),
            far((512, 1024), f32),
            ((512, LANES), f32),
            far((512, 1024), bf16),
            ((512, 2048), bf16),
            far((512, 2048), bf16),
        ],
        (table, late(tokens), own, other, vectors, mine, *(("any", piece) for piece in pieces)),
        scratch=[pltpu.SemaphoreType.DMA, pltpu.SemaphoreType.DMA],
        limit=44,
    )


def down_forward(act, down):
    def kernel(act_ref, down_ref, part_ref):
        for out in narrow(1024):
            low = slice(out.start + 1024, out.stop + 1024)
            part_ref[:, out] = (
                nt(act_ref[:, :1024], down_ref[out, :]) + nt(act_ref[:, 1024:], down_ref[low, :])
            ).astype(bf16)

    return call(kernel, [((512, 1024), bf16)], (act, down), limit=12)[0]


def ffn_backward(blocks, normed_in, own, other, vectors, cot, down, slope, up):
    def kernel(blocks_ref, ni, own_ref, other_ref, vec_ref, cot_late, down, slope, up, keep_ref, away_ref, grad, low_ref, sums_ref, hidden_sums_ref, pre, part_ref, layer_ref):
        sums_ref[...] = jnp.zeros_like(sums_ref)
        hidden_sums_ref[...] = jnp.zeros_like(hidden_sums_ref)
        ni_ref, cot_ref = ni.ref, cot_late.ref

        def norm(rows):
            hidden = ni_ref[rows, :] * vec_ref[3:4, :] + vec_ref[4:5, :]
            residual = hidden + both(own_ref, other_ref, rows) + vec_ref[5:6, :]
            normed, inverse = norm_stats(residual)
            layer_ref[rows, :] = normed * vec_ref[6:7, :] + vec_ref[7:8, :]
            cot_rows = cot_ref[rows, :].astype(f32)
            grad_rows = norm_back(cot_rows, normed, inverse, vec_ref[6:7, :])
            grad.ref[rows, :] = grad_rows
            low_ref[rows, :] = grad_rows.astype(bf16)
            sums_ref[0:1, :] += jnp.sum(grad_rows, axis=0, keepdims=True)
            sums_ref[1:2, :] += jnp.sum(cot_rows * normed, axis=0, keepdims=True)
            sums_ref[2:3, :] += jnp.sum(cot_rows, axis=0, keepdims=True)

        chunks(4, 128, norm)
        grad.push()
        slope_ref = slope.ref
        for xh in range(2):
            down_ref = down.part(0)
            for out in narrow(1024):
                cols = slice(xh * 1024 + out.start, xh * 1024 + out.stop)
                act_grad = nn(low_ref[...], down_ref[xh * 1024 : xh * 1024 + 1024, out]).astype(bf16)
                pre_grad = act_grad.astype(f32) * slope_ref[:, cols].astype(f32)
                hidden_sums_ref[xh : xh + 1, out] = jnp.sum(pre_grad, axis=0, keepdims=True)
                pre.ref[:, cols] = pre_grad.astype(bf16)
        pre.push()
        up_ref = up.ref
        for out in narrow(1024):
            low = slice(out.start + 1024, out.stop + 1024)
            part_ref[:, out] = (
                nt(pre.ref[:, :1024], up_ref[out, :]) + nt(pre.ref[:, 1024:], up_ref[low, :])
            ).astype(bf16)
        keep_ref[...] = layer_ref[:, pl.ds(pl.multiple_of(blocks_ref[0] * 256, 256), 256)]
        away_ref[...] = layer_ref[:, pl.ds(pl.multiple_of(blocks_ref[1] * 256, 256), 256)].astype(bf16)

    return call(
        kernel,
        [((512, 256), f32), ((512, 256), bf16), far((512, 1024), f32), ((512, 1024), bf16), ((8, 1024), f32), ((8, 1024), f32), far((512, 2048), bf16), ((512, 1024), bf16)],
        (blocks, late(normed_in), own, other, vectors, late(cot), late(down, 2), late(slope), late(up)),
        scratch=[((512, 1024), f32)],
        limit=44,
    )


def up_backward(table, hidden_low, pre_low):
    def kernel(table_ref, hidden, pre, *rest):
        pieces, (flip_ref, full_ref) = rest[:4], rest[4:]
        flip_ref[...] = hidden.ref[...].T
        weight_grad(flip_ref, pre.ref, full_ref)
        split_blocks(table_ref, full_ref, pieces, slice(None))
        for piece in pieces:
            piece.push()

    return call(
        kernel,
        [far((512, 1024), bf16)] * 4,
        (table, late(hidden_low), late(pre_low)),
        scratch=[((1024, 512), bf16), ((2048, 1024), bf16)],
        limit=44,
    )


def out_backward(down_table, grad_ffn, own, other, normed_in, inverse, vectors, weights, context, low, act, awaited):
    def kernel(table_ref, gf, own_ref, other_ref, ni, inv_ref, vec_ref, w, ctx, ffn_low_ref, act, _, ga, cg_ref, sums_ref, out_grad, o0, o1, o2, o3, o4, low_ref, flip_ref, full_ref):
        pieces = (o0, o1, o2, o3, o4)
        sums_ref[...] = jnp.zeros_like(sums_ref)
        gf_ref, n_ref = gf.ref, ni.ref

        def norm(rows):
            hidden_grad = gf_ref[rows, :] + both(own_ref, other_ref, rows)
            normed = n_ref[rows, :]
            grad = norm_back(hidden_grad, normed, inv_ref[rows, :1], vec_ref[3:4, :])
            ga.ref[rows, :] = grad
            low_ref[rows, :] = grad.astype(bf16)
            sums_ref[0:1, :] += jnp.sum(grad, axis=0, keepdims=True)
            sums_ref[1:2, :] += jnp.sum(hidden_grad * normed, axis=0, keepdims=True)
            sums_ref[2:3, :] += jnp.sum(hidden_grad, axis=0, keepdims=True)

        chunks(4, 128, norm)
        ga.push()
        flip_ref[...] = ffn_low_ref[...].T
        weight_grad(flip_ref, act.ref, full_ref)
        split_blocks(table_ref, full_ref, pieces, slice(None), RING)
        for piece in pieces:
            piece.push()
        flip_ref[...] = low_ref[...].T
        weight_grad(flip_ref, ctx.ref, out_grad.ref)
        out_grad.push()
        w_ref = w.ref
        for xh in range(2):
            cg_ref[:, xh * 256 : xh * 256 + 256] = nn(low_ref[...], w_ref[xh * 1024 : xh * 1024 + 1024, :]).astype(bf16)

    return call(
        kernel,
        [far((512, 1024), f32), ((512, 512), bf16), ((8, 1024), f32), far((2048, 256), bf16), *[far((count, 1024), bf16) for count in RING_ROWS]],
        (down_table, late(grad_ffn), own, other, late(normed_in), inverse, vectors, late(weights, 1, slice(768, 1024)), late(context), low, late(act), ("any", awaited)),
        scratch=[((512, 1024), bf16), ((1024, 512), bf16), ((2048, 1024), bf16)],
        limit=44,
    )


def attention_backward(table, blocks, queries, keys, values, context_grad, probs, flip, weights, grad_attn, attn_sums, ffn_sums, hidden_sums, out_grad, awaited):
    def kernel(table_ref, blocks_ref, q, k, v, cg_ref, probs, flip, w, ga, as_ref, fs_ref, hs_ref, out_late, _, keep_ref, away_ref, o0, o1, o2, o3, full_ref, d_ref, part_ref, bias_ref, vec_ref):
        pieces = (o0, o1, o2, o3)
        bias_ref[...] = jnp.zeros_like(bias_ref)
        q_ref, k_ref, v_ref = q.ref, k.ref, v.ref
        for pair in range(4):
            lanes = slice(pair * LANES, pair * LANES + LANES)
            base = (pair // 2) * 768 + (pair % 2) * LANES
            p_ref = probs.part(0)
            key_flips, value_flips = [0.0, 0.0], [0.0, 0.0]
            for start in range(0, 512, 256):
                rows = slice(start, start + 256)
                grad = cg_ref[rows, lanes]
                grad_flip = grad.T
                query_flip = q_ref[rows, lanes].T
                low_half = lax.broadcasted_iota(jnp.int32, grad.shape, 1) < HD
                query_grads = []
                for h in range(2):
                    one = slice(h * HD, h * HD + HD)
                    grad_one = jnp.where(low_half == (h == 0), grad, jnp.zeros_like(grad))
                    probs_low = p_ref[2 * pair + h, rows, :]
                    attn = probs_low.astype(f32)
                    prob_grad = nt(grad_one, v_ref[:, lanes])
                    row_dot = jnp.sum(attn * prob_grad, axis=-1, keepdims=True)
                    score_low = (attn * (prob_grad - row_dot) * HD**-0.5).astype(bf16)
                    query_grads.append(nn(score_low, k_ref[:, lanes]))
                    key_flips[h] = key_flips[h] + nn(query_flip[one], score_low)
                    value_flips[h] = value_flips[h] + nn(grad_flip[one], probs_low)
                query_grad = jnp.where(low_half, query_grads[0], query_grads[1])
                bias_ref[0:1, lanes] += jnp.sum(query_grad, axis=0, keepdims=True)
                d_ref[rows, base : base + LANES] = query_grad.astype(bf16)
            key_grad = jnp.concatenate(key_flips, 0).T
            value_grad = jnp.concatenate(value_flips, 0).T
            bias_ref[1:2, lanes] = jnp.sum(value_grad, axis=0, keepdims=True)
            d_ref[:, base + 256 : base + 256 + LANES] = key_grad.astype(bf16)
            d_ref[:, base + 512 : base + 512 + LANES] = value_grad.astype(bf16)
        for xh in range(2):
            own = pl.ds(pl.multiple_of(blocks_ref[4 + xh] * 256, 256), 256)
            here = slice(xh * 256, xh * 256 + 256)
            parts = [bias_ref[0:1, here], bias_ref[1:2, here]]
            parts += [ref[i : i + 1, own] for ref in (as_ref, fs_ref) for i in range(3)]
            parts += [hs_ref[xh : xh + 1, out] for out in narrow(1024)]
            for i, part in enumerate(parts):
                vec_ref[xh * 4 + i // 3 : xh * 4 + i // 3 + 1, (i % 3) * 256 : (i % 3) * 256 + 256] = part
        vec_ref[8:16, :] = jnp.zeros((8, 768), f32)
        for piece in pieces:
            piece.ref[512:528, 0:768] = vec_ref[...].astype(bf16)
            piece.ref[512:528, 768:] = jnp.zeros((VECTOR_ROWS, 256), bf16)
        weight_grad(flip.ref, d_ref, full_ref)
        split_blocks(table_ref, full_ref, pieces, slice(0, 768))
        split_blocks(table_ref, out_late.ref, pieces, slice(768, 1024))
        for piece in pieces:
            piece.push()
        w_ref, ga_ref = w.ref, ga.ref
        for out in narrow(1024):
            low = slice(out.start + 1024, out.stop + 1024)
            part_ref[:, out] = nt(d_ref[:, :768], w_ref[out, :]) + nt(d_ref[:, 768:], w_ref[low, :])
        for i in range(2):
            own = pl.ds(pl.multiple_of(blocks_ref[i] * 256, 256), 256)
            across = pl.ds(pl.multiple_of(blocks_ref[2 + i] * 256, 256), 256)
            keep_ref[i, :, :] = part_ref[:, own] + ga_ref[:, own]
            away_ref[i, :, :] = part_ref[:, across].astype(bf16)

    return call(
        kernel,
        [((2, 512, 256), f32), ((2, 512, 256), bf16), *[far((528, 1024), bf16)] * 4],
        (table, blocks, late(queries), late(keys), late(values), context_grad, late(probs, 4), late(flip), late(weights, 1, slice(0, 768)), late(grad_attn), attn_sums, ffn_sums, hidden_sums, late(out_grad), ("any", awaited)),
        scratch=[((2048, 768), bf16), ((512, 1536), bf16), ((512, 1024), f32), ((8, 512), f32), ((16, 768), f32)],
        limit=44,
    )


def add_refs(refs, rows, cols=slice(None)):
    total = refs[0][rows, cols].astype(f32)
    for ref in refs[1:]:
        total = total + ref[rows, cols].astype(f32)
    return total


def add_split(parts, tail, fetch):
    rows, width = parts[0].shape
    quarter = (rows - tail) // 4

    def kernel(*refs):
        ins, outs = [ref.ref if fetch else ref for ref in refs[:4]], refs[4:]
        for i in range(4):
            outs[i][0:quarter, :] = add_refs(ins, slice(i * quarter, i * quarter + quarter)).astype(bf16)
        if tail:
            vectors = add_refs(ins, slice(4 * quarter, rows)).astype(bf16)
            for i in range(4):
                outs[i][quarter : quarter + tail, :] = vectors

    return call(kernel, [((quarter + tail, width), bf16)] * 4, [late(part) if fetch else part for part in parts], limit=16)


def add_passing(near, back, plus, minus):
    def kernel(near, back, plus, minus, near_ref, back_ref):
        half = slice(0, 256)
        near_ref[...] = add_refs((near.ref, plus.ref), half).astype(bf16)
        back_ref[...] = add_refs((back.ref, minus.ref), half).astype(bf16)

    return call(kernel, [((256, 1024), bf16)] * 2, [late(part) for part in (near, back, plus, minus)])


def add_ring(own, plus, minus, near, back):
    def kernel(own, plus, minus, near, back, *outs):
        own_ref, plus_ref, minus_ref, near_ref, back_ref = own.ref, plus.ref, minus.ref, near.ref, back.ref
        for i in range(4):
            rows, here = slice(i * 128, i * 128 + 128), slice(i % 2 * 128, i % 2 * 128 + 128)
            behind = slice(256 + here.start, 256 + here.stop)
            total = own_ref[rows, :].astype(f32)
            if i < 2:
                total = total + near_ref[here, :].astype(f32) + minus_ref[behind, :].astype(f32)
            else:
                total = total + back_ref[here, :].astype(f32) + plus_ref[behind, :].astype(f32)
            outs[i][...] = total.astype(bf16)

    return call(kernel, [((128, 1024), bf16)] * 4, [late(part) for part in (own, plus, minus, near, back)])


def merge_groups(attn, up, down):
    def kernel(*refs):
        ready, outs = [ref.ref for ref in refs[:12]], refs[12:]
        vectors = add_refs(ready[:4], slice(128, 128 + VECTOR_ROWS)).astype(bf16)
        for i in range(4):
            rows = slice(i * BLOCK, i * BLOCK + BLOCK)
            for group in range(3):
                cols = slice(group * 1024, group * 1024 + 1024)
                outs[i][0:BLOCK, cols] = add_refs(ready[4 * group : 4 * group + 4], rows).astype(bf16)
            outs[i][BLOCK : BLOCK + VECTOR_ROWS, 0:1024] = vectors
            outs[i][BLOCK : BLOCK + VECTOR_ROWS, 1024:] = jnp.zeros((VECTOR_ROWS, 2048), bf16)

    return call(kernel, [((BLOCK + VECTOR_ROWS, 3072), bf16)] * 4, [late(part) for part in (*attn, *up, *down)])


def final_sums(blocks, parts):
    def kernel(blocks_ref, *refs):
        ins, (qkv_ref, out_ref, up_ref, down_ref, *vectors) = refs[:4], refs[4:]
        rows = slice(0, BLOCK)
        for j in range(3):
            qkv_ref[j] = add_refs(ins, rows, slice(j * 256, j * 256 + 256))
        out_ref[...] = add_refs(ins, rows, slice(768, 1024))
        up_ref[...] = add_refs(ins, rows, slice(1024, 2048))
        down_ref[...] = add_refs(ins, rows, slice(2048, 3072))
        sums = add_refs(ins, slice(BLOCK, BLOCK + VECTOR_ROWS), slice(0, 768))
        sums = jnp.where(blocks_ref[6] == 0, sums[0:4], sums[4:8])
        for i in range(12):
            value = sums[i // 3 : i // 3 + 1, (i % 3) * 256 : (i % 3) * 256 + 256]
            if i < 8:
                vectors[i][...] = value
            else:
                vectors[8][:, (i - 8) * 256 : (i - 8) * 256 + 256] = value

    wide = ((BLOCK, 1024), f32)
    outs = [((3, BLOCK, 256), f32), ((BLOCK, 256), f32), wide, wide, *[((1, 256), f32)] * 8, ((1, 1024), f32)]
    return call(kernel, outs, (blocks, *parts))


def body(
    tokens,
    seg_ids,
    qkv_weight,
    q_bias,
    v_bias,
    out_weight,
    out_bias,
    gain_attn,
    shift_attn,
    up_weight,
    up_bias,
    down_weight,
    down_bias,
    gain_ffn,
    shift_ffn,
    out_grad,
):
    length = seg_ids.shape[1]
    cols = tokens.shape[1]
    xh = lax.axis_index("xh")
    core = lax.axis_index("core")
    place = {
        "x": xh * 2 + lax.axis_index("xl"),
        "y": lax.axis_index("y"),
        "z": lax.axis_index("z"),
        "core": core,
    }
    table = block_table(STAGES, place)
    down_table = block_table(DOWN_STAGES, place)
    blocks = jnp.stack(
        [xh * 2 + core, 2 - xh * 2 + core, xh * 2 + 1 - core, 3 - xh * 2 - core, core, 2 + core, xh]
    ).astype(jnp.int32)

    def halves(local):
        pair = local.reshape(2, length, cols)
        own = lax.dynamic_index_in_dim(pair, xh, 0, keepdims=False)
        away = lax.dynamic_index_in_dim(pair, 1 - xh, 0, keepdims=False)
        return own, away

    def two_sequences(own, partner):
        partner = partner.astype(f32)
        return jnp.where(xh == 0, jnp.stack([own, partner]), jnp.stack([partner, own])).reshape(2 * length, cols)

    own_tokens, away_tokens = halves(tokens)
    token_partner = swap_xh(away_tokens)
    vectors = stack_vectors(
        (q_bias, v_bias, out_bias, gain_attn, shift_attn, down_bias, gain_ffn, shift_ffn), up_bias
    )
    vector_partner = swap_xh(vectors)
    first = gather_direct(round_weights(qkv_weight, out_weight, up_weight, down_weight), STAGES[0])
    first = lax.optimization_barrier((*first, token_partner))
    token_partner = first[4]
    attn_level, ffn_level = part_groups(first[:4])
    attn_second = gather_direct(attn_level, STAGES[1])
    token_across = swap_core(jnp.stack([own_tokens, token_partner]))
    vector_across = swap_core(jnp.stack([vectors, vector_partner]))
    attn_second = lax.optimization_barrier((*attn_second, token_across, vector_across))
    token_across, vector_across = attn_second[4:]
    attn_pieces = gather_direct(*stack(attn_second[:4]), STAGES[2])
    token_rows, token_flip = collect_tokens(blocks, own_tokens, token_partner, token_across, True)
    rows, mine = collect_vectors(blocks, vectors, vector_partner, vector_across)
    ffn_second = gather_direct(after(ffn_level, *attn_second[1:4]), STAGES[1])
    ffn_first, ffn_last, ffn_up, ffn_down = gather_halves(*stack(ffn_second, 2, (*attn_pieces[1:], token_flip, mine)), STAGES[2])
    segment = lax.dynamic_index_in_dim(seg_ids, xh, 0, keepdims=False)

    attn_full, queries, keys, values, context, probs, attn_part = attention_forward(
        table, token_rows, attn_pieces, mine, segment[:, None], segment[None, :]
    )
    ffn_beyond = gather_beyond(
        (ffn_up[0], after(ffn_up[1], attn_part)), (after(ffn_down[0], attn_part), ffn_down[1]), STAGES[2]
    )
    ffn_pieces = ffn_first, ffn_last, *ffn_up, *ffn_beyond, *ffn_down
    up_full, down_full, normed_attn, inverse_attn, hidden_low, activated, slope = up_forward(
        table, token_rows, attn_part, swap_core(attn_part), rows, mine, ffn_pieces
    )
    own_cot, away_cot = halves(out_grad.astype(bf16))
    cot_partner = swap_xh(after(away_cot, *ffn_pieces[2:]))
    ffn_part = down_forward(after(activated, cot_partner), down_full)
    cot_rows = collect_tokens(blocks, own_cot, cot_partner, swap_core(jnp.stack([own_cot, cot_partner])), False)[0]
    layer_own, layer_away, grad_resid_ffn, ffn_grad_low, ffn_sums, hidden_sums, pre_grad_low, hidden_part = ffn_backward(
        blocks, normed_attn, ffn_part, swap_core(ffn_part), rows, cot_rows, down_full, slope, up_full
    )
    layer_partner = swap_xh(layer_away)
    up_own, up_near, up_far, up_back = up_backward(table, hidden_low, pre_grad_low)
    up_near = send(after(up_near, layer_partner), STAGES[2], 1)
    up_far = send(up_far, STAGES[2], 2)
    grad_resid_attn, context_grad, attn_sums, out_weight_grad, *down_ring = out_backward(
        down_table, grad_resid_ffn, hidden_part, swap_core(hidden_part), normed_attn, inverse_attn,
        rows, attn_full, context, ffn_grad_low, activated, up_own,
    )
    up_parts = up_own, up_near, up_far, send(after(up_back, attn_sums), STAGES[2], -1)
    down_own, down_plus, down_minus, down_near, down_back = down_ring
    down_plus, down_minus = send(down_plus, DOWN_STAGES[2], 1), send(down_minus, DOWN_STAGES[2], -1)
    input_own, input_away, *attn_parts = attention_backward(
        table, blocks, queries, keys, values, context_grad, probs, token_flip, attn_full,
        grad_resid_attn, attn_sums, ffn_sums, hidden_sums, out_weight_grad, up_parts[0],
    )
    attn_own, attn_near, attn_far, attn_back = lax.optimization_barrier((*attn_parts, *up_parts[1:]))[:4]
    attn_back = after(attn_back, down_plus)
    attn_parts = scatter_direct((attn_own, attn_near, attn_far, attn_back), STAGES[2])
    up_parts = scatter_direct(add_split(up_parts, 0, True), STAGES[1])
    down_near, down_back = add_passing(down_near, down_back, down_plus, down_minus)
    down_near, down_back = send(down_near, DOWN_STAGES[2], 1), send(down_back, DOWN_STAGES[2], -1)
    down_parts = add_ring(down_own, down_plus, down_minus, down_near, down_back)
    down_parts = scatter_direct(down_parts, DOWN_STAGES[1])
    attn_parts = add_split(attn_parts, VECTOR_ROWS, False)
    input_own = input_own + swap_core(after(input_away, attn_parts[0])).astype(f32)
    attn_parts = scatter_direct(lax.optimization_barrier((*attn_parts, up_parts[3]))[:4], STAGES[1])
    input_away = after(input_own[1].astype(bf16), attn_parts[1])
    input_grad = two_sequences(input_own[0], swap_xh(input_away))
    layer_out = two_sequences(layer_own, layer_partner)
    last = scatter_direct(merge_groups(attn_parts, up_parts, down_parts), STAGES[0])
    qkv_grad, out_grad_rows, up_rows, down_rows, *sums = final_sums(blocks, last)
    (
        q_bias_grad,
        v_bias_grad,
        out_bias_grad,
        gain_attn_grad,
        shift_attn_grad,
        down_bias_grad,
        gain_ffn_grad,
        shift_ffn_grad,
        up_bias_grad,
    ) = (value.reshape(-1) for value in sums)
    return (
        layer_out,
        input_grad,
        qkv_grad.transpose(1, 0, 2),
        q_bias_grad,
        v_bias_grad,
        out_grad_rows,
        out_bias_grad,
        gain_attn_grad,
        shift_attn_grad,
        up_rows,
        up_bias_grad,
        down_rows,
        down_bias_grad,
        gain_ffn_grad,
        shift_ffn_grad,
    )


def solution(mesh):
    placed_mesh = Mesh(mesh.devices.reshape(4, 4, 2, 2, 2), AXES)
    placed = (
        P(ROW, COL),
        P(ROW, None),
        P(ROW, None, COL),
        P(COL),
        P(COL),
        P(ROW, COL),
        P(COL),
        P(COL),
        P(COL),
        P(ROW, COL),
        P(COL),
        P(ROW, COL),
        P(COL),
        P(COL),
        P(COL),
        P(ROW, COL),
    )
    return jax.shard_map(
        body,
        mesh=placed_mesh,
        in_specs=placed,
        out_specs=(
            P(ROW, COL),
            P(ROW, COL),
            P(ROW, None, COL),
            P(COL),
            P(COL),
            P(ROW, COL),
            P(COL),
            P(COL),
            P(COL),
            P(ROW, COL),
            P(COL),
            P(ROW, COL),
            P(COL),
            P(COL),
            P(COL),
        ),
        check_vma=False,
    )
```
